256 devices in a mesh: ctx: 64 (over y, z, core), head: 4 (over x).
Axes of the slice: x: 4, y: 4, z: 8, core: 2. Of those that a mesh axis runs over, the one named last changes fastest.
Arguments:
- queries: bfloat16 [65536, 2048], P('ctx', 'head'), may hold values from -6 to 6
- keys: bfloat16 [65536, 2048], P('ctx', 'head'), may hold values from -6 to 6
- values: bfloat16 [65536, 2048], P('ctx', 'head'), may hold values from -6 to 6
- log_decay: float32 [16, 65536], P('head', 'ctx'), may hold values from -0.8 to 0
- write_strength: float32 [16, 65536], P('head', 'ctx'), may hold values from 0 to 0.9
- level_weights: float32 [16, 12, 65536], P('head', None, 'ctx'), may hold values from 0.2 to 2
- segment: int32 [65536], P('ctx'), may hold values from 0 to 3, never falling along the last dimension, each value on 1 to 32768 neighbouring positions
- out_gate: bfloat16 [65536, 2048], P('ctx', 'head'), may hold values from -6 to 6
- norm_gain: float32 [128], replicated, may hold values from 0.1 to 1.9
- w_out: bfloat16 [2048, 2048], P('head'), may hold values from -0.125 to 0.125
Outputs:
- layer_out: bfloat16 [65536, 2048], P(('ctx', 'head'))
The draws below stay inside these ranges and needn't reach their ends.
Inputs may be any that keep to these rules, and one draw needn't show every extreme that they name: `segment`: never falls along the sequence; each id is one contiguous run of at most 32768 tokens, and one run is exactly that long.
All inputs are finite; a program needn't handle non-finite values.
Results may differ from the reference program's by a relative error of at most 0.024.
Values may be sent and summed in bfloat16 or wider, within the bound.
A program may use at most 128 MiB of HBM per device.

```python
import math
import jax
import jax.numpy as jnp
import numpy as np
from jax import lax

D = 2048
H = 16
DK = 128
DV = 128
BLOCK = 128
LEVELS = 12
BRANCHES = 4
TOK_DEV = 1024
TOKENS = 65536
HEADS_DEV = 4
N_HEAD = 4


def slow_heads(key, number):
    ranking = jax.random.permutation(jax.random.fold_in(key, 11), H)
    return (ranking < number).astype(jnp.float32)[:, None]


def draw_log_decay(key, part):
    number = H // 2
    slower = slow_heads(key, number)
    key = jax.random.fold_in(key, 3)
    fast_rate = jax.random.uniform(jax.random.fold_in(key, 1), (H, 1), jnp.float32, 1.0 / 50.0, 1.0 / 30.0)
    slow_rate = jax.random.uniform(jax.random.fold_in(key, 2), (H, 1), jnp.float32, 0.05, 0.25) / TOKENS
    rough = jax.random.uniform(jax.random.fold_in(key, 4), (H, TOKENS), jnp.float32, 0.5, 1.5)
    factor = jnp.exp(jax.random.uniform(jax.random.fold_in(key, 5), (H, TOKENS // TOK_DEV, 1), jnp.float32, math.log(0.5), math.log(2.0)))
    spread = jnp.broadcast_to(factor, (H, TOKENS // TOK_DEV, TOK_DEV)).reshape(H, TOKENS)
    rate = (slower * slow_rate + (1.0 - slower) * fast_rate) * rough * spread
    places = jax.random.randint(jax.random.fold_in(key, 6), (H, 2), 0, TOKENS)
    hits = jnp.any(jnp.arange(TOKENS, dtype=jnp.int32)[None, None, :] == places[:, :, None], axis=1)
    losses = jnp.log(jax.random.uniform(jax.random.fold_in(key, 7), (H, TOKENS), jnp.float32, 0.5, 0.8))
    return (-rate + jnp.where(hits, losses, 0.0)).astype(jnp.float32)


def draw_write_strength(key, part):
    number = H // 2
    slower = slow_heads(key, number)
    key = jax.random.fold_in(key, 5)
    fast_strength = jax.random.uniform(jax.random.fold_in(key, 1), (H, TOKENS), jnp.float32, 0.2, 0.9)
    slow_strength = jax.random.uniform(jax.random.fold_in(key, 2), (H, TOKENS), jnp.float32, 0.1, 0.4) * DK / TOKENS
    return (slower * slow_strength + (1.0 - slower) * fast_strength).astype(jnp.float32)


def level_of(key, dims, cuts, smallest, largest):
    level = 1.0
    for axis_at, shards_of in cuts:
        steps = jax.random.uniform(jax.random.fold_in(jax.random.fold_in(key, 6), axis_at), (shards_of,), jnp.float32, smallest / len(cuts), largest / len(cuts))
        level = level * jnp.repeat(jnp.exp(steps), dims[axis_at] // shards_of).reshape((-1,) + (1,) * (len(dims) - 1 - axis_at))
    return level


def split_up(count, total, limit, lean):
    loads = [(1 << 20) // math.isqrt(standing ** lean) + 1 for standing in range(2, count + 1)]
    surplus, counts = total - limit - (count - 1), [1] * (count - 1)
    while surplus > 0:
        candidates = [i for i in range(count - 1) if counts[i] < limit]
        pool, budget = sum([loads[i] for i in candidates]), surplus
        for i in candidates:
            addition = min(limit - counts[i], max(1, budget * loads[i] // pool), surplus)
            counts[i] = counts[i] + addition
            surplus = surplus - addition
    return np.array([limit] + counts)


def uneven(own_key, number_of, total, most, skew):
    if number_of == 2:
        one = jax.random.randint(own_key, (), max(1, total - most), min(most, total - 1) + 1)
        return jnp.stack([one, total - one])
    tallies = jnp.asarray(split_up(number_of, total, most, skew), jnp.int32)
    couples = (number_of - 1) // 2
    donor, sink = tallies[1:1 + 2 * couples:2], tallies[2:2 + 2 * couples:2]
    margin = jnp.minimum(donor - 1, most - sink)
    passed = jax.random.randint(jax.random.fold_in(own_key, 1), (couples,), 0, 1 << 20) % (margin + 1)
    tallies = tallies.at[1:1 + 2 * couples:2].set(donor - passed).at[2:2 + 2 * couples:2].set(sink + passed)
    return tallies[jax.random.permutation(jax.random.fold_in(own_key, 2), number_of)]


def noise(rng, shape, width, limit, split=(), kind=jnp.bfloat16):
    drawn = jax.random.normal(rng, shape, jnp.float32) * width
    if len(split) > 0:
        drawn = level_of(rng, shape, split, -0.22, 0.18) * drawn
    return jnp.clip(drawn, min=-limit, max=limit).astype(kind)


def setup_inputs(seed: int = 0) -> dict:
    arg_keys = jax.random.split(jax.random.key(seed), 11)
    queries = noise(arg_keys[0], (TOKENS, H * DK), 1.0, 6.0, ((0, 64), (1, 4)))
    keys = noise(arg_keys[1], (TOKENS, H * DK), 1.0, 6.0, ((0, 64), (1, 4)))
    values = noise(arg_keys[2], (TOKENS, H * DV), 1.0, 6.0, ((0, 64), (1, 4)))
    log_decay = draw_log_decay(jax.random.fold_in(arg_keys[10], 71), 0)
    write_strength = draw_write_strength(jax.random.fold_in(arg_keys[10], 71), 0)
    level_weights = jnp.clip(jnp.exp(math.log(2.0) - 2.3025851 * jax.random.uniform(arg_keys[5], (H, LEVELS, TOKENS), jnp.float32) ** level_of(arg_keys[5], (H, LEVELS, TOKENS), ((0, 4), (2, 64)), -0.2, 0.2)), 0.2, 2.0)
    segment = jnp.searchsorted(jnp.cumsum(uneven(arg_keys[6], BRANCHES, TOKENS, TOKENS // 2, 0)), jnp.arange(TOKENS), side="right").astype(jnp.int32)
    out_gate = noise(arg_keys[7], (TOKENS, H * DV), 1.0, 6.0, ((0, 64), (1, 4)))
    norm_gain = jnp.clip(1.0 + 0.18 * jax.random.normal(arg_keys[8], (DV,), jnp.float32), 0.1, 1.9)
    w_out = noise(arg_keys[9], (H * DV, D), (H * DV) ** -0.5, 0.125, ((0, 4),))
    return {"queries": queries, "keys": keys, "values": values, "log_decay": log_decay, "write_strength": write_strength, "level_weights": level_weights, "segment": segment, "out_gate": out_gate, "norm_gain": norm_gain, "w_out": w_out}


EPSILON = 1e-06
HIGHEST = lax.Precision.HIGHEST

def unit_rows(matrix):
    return matrix / jnp.sqrt(lax.optimization_barrier(jnp.sum(matrix * matrix, axis=-1, keepdims=True)) + EPSILON)

def unit_lower_inverse(strict_part, length):
    power = -strict_part
    inverse = jnp.eye(length, dtype=jnp.float32) + power
    reach = 2
    while reach < length:
        power = jnp.dot(power, power, precision=HIGHEST)
        inverse = inverse + jnp.dot(inverse, power, precision=HIGHEST)
        reach = reach * 2
    return inverse

def block_terms(query, key_rows, value_rows, log_decay, strength, segment, previous):
    query_half = lax.optimization_barrier(unit_rows(query.astype(jnp.float32)).astype(jnp.bfloat16))
    key_half = lax.optimization_barrier(unit_rows(key_rows.astype(jnp.float32)).astype(jnp.bfloat16))
    query = query_half.astype(jnp.float32)
    key_rows = key_half.astype(jnp.float32)
    value_rows = value_rows.astype(jnp.float32)
    length = log_decay.shape[0]
    key_width = key_rows.shape[1]
    value_width = value_rows.shape[1]
    summed = jnp.cumsum(log_decay)
    row_index = lax.broadcasted_iota(jnp.int32, (length, length), 0)
    col_index = lax.broadcasted_iota(jnp.int32, (length, length), 1)
    inside = (row_index >= col_index) & (segment[:, None] == segment[None, :])
    spacing = summed[:, None] - summed[None, :]
    fading = jnp.where(inside, jnp.exp(jnp.where(inside, spacing, 0.0)), 0.0)
    opening = jnp.exp(summed) * (segment == previous).astype(jnp.float32)
    closing = jnp.exp(summed[-1] - summed) * (segment == segment[-1]).astype(jnp.float32)
    key_inner = jnp.dot(key_half, key_half.T, preferred_element_type=jnp.float32)
    strict = jnp.where(row_index > col_index, fading * key_inner, 0.0)
    inverse = unit_lower_inverse(strength[:, None] * strict, length)
    stacked = jnp.concatenate([strength[:, None] * value_rows, (strength * opening)[:, None] * key_rows], axis=1)
    solved = jnp.dot(inverse, stacked, precision=HIGHEST)
    writes = solved[:, :value_width]
    erasing = solved[:, value_width:]
    scores = fading * jnp.dot(query_half, key_half.T, preferred_element_type=jnp.float32)
    inner_out = jnp.dot(scores, writes, precision=HIGHEST)
    readout = opening[:, None] * query - jnp.dot(scores, erasing, precision=HIGHEST)
    ended = closing[:, None] * key_rows
    carry_map = opening[-1] * jnp.eye(key_width, dtype=jnp.float32) - jnp.dot(ended.T, erasing, precision=HIGHEST)
    fresh = jnp.dot(ended.T, writes, precision=HIGHEST)
    return (inner_out, readout, carry_map, fresh)

def level_sweep(stack, block_ids, inner_out, readout, carry_map, fresh, weights):
    ladder = jnp.arange(stack.shape[0], dtype=jnp.int32)

    def advance(state, inputs):
        block_id, inner_block, read_block, map_block, fresh_block, weight_block = inputs
        spread = jnp.einsum('ck,lkv->lcv', read_block, state, precision=HIGHEST)
        produced = weight_block[0][:, None] * inner_block + jnp.einsum('lc,lcv->cv', weight_block, spread, precision=HIGHEST)
        carried = block_id >> ladder & 1
        target = jnp.sum(jnp.cumprod(carried)) + 1
        moved = jnp.einsum('kj,ljv->lkv', map_block, state, precision=HIGHEST)
        merged = lax.optimization_barrier(jnp.sum(jnp.where((ladder < target)[:, None, None], moved, 0.0), axis=0)) + fresh_block
        updated = jnp.where((ladder > target)[:, None, None], moved, 0.0) + jnp.where((ladder == target)[:, None, None], merged[None], 0.0)
        return (updated, produced)
    final_state, produced = lax.scan(advance, stack, (block_ids, inner_out, readout, carry_map, fresh, weights))
    return produced

def head_output(query, key_rows, value_rows, log_decay, strength, weights, segment):
    blocks = TOKENS // BLOCK

    def to_blocks(array):
        return array.reshape((blocks, BLOCK) + array.shape[1:])
    segment_blocks = to_blocks(segment)
    previous = jnp.concatenate([segment_blocks[:1, 0], segment_blocks[:-1, -1]])
    inner_out, readout, carry_map, fresh = jax.vmap(block_terms)(to_blocks(query), to_blocks(key_rows), to_blocks(value_rows), to_blocks(log_decay), to_blocks(strength), segment_blocks, previous)
    block_weights = weights.reshape(LEVELS, blocks, BLOCK).transpose(1, 0, 2)
    stack = jnp.zeros((LEVELS, DK, DV), jnp.float32)
    block_ids = jnp.arange(blocks, dtype=jnp.int32)
    produced = level_sweep(stack, block_ids, inner_out, readout, carry_map, fresh, block_weights)
    return produced.reshape(TOKENS, DV)

def reference(queries, keys, values, log_decay, write_strength, level_weights, segment, out_gate, norm_gain, w_out):

    def by_head(array):
        return array.reshape(TOKENS, H, -1).transpose(1, 0, 2)

    def per_head(inputs):
        return head_output(inputs[0], inputs[1], inputs[2], inputs[3], inputs[4], inputs[5], segment)
    outputs = lax.map(per_head, (by_head(queries), by_head(keys), by_head(values), log_decay, write_strength, level_weights))
    gate = by_head(out_gate).astype(jnp.float32)
    scale = lax.rsqrt(lax.optimization_barrier(jnp.mean(outputs * outputs, axis=-1, keepdims=True)) + EPSILON)
    normed = (outputs * scale * norm_gain * jax.nn.silu(gate)).astype(jnp.bfloat16)
    flat = normed.transpose(1, 0, 2).reshape(TOKENS, H * DV)
    group_rows = HEADS_DEV * DV
    total = jnp.zeros((TOKENS, D), jnp.float32)
    for group in range(N_HEAD):
        partial_out = jnp.dot(flat[:, group * group_rows:(group + 1) * group_rows], w_out[group * group_rows:(group + 1) * group_rows], preferred_element_type=jnp.float32).astype(jnp.bfloat16)
        total = total + lax.optimization_barrier(partial_out).astype(jnp.float32)
    return total.astype(jnp.bfloat16)
```

```python
import jax
import jax.numpy as jnp
from jax import lax
from jax.experimental import pallas as pl
from jax.experimental.pallas import tpu as pltpu
from jax.sharding import PartitionSpec as P

BLOCK = 128
BLOCKS = 8
TOKENS_HERE = 1024
HEADS_HERE = 4
WIDTH = 128
LEVELS = 12
EPSILON = 1e-06
FAR = -1e4
MESSAGE_ROWS = 144

F32 = jnp.float32
BF16 = jnp.bfloat16


def dot(left, right):
    return jnp.dot(left, right, preferred_element_type=F32)


def dot_rows(left, right):
    return lax.dot_general(left, right, (((1,), (1,)), ((), ())), preferred_element_type=F32)


def dot_columns(left, right):
    return lax.dot_general(left, right, (((0,), (0,)), ((), ())), preferred_element_type=F32)


def split3(value):
    first = value.astype(BF16)
    rest = value - first.astype(F32)
    second = rest.astype(BF16)
    third = (rest - second.astype(F32)).astype(BF16)
    return first, second, third


def rows_of(block):
    return slice(block * BLOCK, (block + 1) * BLOCK)


def weight_column(level):
    return level if level < 8 else level + 4


def prepare_masks(seg_ref, far_ref, pair_ref):
    row = lax.broadcasted_iota(jnp.int32, (BLOCK, BLOCK), 0)
    col = lax.broadcasted_iota(jnp.int32, (BLOCK, BLOCK), 1)
    segs = seg_ref[...].astype(F32)
    padded = jnp.concatenate([segs, jnp.zeros((BLOCK - BLOCKS, BLOCK), F32)], axis=0)
    seg_cols = padded.T
    for block in range(BLOCKS):
        same = seg_cols[:, block : block + 1] == segs[block : block + 1, :]
        far_ref[block] = jnp.where(same & (row >= col), 0.0, FAR)
    for step in range(7):
        size = 1 << step
        chosen = (row // size == col // size + 1) & (row // size % 2 == 1)
        pair_ref[step] = jnp.where(chosen, 1.0, 0.0).astype(BF16)


def unit_rows(rows, ones):
    wide = rows.astype(F32)
    total = dot((wide * wide).astype(BF16), ones)
    return (wide * lax.rsqrt(total + EPSILON)).astype(BF16)


def head_terms(q, k, v, decay, strength, level_weights, segs, far_ref, pair_ref):
    row = lax.broadcasted_iota(jnp.int32, (BLOCK, BLOCK), 0)
    col = lax.broadcasted_iota(jnp.int32, (BLOCK, BLOCK), 1)
    every = range(BLOCKS)
    ones = jnp.ones((BLOCK, BLOCK), BF16)
    upto = jnp.where(row <= col, 1.0, 0.0).astype(BF16)
    summed = sum(dot(part, upto) for part in split3(decay))
    last_sum = jnp.broadcast_to(summed[:, BLOCK - 1 :], (BLOCKS, BLOCK))
    last_seg = jnp.broadcast_to(segs[:, BLOCK - 1 :], (BLOCKS, BLOCK))
    first_seg = jnp.broadcast_to(segs[:, :1], (BLOCKS, BLOCK))
    before = jnp.concatenate([first_seg[:1], last_seg[:-1]], axis=0)
    opening = jnp.exp(summed) * (segs == before).astype(F32)
    closing = jnp.exp(last_sum - summed) * (segs == last_seg).astype(F32)
    keeps = jnp.exp(last_sum) * (last_seg == before).astype(F32)
    stacked = jnp.concatenate(
        [summed, strength, opening, strength * opening, closing, jnp.zeros((BLOCK - 40, BLOCK), F32)], axis=0
    )
    cols = stacked.T
    wcols = jnp.concatenate(level_weights, axis=0).T

    def column(kind, block):
        return cols[:, kind * 8 + block : kind * 8 + block + 1]

    def weight(level, block):
        at = block * 16 + weight_column(level)
        return wcols[:, at : at + 1]

    qn = unit_rows(q, ones)
    kn = unit_rows(k, ones)
    grams = [
        dot_rows(jnp.concatenate([kn[rows_of(b)], qn[rows_of(b)]], axis=0), kn[rows_of(b)]) for b in every
    ]
    fading = [jnp.exp(column(0, b) - summed[b : b + 1, :] + far_ref[b]) for b in every]
    lower = [(column(1, b) * fading[b] * grams[b][:BLOCK]).astype(BF16) for b in every]
    scores = [(fading[b] * grams[b][BLOCK:]).astype(BF16) for b in every]
    eye = jnp.where(row == col, 1.0, 0.0).astype(BF16)
    inverse = [eye - lower[b] * pair_ref[0] for b in every]
    for step in range(1, 7):
        mask = pair_ref[step]
        half = [dot(inverse[b], lower[b] * mask).astype(BF16) for b in every]
        inverse = [inverse[b] - dot(half[b], inverse[b]).astype(BF16) for b in every]
    right = [
        jnp.concatenate(
            [
                (column(1, b) * v[rows_of(b)].astype(F32)).astype(BF16),
                (column(3, b) * kn[rows_of(b)].astype(F32)).astype(BF16),
            ],
            axis=1,
        )
        for b in every
    ]
    solved = [dot(inverse[b], right[b]).astype(BF16) for b in every]
    read = [dot(scores[b], solved[b]) for b in every]
    out = [weight(0, b) * read[b][:, :WIDTH] for b in every]
    reads = [column(2, b) * qn[rows_of(b)].astype(F32) - read[b][:, WIDTH:] for b in every]
    ended = [(column(4, b) * kn[rows_of(b)].astype(F32)).astype(BF16) for b in every]
    joined = [dot_columns(ended[b], solved[b]) for b in every]
    fresh = [joined[b][:, :WIDTH] for b in every]
    erase = [joined[b][:, WIDTH:] for b in every]
    keep = [keeps[b : b + 1] for b in every]
    for level in range(1, 4):
        span = 1 << (level - 1)
        fresh2, erase2, keep2 = [], [], []
        for pair in range(len(fresh) // 2):
            e, o = 2 * pair, 2 * pair + 1
            later = [b for b in every if b // span == o]
            stack = jnp.concatenate([reads[b] for b in later] + [erase[o]], axis=0).astype(BF16)
            both = dot(stack, jnp.concatenate([fresh[e], erase[e]], axis=1).astype(BF16))
            for at, b in enumerate(later):
                part = both[at * BLOCK : (at + 1) * BLOCK]
                out[b] = out[b] + weight(level, b) * part[:, :WIDTH]
                reads[b] = keep[e] * reads[b] - part[:, WIDTH:]
            part = both[len(later) * BLOCK :]
            fresh2.append(keep[o] * fresh[e] - part[:, :WIDTH] + fresh[o])
            erase2.append(keep[o] * erase[e] + keep[e] * erase[o] - part[:, WIDTH:])
            keep2.append(keep[e] * keep[o])
        fresh, erase, keep = fresh2, erase2, keep2
    return out, reads, fresh[0], erase[0], keep[0]


def local_kernel(q_ref, k_ref, v_ref, decay_ref, strength_ref, weights_ref, seg_ref, out_ref, read_ref, message_ref, far_ref, pair_ref, spread_ref):
    head = pl.program_id(0)

    @pl.when(head == 0)
    def _():
        prepare_masks(seg_ref, far_ref, pair_ref)
        for source, at in ((decay_ref, 0), (strength_ref, 1)):
            for each in range(HEADS_HERE):
                for b in range(BLOCKS):
                    spread_ref[at, each, b : b + 1, :] = source[each : each + 1, rows_of(b)]

    weights = [
        part
        for b in range(BLOCKS)
        for part in (weights_ref[0, 0:8, rows_of(b)], weights_ref[0, 4:12, rows_of(b)])
    ]
    out, reads, fresh, erase, keep = head_terms(
        q_ref[...],
        k_ref[...],
        v_ref[...],
        spread_ref[0, head],
        spread_ref[1, head],
        weights,
        seg_ref[...].astype(F32),
        far_ref,
        pair_ref,
    )
    for b in range(BLOCKS):
        out_ref[rows_of(b), :] = out[b]
        read_ref[rows_of(b), :] = reads[b].astype(BF16)
    message_ref[0, :BLOCK, :WIDTH] = fresh.astype(BF16)
    message_ref[0, :BLOCK, WIDTH:] = erase.astype(BF16)
    wide = jnp.concatenate([keep, keep], axis=1)
    first, second, third = split3(wide)
    message_ref[0, BLOCK:, :] = jnp.concatenate(
        [first.astype(F32), second.astype(F32), third.astype(F32), jnp.zeros((13, 2 * WIDTH), F32)], axis=0
    ).astype(BF16)


def local_terms(queries, keys, values, decay, strength, weights, segs):
    tall = pl.BlockSpec((TOKENS_HERE, WIDTH), lambda h: (0, h))
    whole = pl.BlockSpec((HEADS_HERE, TOKENS_HERE), lambda h: (0, 0))
    return pl.pallas_call(
        local_kernel,
        grid=(HEADS_HERE,),
        in_specs=[
            tall,
            tall,
            tall,
            whole,
            whole,
            pl.BlockSpec((1, LEVELS, TOKENS_HERE), lambda h: (h, 0, 0)),
            pl.BlockSpec((BLOCKS, BLOCK), lambda h: (0, 0)),
        ],
        out_specs=[tall, tall, pl.BlockSpec((1, MESSAGE_ROWS, 2 * WIDTH), lambda h: (h, 0, 0))],
        out_shape=[
            jax.ShapeDtypeStruct((TOKENS_HERE, HEADS_HERE * WIDTH), F32),
            jax.ShapeDtypeStruct((TOKENS_HERE, HEADS_HERE * WIDTH), BF16),
            jax.ShapeDtypeStruct((HEADS_HERE, MESSAGE_ROWS, 2 * WIDTH), BF16),
        ],
        scratch_shapes=[
            pltpu.VMEM((BLOCKS, BLOCK, BLOCK), F32),
            pltpu.VMEM((7, BLOCK, BLOCK), BF16),
            pltpu.VMEM((2, HEADS_HERE, BLOCKS, BLOCK), F32),
        ],
        compiler_params=pltpu.CompilerParams(vmem_limit_bytes=48 << 20),
        cost_estimate=pl.CostEstimate(flops=20_000_000_000, bytes_accessed=8_000_000, transcendentals=0),
    )(queries, keys, values, decay, strength, weights, segs)


def finish_block(out, read, states, columns, gate, gain, ones):
    wide = read.astype(F32)
    lhs = jnp.concatenate([(column * wide).astype(BF16) for column in columns], axis=1)
    total = out + dot(lhs, states)
    mean = dot((total * total).astype(BF16), ones) * (1.0 / WIDTH)
    gate = gate.astype(F32)
    silu = gate / (1.0 + jnp.exp(-gate))
    return (total * lax.rsqrt(mean + EPSILON) * gain * silu).astype(BF16)


def finish_kernel(out_ref, read_ref, states_ref, weights_ref, gate_ref, gain_ref, normed_ref):
    ones = jnp.ones((WIDTH, WIDTH), BF16)
    weights = jnp.concatenate([weights_ref[0, 4:12, rows_of(b)] for b in range(BLOCKS)], axis=0)
    weights = jnp.concatenate([weights, jnp.zeros((BLOCK - 8 * BLOCKS, BLOCK), F32)], axis=0).T
    for b in range(BLOCKS):
        columns = [weights[:, b * 8 + level : b * 8 + level + 1] for level in range(6)]
        normed_ref[rows_of(b), :] = finish_block(
            out_ref[rows_of(b), :],
            read_ref[rows_of(b), :],
            states_ref[0],
            columns,
            gate_ref[rows_of(b), :],
            gain_ref[...],
            ones,
        )


def finish(out, read, states, weights, gate, gain):
    tall = pl.BlockSpec((TOKENS_HERE, WIDTH), lambda h: (0, h))
    return pl.pallas_call(
        finish_kernel,
        grid=(HEADS_HERE,),
        in_specs=[
            tall,
            tall,
            pl.BlockSpec((1, 6 * WIDTH, WIDTH), lambda h: (h, 0, 0)),
            pl.BlockSpec((1, LEVELS, TOKENS_HERE), lambda h: (h, 0, 0)),
            tall,
            pl.BlockSpec((1, WIDTH), lambda h: (0, 0)),
        ],
        out_specs=tall,
        out_shape=jax.ShapeDtypeStruct((TOKENS_HERE, HEADS_HERE * WIDTH), BF16),
        compiler_params=pltpu.CompilerParams(vmem_limit_bytes=48 << 20),
        cost_estimate=pl.CostEstimate(flops=2_000_000_000, bytes_accessed=6_000_000, transcendentals=0),
    )(out, read, states, weights, gate, gain)


def partner(value, bit):
    return lax.ppermute(value, "ctx", [(i, i ^ 1 << bit) for i in range(lax.axis_size("ctx"))])


def unpack(message):
    keep = jnp.sum(message[:, BLOCK : BLOCK + 3, :1].astype(F32), axis=1, keepdims=True)
    body = message[:, :BLOCK].astype(F32)
    return keep, body


def pack(keep, body):
    wide = jnp.broadcast_to(keep, (HEADS_HERE, 1, 2 * WIDTH))
    zeros = jnp.zeros((HEADS_HERE, 13, 2 * WIDTH), BF16)
    return jnp.concatenate([body.astype(BF16), *split3(wide), zeros], axis=1)


def compose(later, earlier):
    keep_l, body_l = later
    keep_e, body_e = earlier
    erase = body_l[:, :, WIDTH:].astype(BF16)
    moved = jnp.einsum("hij,hjk->hik", erase, body_e.astype(BF16), preferred_element_type=F32)
    carried = jnp.concatenate([body_l[:, :, :WIDTH], keep_e * body_l[:, :, WIDTH:]], axis=2)
    return keep_l * keep_e, keep_l * body_e + carried - moved


def scan_levels(message, flag):
    position = lax.axis_index("ctx")
    keep, body = unpack(message)
    scale = jnp.where(lax.broadcasted_iota(jnp.int32, body.shape, 2) < WIDTH, 1.0, flag)
    total = keep * flag, body * scale
    prefix = jnp.ones_like(keep), jnp.zeros_like(body)
    states = []
    for bit in range(6):
        upper = position >> bit & 1 == 1
        other = unpack(partner(pack(*total), bit))
        moved = compose((prefix[0], prefix[1].at[:, :, :WIDTH].set(0.0)), other)
        states.append(jnp.where(upper, flag * moved[1][:, :, :WIDTH], 0.0).astype(BF16))
        prefix = jnp.where(upper, moved[0], prefix[0]), jnp.where(upper, moved[1], prefix[1])
        later = tuple(jnp.where(upper, a, b) for a, b in zip(total, other))
        earlier = tuple(jnp.where(upper, b, a) for a, b in zip(total, other))
        total = compose(later, earlier)
    return jnp.concatenate(states, axis=1)


def shards(queries, keys, values, log_decay, write_strength, level_weights, segment, out_gate, norm_gain, w_out):
    count = lax.axis_size("ctx")
    before = lax.ppermute(segment[-1:] + 1, "ctx", [(i, i + 1) for i in range(count - 1)]) - 1
    flag = (before[0] == segment[0]).astype(F32)
    whole = lax.all_gather(w_out, "head", axis=0, tiled=True)
    out, read, message = local_terms(
        queries, keys, values, log_decay, write_strength, level_weights, segment.reshape(BLOCKS, BLOCK)
    )
    states = scan_levels(message, flag)
    normed = finish(out, read, states, level_weights, out_gate, norm_gain.reshape(1, WIDTH))
    gathered = lax.all_to_all(normed, "head", split_axis=0, concat_axis=1, tiled=True)
    return jnp.dot(gathered, whole, preferred_element_type=F32).astype(BF16)


def solution(mesh):
    placed = (
        P("ctx", "head"),
        P("ctx", "head"),
        P("ctx", "head"),
        P("head", "ctx"),
        P("head", "ctx"),
        P("head", None, "ctx"),
        P("ctx"),
        P("ctx", "head"),
        P(),
        P("head", None),
    )
    return jax.shard_map(
        shards, mesh=mesh, in_specs=placed, out_specs=P(("ctx", "head"), None), check_vma=False
    )
```

```python
import jax
import jax.numpy as jnp
from jax import lax
from jax.experimental import pallas as pl
from jax.experimental.pallas import tpu as pltpu
from jax.sharding import PartitionSpec as P

BLOCK = 128
BLOCKS = 8
TOKENS_HERE = 1024
HEADS_HERE = 4
WIDTH = 128
LEVELS = 12
EPSILON = 1e-06
FAR = -1e4
MESSAGE_ROWS = 144

F32 = jnp.float32
BF16 = jnp.bfloat16


def dot(left, right):
    return jnp.dot(left, right, preferred_element_type=F32)


def dot_rows(left, right):
    return lax.dot_general(left, right, (((1,), (1,)), ((), ())), preferred_element_type=F32)


def dot_columns(left, right):
    return lax.dot_general(left, right, (((0,), (0,)), ((), ())), preferred_element_type=F32)


def split3(value):
    first = value.astype(BF16)
    rest = value - first.astype(F32)
    second = rest.astype(BF16)
    third = (rest - second.astype(F32)).astype(BF16)
    return first, second, third


def rows_of(block):
    return slice(block * BLOCK, (block + 1) * BLOCK)


def weight_column(level):
    return level if level < 8 else level + 4


def prepare_masks(seg_ref, far_ref, pair_ref):
    row = lax.broadcasted_iota(jnp.int32, (BLOCK, BLOCK), 0)
    col = lax.broadcasted_iota(jnp.int32, (BLOCK, BLOCK), 1)
    segs = seg_ref[...].astype(F32)
    padded = jnp.concatenate([segs, jnp.zeros((BLOCK - BLOCKS, BLOCK), F32)], axis=0)
    seg_cols = padded.T
    for block in range(BLOCKS):
        same = seg_cols[:, block : block + 1] == segs[block : block + 1, :]
        far_ref[block] = jnp.where(same & (row >= col), 0.0, FAR)
    for step in range(7):
        size = 1 << step
        chosen = (row // size == col // size + 1) & (row // size % 2 == 1)
        pair_ref[step] = jnp.where(chosen, 1.0, 0.0).astype(BF16)


def unit_rows(rows, ones):
    wide = rows.astype(F32)
    total = dot((wide * wide).astype(BF16), ones)
    return (wide * lax.rsqrt(total + EPSILON)).astype(BF16)


def head_terms(q, k, v, decay, strength, level_weights, segs, far_ref, pair_ref):
    row = lax.broadcasted_iota(jnp.int32, (BLOCK, BLOCK), 0)
    col = lax.broadcasted_iota(jnp.int32, (BLOCK, BLOCK), 1)
    every = range(BLOCKS)
    ones = jnp.ones((BLOCK, BLOCK), BF16)
    upto = jnp.where(row <= col, 1.0, 0.0).astype(BF16)
    summed = sum(dot(part, upto) for part in split3(decay))
    last_sum = jnp.broadcast_to(summed[:, BLOCK - 1 :], (BLOCKS, BLOCK))
    last_seg = jnp.broadcast_to(segs[:, BLOCK - 1 :], (BLOCKS, BLOCK))
    first_seg = jnp.broadcast_to(segs[:, :1], (BLOCKS, BLOCK))
    before = jnp.concatenate([first_seg[:1], last_seg[:-1]], axis=0)
    opening = jnp.exp(summed) * (segs == before).astype(F32)
    closing = jnp.exp(last_sum - summed) * (segs == last_seg).astype(F32)
    keeps = jnp.exp(last_sum) * (last_seg == before).astype(F32)
    stacked = jnp.concatenate(
        [summed, strength, opening, strength * opening, closing, jnp.zeros((BLOCK - 40, BLOCK), F32)], axis=0
    )
    cols = stacked.T
    wcols = jnp.concatenate(level_weights, axis=0).T

    def column(kind, block):
        return cols[:, kind * 8 + block : kind * 8 + block + 1]

    def weight(level, block):
        at = block * 16 + weight_column(level)
        return wcols[:, at : at + 1]

    qn = unit_rows(q, ones)
    kn = unit_rows(k, ones)
    grams = [
        dot_rows(jnp.concatenate([kn[rows_of(b)], qn[rows_of(b)]], axis=0), kn[rows_of(b)]) for b in every
    ]
    fading = [jnp.exp(column(0, b) - summed[b : b + 1, :] + far_ref[b]) for b in every]
    lower = [(column(1, b) * fading[b] * grams[b][:BLOCK]).astype(BF16) for b in every]
    scores = [(fading[b] * grams[b][BLOCK:]).astype(BF16) for b in every]
    eye = jnp.where(row == col, 1.0, 0.0).astype(BF16)
    inverse = [eye - lower[b] * pair_ref[0] for b in every]
    for step in range(1, 7):
        mask = pair_ref[step]
        half = [dot(inverse[b], lower[b] * mask).astype(BF16) for b in every]
        inverse = [inverse[b] - dot(half[b], inverse[b]).astype(BF16) for b in every]
    right = [
        jnp.concatenate(
            [
                (column(1, b) * v[rows_of(b)].astype(F32)).astype(BF16),
                (column(3, b) * kn[rows_of(b)].astype(F32)).astype(BF16),
            ],
            axis=1,
        )
        for b in every
    ]
    solved = [dot(inverse[b], right[b]).astype(BF16) for b in every]
    read = [dot(scores[b], solved[b]) for b in every]
    out = [weight(0, b) * read[b][:, :WIDTH] for b in every]
    reads = [column(2, b) * qn[rows_of(b)].astype(F32) - read[b][:, WIDTH:] for b in every]
    ended = [(column(4, b) * kn[rows_of(b)].astype(F32)).astype(BF16) for b in every]
    joined = [dot_columns(ended[b], solved[b]) for b in every]
    fresh = [joined[b][:, :WIDTH] for b in every]
    erase = [joined[b][:, WIDTH:] for b in every]
    keep = [keeps[b : b + 1] for b in every]
    for level in range(1, 4):
        span = 1 << (level - 1)
        fresh2, erase2, keep2 = [], [], []
        for pair in range(len(fresh) // 2):
            e, o = 2 * pair, 2 * pair + 1
            later = [b for b in every if b // span == o]
            stack = jnp.concatenate([reads[b] for b in later] + [erase[o]], axis=0).astype(BF16)
            both = dot(stack, jnp.concatenate([fresh[e], erase[e]], axis=1).astype(BF16))
            for at, b in enumerate(later):
                part = both[at * BLOCK : (at + 1) * BLOCK]
                out[b] = out[b] + weight(level, b) * part[:, :WIDTH]
                reads[b] = keep[e] * reads[b] - part[:, WIDTH:]
            part = both[len(later) * BLOCK :]
            fresh2.append(keep[o] * fresh[e] - part[:, :WIDTH] + fresh[o])
            erase2.append(keep[o] * erase[e] + keep[e] * erase[o] - part[:, WIDTH:])
            keep2.append(keep[e] * keep[o])
        fresh, erase, keep = fresh2, erase2, keep2
    return out, reads, fresh[0], erase[0], keep[0], wcols


def finish_block(out, read, states, columns, gate, gain, ones):
    wide = read.astype(F32)
    lhs = jnp.concatenate([(column * wide).astype(BF16) for column in columns], axis=1)
    total = out + dot(lhs, states)
    mean = dot((total * total).astype(BF16), ones) * (1.0 / WIDTH)
    gate = gate.astype(F32)
    silu = gate / (1.0 + jnp.exp(-gate))
    return (total * lax.rsqrt(mean + EPSILON) * gain * silu).astype(BF16)


STAGES = 6
HOPS = (1, 2, 4, 14, 16, 48)
STEPS = HEADS_HERE + STAGES + 1
MESH = pl.DeviceIdType.MESH


def layer_kernel(
    q_hbm,
    k_hbm,
    v_hbm,
    gate_hbm,
    w_hbm,
    decay_ref,
    strength_ref,
    weights_ref,
    seg_ref,
    gain_ref,
    result_ref,
    q_ref,
    k_ref,
    v_ref,
    gate_ref,
    whole_ref,
    far_ref,
    pair_ref,
    spread_ref,
    out_ref,
    read_ref,
    column_ref,
    normed_ref,
    gathered_ref,
    sent_ref,
    came_ref,
    total_ref,
    keep_ref,
    prefix_ref,
    prekeep_ref,
    chip_ref,
    states_ref,
    segs_ref,
    before_ref,
    load_sem,
    own_sem,
    seg_sem,
    sent_sem,
    came_sem,
    chip_sent_sem,
    chip_came_sem,
    out_sem,
    in_sem,
    w_sent_sem,
    w_came_sem,
):
    ctx = lax.axis_index("ctx")
    x = lax.axis_index("head")
    core = lax.rem(ctx, 2)
    count = lax.axis_size("ctx")
    right, left = lax.rem(x + 1, 4), lax.rem(x + 3, 4)
    after, ahead = lax.rem(ctx + 1, count), lax.rem(ctx + count - 1, count)

    def flipped(hop):
        place, rest = 0, ctx
        for bit in range(6):
            digit = lax.rem(rest, 2)
            rest = rest // 2
            place = place + ((1 - digit) if hop >> bit & 1 else digit) * (1 << bit)
        return place

    def remote(source, target, sent, came, axis, at):
        return pltpu.make_async_remote_copy(
            src_ref=source,
            dst_ref=target,
            send_sem=sent,
            recv_sem=came,
            device_id={axis: at},
            device_id_type=MESH,
        )

    partners = [("ctx", flipped(hop)) for hop in HOPS]
    partners += [("head", lax.rem(x + d, 4)) for d in (1, 2, 3)] + [("ctx", after), ("ctx", ahead)]

    sources = ((q_hbm, q_ref), (k_hbm, k_ref), (v_hbm, v_ref), (gate_hbm, gate_ref))

    def load(which, head):
        source, target = sources[which]
        columns = pl.ds(pl.multiple_of(head * WIDTH, WIDTH), WIDTH)
        return pltpu.make_async_copy(source.at[:, columns], target.at[head], load_sem.at[which, head])

    own_w = pltpu.make_async_copy(w_hbm, whole_ref.at[x], own_sem)
    quarters = [pl.ds(pl.multiple_of(core * 256 + part * 128, 128), 128) for part in range(2)]
    half = pl.ds(pl.multiple_of(core * 256, 256), 256)
    other_core = flipped(1)

    def w_copy(at, source, shard, rows, axis, to):
        return remote(source, whole_ref.at[shard, rows], w_sent_sem.at[at], w_came_sem.at[at], axis, to)

    w_first = [
        w_copy(0, w_hbm.at[quarters[0]], x, quarters[0], "head", right),
        w_copy(1, w_hbm.at[quarters[1]], x, quarters[1], "head", left),
        w_copy(2, w_hbm.at[quarters[1]], x, quarters[1], "head", right),
        w_copy(3, w_hbm.at[quarters[0]], x, quarters[0], "head", left),
    ]
    w_relay = [
        w_copy(4, whole_ref.at[left, quarters[0]], left, quarters[0], "head", right),
        w_copy(5, whole_ref.at[right, quarters[1]], right, quarters[1], "head", left),
    ]
    w_core = [
        w_copy(6 + at, whole_ref.at[shard, half], shard, half, "ctx", other_core)
        for at, shard in enumerate((left, right, lax.rem(x + 2, 4)))
    ]
    seg_copy = remote(segs_ref, before_ref, seg_sem.at[0], seg_sem.at[1], "ctx", after)

    def message(stage, head):
        return remote(
            sent_ref.at[stage, head],
            came_ref.at[stage, head],
            sent_sem.at[stage, head],
            came_sem.at[stage, head],
            "ctx",
            flipped(HOPS[stage]),
        )

    def chip_copy(head):
        return remote(
            chip_ref.at[head], chip_ref.at[head], chip_sent_sem.at[head], chip_came_sem.at[head], "ctx", other_core
        )

    def spread_copy(head, d):
        to = lax.rem(x + d, 4)
        rows = pl.ds(pl.multiple_of(to * 256, 256), 256)
        columns = pl.ds(pl.multiple_of(x * 512 + head * WIDTH, WIDTH), WIDTH)
        return remote(
            normed_ref.at[head, rows],
            gathered_ref.at[:, columns],
            out_sem.at[head, d - 1],
            in_sem.at[head, d - 1],
            "head",
            to,
        )

    def owns(head):
        return lax.rem(head, 2) == core

    def write_message(stage, head, body, keep):
        sent_ref[stage, head, :BLOCK, :] = body.astype(BF16)
        first, second, third = split3(keep)
        sent_ref[stage, head, BLOCK:, :] = jnp.concatenate(
            [first.astype(F32), second.astype(F32), third.astype(F32), jnp.zeros((13, 2 * WIDTH), F32)], axis=0
        ).astype(BF16)

    def read_keep(stage, head):
        tail = came_ref[stage, head, BLOCK:, :].astype(F32)
        return tail[0:1] + tail[1:2] + tail[2:3]

    def flag_row():
        return (before_ref[7:8, WIDTH - 1 :] == segs_ref[0:1, :1]).astype(F32)

    def store_total(head, body, keep):
        total_ref[head] = body
        keep_ref[head] = jnp.broadcast_to(keep, (8, 2 * WIDTH))

    def local_step(head):
        for which in range(3):
            load(which, head).wait()
        weights = [
            part
            for b in range(BLOCKS)
            for part in (weights_ref[head, 0:8, rows_of(b)], weights_ref[head, 4:12, rows_of(b)])
        ]
        out, reads, fresh, erase, keep, wcols = head_terms(
            q_ref[head],
            k_ref[head],
            v_ref[head],
            spread_ref[0, head],
            spread_ref[1, head],
            weights,
            segs_ref[...],
            far_ref,
            pair_ref,
        )
        column_ref[head] = wcols
        for b in range(BLOCKS):
            out_ref[head, rows_of(b), :] = out[b]
            read_ref[head, rows_of(b), :] = reads[b].astype(BF16)

        @pl.when(head == 0)
        def _():
            seg_copy.wait_recv()

        flag = jnp.broadcast_to(flag_row(), (1, WIDTH))
        body = jnp.concatenate([fresh, flag * erase], axis=1)
        keep = jnp.concatenate([flag * keep, flag * keep], axis=1)
        store_total(head, body, keep)
        write_message(0, head, body, keep)
        message(0, head).start()

    def combine(stage, head, upper, with_prefix, with_total):
        other = came_ref[stage, head, :BLOCK, :]
        other_keep = read_keep(stage, head)
        mine = total_ref[head]
        keep = keep_ref[head, 0:1, :]
        columns = slice((stage - 1) * WIDTH, stage * WIDTH)
        wide = other.astype(F32)
        if upper:
            parts = []
            if with_prefix:
                prefix = prefix_ref[head]
                parts.append(prefix.astype(BF16))
            if with_total:
                parts.append(mine[:, WIDTH:].astype(BF16))
            both = dot(jnp.concatenate(parts, axis=0) if len(parts) > 1 else parts[0], other)
            if with_prefix:
                moved = both[:BLOCK]
                prekeep = prekeep_ref[head, 0:1, :]
                chip_ref[head, :, columns] = (prekeep[:, :WIDTH] * wide[:, :WIDTH] - moved[:, :WIDTH]).astype(BF16)
                prefix_ref[head] = (
                    prekeep[:, WIDTH:] * wide[:, WIDTH:] + other_keep[:, WIDTH:] * prefix - moved[:, WIDTH:]
                )
                prekeep_ref[head] = jnp.broadcast_to(prekeep * other_keep, (8, 2 * WIDTH))
            if with_total:
                carried = jnp.concatenate([mine[:, :WIDTH], other_keep[:, WIDTH:] * mine[:, WIDTH:]], axis=1)
                body = keep * wide + carried - both[len(parts) * BLOCK - BLOCK :]
        else:
            if with_prefix:
                chip_ref[head, :, columns] = jnp.zeros((BLOCK, WIDTH), BF16)
            if with_total:
                moved = dot(other[:, WIDTH:], mine.astype(BF16))
                carried = jnp.concatenate([wide[:, :WIDTH], keep[:, WIDTH:] * wide[:, WIDTH:]], axis=1)
                body = other_keep * mine + carried - moved
        if with_total:
            keep = keep * other_keep
            store_total(head, body, keep)
            write_message(stage + 1, head, body, keep)

    def join_step(stage, head):
        last = stage == STAGES - 1

        def both_sides():
            digit = lax.rem(ctx // (1 << stage), 2)

            @pl.when(digit == 1)
            def _():
                combine(stage, head, True, stage > 0, not last)

            @pl.when(digit == 0)
            def _():
                combine(stage, head, False, stage > 0, not last)

        if stage == 0:
            message(0, head).wait_recv()

        @pl.when(owns(head))
        def _():
            if stage == 0:
                prefix_ref[head] = jnp.zeros((BLOCK, WIDTH), F32)
                prekeep_ref[head] = jnp.ones((8, 2 * WIDTH), F32)
            else:
                message(stage, head).wait_recv()
            both_sides()
            if last:
                chip_copy(head).start()
            else:
                message(stage + 1, head).start()

    def finish_step(head):
        @pl.when(jnp.logical_not(owns(head)))
        def _():
            chip_copy(head).wait_recv()

        load(3, head).wait()
        flag = jnp.broadcast_to(flag_row(), (1, WIDTH))
        chip = chip_ref[head]

        @pl.when(core == 0)
        def _():
            states_ref[:BLOCK, :] = jnp.zeros((BLOCK, WIDTH), BF16)
            for level in range(5):
                part = chip[:, level * WIDTH : (level + 1) * WIDTH].astype(F32)
                states_ref[(level + 1) * BLOCK : (level + 2) * BLOCK, :] = (flag * part).astype(BF16)

        @pl.when(core == 1)
        def _():
            other = came_ref[0, head, :BLOCK, :]
            keep = read_keep(0, head)[:, :WIDTH]
            states_ref[:BLOCK, :] = (flag * other[:, :WIDTH].astype(F32)).astype(BF16)
            moved = dot(other[:, WIDTH:], chip)
            for level in range(5):
                columns = slice(level * WIDTH, (level + 1) * WIDTH)
                part = keep * chip[:, columns].astype(F32) - moved[:, columns]
                states_ref[(level + 1) * BLOCK : (level + 2) * BLOCK, :] = (flag * part).astype(BF16)

        ones = jnp.ones((WIDTH, WIDTH), BF16)
        states = states_ref[...]
        for b in range(BLOCKS):
            columns = [
                column_ref[head, :, b * 16 + weight_column(level) : b * 16 + weight_column(level) + 1]
                for level in range(4, 10)
            ]
            normed_ref[head, rows_of(b), :] = finish_block(
                out_ref[head, rows_of(b), :],
                read_ref[head, rows_of(b), :],
                states,
                columns,
                gate_ref[head, rows_of(b), :],
                gain_ref[...],
                ones,
            )
        for d in (1, 3, 2):
            spread_copy(head, d).start()
        rows = pl.ds(pl.multiple_of(x * 256, 256), 256)
        columns = pl.ds(pl.multiple_of(x * 512 + head * WIDTH, WIDTH), WIDTH)
        gathered_ref[:, columns] = normed_ref[head, rows, :]

    for head in range(HEADS_HERE):
        for which in range(4):
            load(which, head).start()
    own_w.start()
    segs_ref[...] = seg_ref[...].astype(F32)
    barrier = pltpu.get_barrier_semaphore()
    for axis, at in partners:
        pl.semaphore_signal(barrier, inc=1, device_id={axis: at}, device_id_type=MESH)
    pl.semaphore_wait(barrier, len(partners))
    seg_copy.start()
    for copy in w_first:
        copy.start()
    prepare_masks(seg_ref, far_ref, pair_ref)
    for source, at in ((decay_ref, 0), (strength_ref, 1)):
        for each in range(HEADS_HERE):
            for b in range(BLOCKS):
                spread_ref[at, each, b : b + 1, :] = source[each : each + 1, rows_of(b)]

    def step(t, carry):
        @pl.when(t < HEADS_HERE)
        def _():
            local_step(t)

        for stage in reversed(range(STAGES)):
            head = t - 1 - stage

            @pl.when((head >= 0) & (head < HEADS_HERE))
            def _():
                join_step(stage, head)

        @pl.when(t == 5)
        def _():
            for at in range(2):
                w_first[at].wait_recv()
                w_relay[at].start()

        @pl.when(t == 7)
        def _():
            for at in range(2):
                w_first[2 + at].wait_recv()
                w_core[at].start()

        @pl.when(t >= STAGES + 1)
        def _():
            finish_step(t - STAGES - 1)

        return carry

    lax.fori_loop(0, STEPS, step, 0)
    for copy in w_relay:
        copy.wait_recv()
    w_core[2].start()
    own_w.wait()
    for copy in w_core:
        copy.wait_recv()
    for head in range(HEADS_HERE):
        for d in (1, 2, 3):
            spread_copy(head, d).wait_recv()

    def project(at, carry):
        columns = pl.ds(pl.multiple_of(at * 256, 256), 256)
        total = dot(gathered_ref[:, 0:512], whole_ref[0, :, columns])
        for shard in range(1, 4):
            total = total + dot(gathered_ref[:, shard * 512 : (shard + 1) * 512], whole_ref[shard, :, columns])
        result_ref[:, columns] = total.astype(BF16)
        return carry

    lax.fori_loop(0, 8, project, 0)
    seg_copy.wait_send()
    for copy in w_first + w_relay + w_core:
        copy.wait_send()
    for head in range(HEADS_HERE):
        message(0, head).wait_send()
        for d in (1, 2, 3):
            spread_copy(head, d).wait_send()

        @pl.when(owns(head))
        def _():
            for stage in range(1, STAGES):
                message(stage, head).wait_send()
            chip_copy(head).wait_send()


def shards(queries, keys, values, log_decay, write_strength, level_weights, segment, out_gate, norm_gain, w_out):
    far = pl.BlockSpec(memory_space=pl.ANY)
    near = pl.BlockSpec(memory_space=pltpu.VMEM)
    tall = (HEADS_HERE, TOKENS_HERE, WIDTH)
    return pl.pallas_call(
        layer_kernel,
        out_shape=jax.ShapeDtypeStruct((256, 2048), BF16),
        in_specs=[far] * 5 + [near] * 5,
        out_specs=near,
        scratch_shapes=[
            pltpu.VMEM(tall, BF16),
            pltpu.VMEM(tall, BF16),
            pltpu.VMEM(tall, BF16),
            pltpu.VMEM(tall, BF16),
            pltpu.VMEM((4, 512, 2048), BF16),
            pltpu.VMEM((BLOCKS, BLOCK, BLOCK), F32),
            pltpu.VMEM((7, BLOCK, BLOCK), BF16),
            pltpu.VMEM((2, HEADS_HERE, BLOCKS, BLOCK), F32),
            pltpu.VMEM(tall, F32),
            pltpu.VMEM(tall, BF16),
            pltpu.VMEM((HEADS_HERE, BLOCK, BLOCK), F32),
            pltpu.VMEM(tall, BF16),
            pltpu.VMEM((256, 2048), BF16),
            pltpu.VMEM((STAGES, HEADS_HERE, MESSAGE_ROWS, 2 * WIDTH), BF16),
            pltpu.VMEM((STAGES, HEADS_HERE, MESSAGE_ROWS, 2 * WIDTH), BF16),
            pltpu.VMEM((HEADS_HERE, BLOCK, 2 * WIDTH), F32),
            pltpu.VMEM((HEADS_HERE, 8, 2 * WIDTH), F32),
            pltpu.VMEM((HEADS_HERE, BLOCK, WIDTH), F32),
            pltpu.VMEM((HEADS_HERE, 8, 2 * WIDTH), F32),
            pltpu.VMEM((HEADS_HERE, BLOCK, 5 * WIDTH), BF16),
            pltpu.VMEM((6 * BLOCK, WIDTH), BF16),
            pltpu.VMEM((BLOCKS, BLOCK), F32),
            pltpu.VMEM((BLOCKS, BLOCK), F32),
            pltpu.SemaphoreType.DMA((4, HEADS_HERE)),
            pltpu.SemaphoreType.DMA,
            pltpu.SemaphoreType.DMA((2,)),
            pltpu.SemaphoreType.DMA((STAGES, HEADS_HERE)),
            pltpu.SemaphoreType.DMA((STAGES, HEADS_HERE)),
            pltpu.SemaphoreType.DMA((HEADS_HERE,)),
            pltpu.SemaphoreType.DMA((HEADS_HERE,)),
            pltpu.SemaphoreType.DMA((HEADS_HERE, 3)),
            pltpu.SemaphoreType.DMA((HEADS_HERE, 3)),
            pltpu.SemaphoreType.DMA((9,)),
            pltpu.SemaphoreType.DMA((9,)),
        ],
        compiler_params=pltpu.CompilerParams(
            collective_id=0, has_side_effects=True, vmem_limit_bytes=52 << 20
        ),
        cost_estimate=pl.CostEstimate(flops=24_000_000_000, bytes_accessed=16_000_000, transcendentals=0),
    )(
        queries,
        keys,
        values,
        out_gate,
        w_out,
        log_decay,
        write_strength,
        level_weights,
        segment.reshape(BLOCKS, BLOCK),
        norm_gain.reshape(1, WIDTH),
    )


def solution(mesh):
    placed = (
        P("ctx", "head"),
        P("ctx", "head"),
        P("ctx", "head"),
        P("head", "ctx"),
        P("head", "ctx"),
        P("head", None, "ctx"),
        P("ctx"),
        P("ctx", "head"),
        P(),
        P("head", None),
    )
    return jax.shard_map(
        shards, mesh=mesh, in_specs=placed, out_specs=P(("ctx", "head"), None), check_vma=False
    )
```

```python
import jax
import jax.numpy as jnp
from jax import lax
from jax.experimental import pallas as pl
from jax.experimental.pallas import tpu as pltpu
from jax.sharding import PartitionSpec as P

BLOCK = 128
BLOCKS = 8
TOKENS_HERE = 1024
HEADS_HERE = 4
WIDTH = 128
LEVELS = 12
EPSILON = 1e-06
FAR = -1e4
MESSAGE_ROWS = 144

F32 = jnp.float32
BF16 = jnp.bfloat16


def dot(left, right):
    return jnp.dot(left, right, preferred_element_type=F32)


def dot_rows(left, right):
    return lax.dot_general(left, right, (((1,), (1,)), ((), ())), preferred_element_type=F32)


def dot_columns(left, right):
    return lax.dot_general(left, right, (((0,), (0,)), ((), ())), preferred_element_type=F32)


def split3(value):
    first = value.astype(BF16)
    rest = value - first.astype(F32)
    second = rest.astype(BF16)
    third = (rest - second.astype(F32)).astype(BF16)
    return first, second, third


def rows_of(block):
    return slice(block * BLOCK, (block + 1) * BLOCK)


def prepare_masks(seg_ref, far_ref, pair_ref):
    row = lax.broadcasted_iota(jnp.int32, (BLOCK, BLOCK), 0)
    col = lax.broadcasted_iota(jnp.int32, (BLOCK, BLOCK), 1)
    segs = seg_ref[...].astype(F32)
    padded = jnp.concatenate([segs, jnp.zeros((BLOCK - BLOCKS, BLOCK), F32)], axis=0)
    seg_cols = padded.T
    for block in range(BLOCKS):
        same = seg_cols[:, block : block + 1] == segs[block : block + 1, :]
        far_ref[block] = jnp.where(same & (row >= col), 0.0, FAR)
    for step in range(7):
        size = 1 << step
        chosen = (row // size == col // size + 1) & (row // size % 2 == 1)
        pair_ref[step] = jnp.where(chosen, 1.0, 0.0).astype(BF16)


def unit_rows(rows, ones):
    wide = rows.astype(F32)
    total = dot((wide * wide).astype(BF16), ones)
    return (wide * lax.rsqrt(total + EPSILON)).astype(BF16)


def columns_of(rows):
    return jnp.concatenate([rows, jnp.zeros((BLOCK - rows.shape[0], BLOCK), F32)], axis=0).T


def column_at(columns, kind, block):
    at = kind * BLOCKS + block
    return columns[:, at : at + 1]


def summary_terms(heads, k_ref, v_ref, spread_ref, segs, far_ref, pair_ref, keys_ref, fading_ref, solved_ref, node_ref, keeps_ref, column_ref, between):
    row = lax.broadcasted_iota(jnp.int32, (BLOCK, BLOCK), 0)
    col = lax.broadcasted_iota(jnp.int32, (BLOCK, BLOCK), 1)
    every = range(BLOCKS)
    all_blocks = [(h, b) for h in range(len(heads)) for b in every]
    ones = jnp.ones((BLOCK, BLOCK), BF16)
    upto = jnp.where(row <= col, 1.0, 0.0).astype(BF16)
    last_seg = jnp.broadcast_to(segs[:, BLOCK - 1 :], (BLOCKS, BLOCK))
    first_seg = jnp.broadcast_to(segs[:, :1], (BLOCKS, BLOCK))
    before = jnp.concatenate([first_seg[:1], last_seg[:-1]], axis=0)
    opens = (segs == before).astype(F32)
    closes = (segs == last_seg).astype(F32)
    through = (last_seg == before).astype(F32)
    summed, columns, keep = [], [], []
    for head in heads:
        strength = spread_ref[1, head]
        total = sum(dot(part, upto) for part in split3(spread_ref[0, head]))
        last_sum = jnp.broadcast_to(total[:, BLOCK - 1 :], (BLOCKS, BLOCK))
        opening = jnp.exp(total) * opens
        closing = jnp.exp(last_sum - total) * closes
        keeps = jnp.exp(last_sum) * through
        columns.append(
            columns_of(jnp.concatenate([total, strength, opening, strength * opening, closing], axis=0))
        )
        summed.append(total)
        keep.append([keeps[b : b + 1] for b in every])
        column_ref[head] = columns[-1]
    kn = {}
    for h, head in enumerate(heads):
        unit = unit_rows(k_ref[head], ones)
        for b in every:
            kn[h, b] = unit[rows_of(b)]
    grams = {i: dot_rows(kn[i], kn[i]) for i in all_blocks}
    lower = {}
    for h, b in all_blocks:
        fading = jnp.exp(column_at(columns[h], 0, b) - summed[h][b : b + 1, :] + far_ref[b])
        fading_ref[heads[h], b] = fading
        lower[h, b] = (column_at(columns[h], 1, b) * fading * grams[h, b]).astype(BF16)
    between()
    eye = jnp.where(row == col, 1.0, 0.0).astype(BF16)
    inverse = {i: eye - lower[i] * pair_ref[0] for i in all_blocks}
    for step in range(1, 7):
        mask = pair_ref[step]
        half = {i: dot(inverse[i], lower[i] * mask).astype(BF16) for i in all_blocks}
        inverse = {i: inverse[i] - dot(half[i], inverse[i]).astype(BF16) for i in all_blocks}
    joined = {}
    for h, b in all_blocks:
        wide = kn[h, b].astype(F32)
        right = jnp.concatenate(
            [
                (column_at(columns[h], 1, b) * v_ref[heads[h], rows_of(b), :].astype(F32)).astype(BF16),
                (column_at(columns[h], 3, b) * wide).astype(BF16),
            ],
            axis=1,
        )
        solved = dot(inverse[h, b], right).astype(BF16)
        solved_ref[heads[h], b] = solved
        ended = (column_at(columns[h], 4, b) * wide).astype(BF16)
        joined[h, b] = dot_columns(ended, solved)
        keys_ref[heads[h], rows_of(b), :] = kn[h, b]
    nodes = [[joined[h, b] for b in every] for h in range(len(heads))]
    first = 0
    for level in range(3):
        many = len(nodes[0]) // 2
        for h, head in enumerate(heads):
            merged, kept = [], []
            for pair in range(many):
                early, late = nodes[h][2 * pair], nodes[h][2 * pair + 1]
                keep_e, keep_o = keep[h][2 * pair], keep[h][2 * pair + 1]
                node = early.astype(BF16)
                node_ref[head, first + pair] = node
                keeps_ref[head, first + pair : first + pair + 1, :] = keep_e
                moved = dot(late[:, WIDTH:].astype(BF16), node)
                carried = jnp.concatenate([late[:, :WIDTH], keep_e * late[:, WIDTH:]], axis=1)
                merged.append(jnp.concatenate([keep_o, keep_o], axis=1) * early + carried - moved)
                kept.append(keep_e * keep_o)
            nodes[h], keep[h] = merged, kept
        first = first + many
    return [(nodes[h][0], keep[h][0]) for h in range(len(heads))]


def readout_terms(head, q_ref, weight_ref, keys_ref, fading_ref, solved_ref, node_ref, keeps_ref, column_ref, out_ref, weighted_ref):
    every = range(BLOCKS)
    ones = jnp.ones((BLOCK, BLOCK), BF16)
    columns = column_ref[head]
    wcols = weight_ref[head].T

    def weight(level, block):
        at = block * 16 + level
        return wcols[:, at : at + 1]

    qn = unit_rows(q_ref[head], ones)
    scores = [
        (fading_ref[head, b] * dot_rows(qn[rows_of(b)], keys_ref[head, rows_of(b), :])).astype(BF16) for b in every
    ]
    both = [dot(scores[b], solved_ref[head, b]) for b in every]
    out = [weight(0, b) * both[b][:, :WIDTH] for b in every]
    reads = [column_at(columns, 2, b) * qn[rows_of(b)].astype(F32) - both[b][:, WIDTH:] for b in every]
    first = 0
    for level in range(1, 4):
        span = 1 << (level - 1)
        many = BLOCKS // (2 * span)
        for pair in range(many):
            later = [b for b in every if b // span == 2 * pair + 1]
            stack = jnp.concatenate([reads[b] for b in later], axis=0).astype(BF16)
            moved = dot(stack, node_ref[head, first + pair])
            keep = keeps_ref[head, first + pair : first + pair + 1, :]
            for at, b in enumerate(later):
                part = moved[at * BLOCK : (at + 1) * BLOCK]
                out[b] = out[b] + weight(level, b) * part[:, :WIDTH]
                reads[b] = keep * reads[b] - part[:, WIDTH:]
        first = first + many
    for b in every:
        out_ref[head, rows_of(b), :] = out[b]
        weighted_ref[head, rows_of(b), :] = jnp.concatenate(
            [(weight(level, b) * reads[b]).astype(BF16) for level in range(4, 10)], axis=1
        )

MESH = pl.DeviceIdType.MESH
GROUPS = 2


def joined(late, early):
    keep_l, body_l = late
    keep_e, body_e = early
    moved = dot(body_l[:, WIDTH:].astype(BF16), body_e.astype(BF16))
    carried = jnp.concatenate([body_l[:, :WIDTH], keep_e[:, WIDTH:] * body_l[:, WIDTH:]], axis=1)
    return keep_l * keep_e, keep_l * body_e + carried - moved


def without_state(summary):
    keep, body = summary
    return keep, jnp.concatenate([jnp.zeros((BLOCK, WIDTH), F32), body[:, WIDTH:]], axis=1)


def keep_rows(keep):
    first, second, third = split3(keep)
    return jnp.concatenate(
        [first.astype(F32), second.astype(F32), third.astype(F32), jnp.zeros((13, 2 * WIDTH), F32)], axis=0
    ).astype(BF16)


def layer_kernel(
    q_hbm,
    k_hbm,
    v_hbm,
    gate_hbm,
    w_hbm,
    decay_hbm,
    strength_hbm,
    weights_hbm,
    seg_hbm,
    gain_hbm,
    result_ref,
    q_ref,
    k_ref,
    v_ref,
    gate_ref,
    whole_ref,
    decay_ref,
    strength_ref,
    weights_ref,
    seg_ref,
    gain_ref,
    far_ref,
    pair_ref,
    spread_ref,
    weight_ref,
    keys_ref,
    fading_ref,
    solved_ref,
    node_ref,
    keeps_ref,
    column_ref,
    out_ref,
    weighted_ref,
    silu_ref,
    normed_ref,
    gathered_ref,
    sum_ref,
    core_sent_ref,
    core_came_ref,
    quad_ref,
    oct_sent_ref,
    oct_ref,
    total_ref,
    keep_ref,
    prefix_ref,
    prekeep_ref,
    chip_ref,
    segs_ref,
    before_ref,
    load_sem,
    small_sem,
    own_sem,
    seg_sem,
    core_sem,
    quad_sem,
    oct_sem,
    chip_sem,
    out_sem,
    in_sem,
    w_sent_sem,
    w_came_sem,
):
    ctx = lax.axis_index("ctx")
    x = lax.axis_index("head")
    core = lax.rem(ctx, 2)
    z = lax.rem(ctx // 2, 8)
    y = ctx // 16
    zq = lax.rem(z, 4)
    zh = z // 4
    place = 2 * y + zh
    count = lax.axis_size("ctx")
    right, left = lax.rem(x + 1, 4), lax.rem(x + 3, 4)
    after, ahead = lax.rem(ctx + 1, count), lax.rem(ctx + count - 1, count)
    other_core = ctx + 1 - 2 * core

    def at(y_to, z_to):
        return (y_to * 8 + z_to) * 2 + core

    def quad_to(d):
        return at(y, zh * 4 + lax.rem(zq + d, 4))

    def oct_to(d):
        to = lax.rem(place + d, 8)
        half = lax.rem(to, 2)
        across = zh + half - 2 * zh * half
        return at(to // 2, z + across * (7 - 2 * z))

    def remote(source, target, sent, came, axis, to):
        return pltpu.make_async_remote_copy(
            src_ref=source,
            dst_ref=target,
            send_sem=sent,
            recv_sem=came,
            device_id={axis: to},
            device_id_type=MESH,
        )

    partners = [("ctx", other_core), ("ctx", after), ("ctx", ahead)]
    partners += [("ctx", quad_to(d)) for d in (1, 2, 3)]
    partners += [("ctx", oct_to(d)) for d in range(1, 8)]
    partners += [("head", lax.rem(x + d, 4)) for d in (1, 2, 3)]

    sources = ((k_hbm, k_ref), (v_hbm, v_ref), (q_hbm, q_ref), (gate_hbm, gate_ref))

    def load(which, head):
        source, target = sources[which]
        columns = slice(head * WIDTH, (head + 1) * WIDTH)
        return pltpu.make_async_copy(source.at[:, columns], target.at[head], load_sem.at[which, head])

    smalls = [
        pltpu.make_async_copy(source, target, small_sem.at[n])
        for n, (source, target) in enumerate(
            (
                (seg_hbm, seg_ref),
                (decay_hbm, decay_ref),
                (strength_hbm, strength_ref),
                (weights_hbm, weights_ref),
                (gain_hbm, gain_ref),
            )
        )
    ]
    own_w = pltpu.make_async_copy(w_hbm, whole_ref.at[x], own_sem)
    quarters = [pl.ds(pl.multiple_of(core * 256 + part * 128, 128), 128) for part in range(2)]
    half_rows = pl.ds(pl.multiple_of(core * 256, 256), 256)

    def w_copy(n, source, shard, rows, axis, to):
        return remote(source, whole_ref.at[shard, rows], w_sent_sem.at[n], w_came_sem.at[n], axis, to)

    w_first = [
        w_copy(0, w_hbm.at[quarters[0]], x, quarters[0], "head", right),
        w_copy(1, w_hbm.at[quarters[1]], x, quarters[1], "head", left),
        w_copy(2, w_hbm.at[quarters[1]], x, quarters[1], "head", right),
        w_copy(3, w_hbm.at[quarters[0]], x, quarters[0], "head", left),
    ]
    w_relay = [
        w_copy(4, whole_ref.at[left, quarters[0]], left, quarters[0], "head", right),
        w_copy(5, whole_ref.at[right, quarters[1]], right, quarters[1], "head", left),
    ]
    w_core = [
        w_copy(6 + n, whole_ref.at[shard, half_rows], shard, half_rows, "ctx", other_core)
        for n, shard in enumerate((left, right, lax.rem(x + 2, 4)))
    ]
    seg_copy = remote(segs_ref, before_ref, seg_sem.at[0], seg_sem.at[1], "ctx", after)

    def core_copy(head):
        return remote(
            core_sent_ref.at[head], core_came_ref.at[head], core_sem.at[0, head], core_sem.at[1, head], "ctx", other_core
        )

    def quad_copy(group, d):
        mine = quad_ref.at[group, zq]
        return remote(mine, mine, quad_sem.at[0, group, d - 1], quad_sem.at[1, group, d - 1], "ctx", quad_to(d))

    def oct_copy(group, d):
        return remote(
            oct_sent_ref.at[group],
            oct_ref.at[group, place],
            oct_sem.at[0, group, d - 1],
            oct_sem.at[1, group, d - 1],
            "ctx",
            oct_to(d),
        )

    def chip_copy(group, part, head):
        mine = chip_ref.at[head, pl.ds(2 * part, 2 + part)]
        return remote(mine, mine, chip_sem.at[0, group, part], chip_sem.at[1, group, part], "ctx", other_core)

    def spread_copy(head, d):
        to = lax.rem(x + d, 4)
        rows = pl.ds(pl.multiple_of(to * 256, 256), 256)
        columns = pl.ds(pl.multiple_of(x * 512 + head * WIDTH, WIDTH), WIDTH)
        return remote(
            normed_ref.at[head, rows],
            gathered_ref.at[:, columns],
            out_sem.at[head, d - 1],
            in_sem.at[head, d - 1],
            "head",
            to,
        )

    def own_head(group):
        return 2 * group + core

    def read(ref):
        tail = ref[BLOCK:, :].astype(F32)
        return tail[0:1] + tail[1:2] + tail[2:3], ref[:BLOCK, :].astype(F32)

    def write(ref, summary):
        keep, body = summary
        ref[:BLOCK, :] = body.astype(BF16)
        ref[BLOCK:, :] = keep_rows(keep)

    def flag_row():
        same = (before_ref[7:8, WIDTH - 1 :] == segs_ref[0:1, :1]).astype(F32)
        return jnp.broadcast_to(same, (1, WIDTH))

    def summary_step(group, between):
        heads = [2 * group, 2 * group + 1]
        for head in heads:
            for which in range(2):
                load(which, head).wait()
        found = summary_terms(
            heads,
            k_ref,
            v_ref,
            spread_ref,
            segs_ref[...],
            far_ref,
            pair_ref,
            keys_ref,
            fading_ref,
            solved_ref,
            node_ref,
            keeps_ref,
            column_ref,
            between,
        )
        if group == 0:
            seg_copy.wait_recv()
        flag = flag_row()
        for head, (body, keep) in zip(heads, found):
            keep = jnp.concatenate([flag * keep, flag * keep], axis=1)
            body = jnp.concatenate([body[:, :WIDTH], flag * body[:, WIDTH:]], axis=1)
            total_ref[head] = body
            keep_ref[head] = jnp.broadcast_to(keep, (8, 2 * WIDTH))
            write(core_sent_ref.at[head], (keep, body))
            core_copy(head).start()

    def chip_step(group):
        for head in (2 * group, 2 * group + 1):
            core_copy(head).wait_recv()
        head = own_head(group)
        mine = keep_ref[head, 0:1, :], total_ref[head]
        other = read(core_came_ref.at[head])
        to = quad_ref.at[group, zq]

        @pl.when(core == 1)
        def _():
            write(to, joined(mine, other))

        @pl.when(core == 0)
        def _():
            write(to, joined(other, mine))

        for d in (1, 3, 2):
            quad_copy(group, d).start()

    def quad_step(group):
        for d in (1, 2, 3):
            quad_copy(group, d).wait_recv()
        parts = [read(quad_ref.at[group, n]) for n in range(4)]
        first, second = joined(parts[1], parts[0]), joined(parts[3], parts[2])
        write(oct_sent_ref.at[group], joined(second, first))
        for d in range(1, 8):

            @pl.when(place + d < 8)
            def _():
                oct_copy(group, d).start()

        head = own_head(group)
        odd = lax.rem(zq, 2)
        upper = zq // 2
        keep, body = read(quad_ref.at[group, odd * (zq - odd)])
        odd, upper = odd.astype(F32), upper.astype(F32)
        keep, body = odd * keep + (1.0 - odd), odd * body
        chip_ref[head, 0] = body[:, :WIDTH].astype(BF16)
        before = without_state((keep, body))
        over_keep, over = joined(before, first)
        chip_ref[head, 1] = (upper * over[:, :WIDTH]).astype(BF16)
        chip_copy(group, 0, head).start()
        keep = upper * over_keep + (1.0 - upper) * before[0]
        prekeep_ref[group] = jnp.broadcast_to(keep, (8, 2 * WIDTH))
        prefix_ref[group] = upper * over + (1.0 - upper) * before[1]

    def oct_step(group):
        for d in range(1, 8):

            @pl.when(place >= d)
            def _():
                oct_copy(group, d).wait_recv()

        head = own_head(group)
        odd, upper = lax.rem(y, 2), y // 2

        def slot(use, n):
            return read(oct_ref.at[group, use * n + (1 - use) * 7])

        prefix = without_state((prekeep_ref[group, 0:1, :], prefix_ref[group]))
        sibling = joined(slot(odd, 2 * y - 1), slot(odd, 2 * y - 2))
        pair = joined(slot(upper, 1), slot(upper, 0)), joined(slot(upper, 3), slot(upper, 2))
        over = joined(prefix, slot(zh, place - 1))
        oldest = joined(pair[1], pair[0])
        chip_ref[head, 2] = over[1][:, :WIDTH].astype(BF16)
        over = joined(without_state(over), sibling)
        chip_ref[head, 3] = over[1][:, :WIDTH].astype(BF16)
        over = joined(without_state(over), oldest)
        chip_ref[head, 4] = over[1][:, :WIDTH].astype(BF16)
        chip_copy(group, 1, head).start()

    def readout_step(head):
        load(2, head).wait()
        readout_terms(
            head,
            q_ref,
            weight_ref,
            keys_ref,
            fading_ref,
            solved_ref,
            node_ref,
            keeps_ref,
            column_ref,
            out_ref,
            weighted_ref,
        )

    def gate_step(head):
        load(3, head).wait()
        gate = gate_ref[head].astype(F32)
        silu_ref[head] = gate / (1.0 + jnp.exp(-gate)) * gain_ref[...]

    def own_states(head, first, last):
        later = core.astype(F32)
        keep, body = read(core_came_ref.at[head])
        keep = later * keep[:, :WIDTH] + (1.0 - later)
        erase = (later * body[:, WIDTH:]).astype(BF16)
        states = [chip_ref[head, n] for n in range(first, last)]
        moved = dot(erase, jnp.concatenate(states, axis=1))
        flag = flag_row()
        carried = [
            (flag * (keep * state.astype(F32) - moved[:, n * WIDTH : (n + 1) * WIDTH])).astype(BF16)
            for n, state in enumerate(states)
        ]
        if first == 0:
            carried = [(flag * later * body[:, :WIDTH]).astype(BF16)] + carried
        return jnp.concatenate(carried, axis=0)

    def await_states(group, part, head):
        @pl.when(head != own_head(group))
        def _():
            chip_copy(group, part, head).wait_recv()

    def near_step(group, head):
        await_states(group, 0, head)
        states = own_states(head, 0, 2)
        out_ref[head] += dot(weighted_ref[head, :, : 3 * WIDTH], states)

    def finish_step(group, head):
        await_states(group, 1, head)
        states = own_states(head, 2, 5)
        ones = jnp.ones((WIDTH, WIDTH), BF16)
        total = out_ref[head] + dot(weighted_ref[head, :, 3 * WIDTH :], states)
        mean = dot((total * total).astype(BF16), ones) * (1.0 / WIDTH)
        normed_ref[head] = (total * lax.rsqrt(mean + EPSILON) * silu_ref[head]).astype(BF16)
        for d in (2, 1, 3):
            spread_copy(head, d).start()
        rows = pl.ds(pl.multiple_of(x * 256, 256), 256)
        columns = pl.ds(pl.multiple_of(x * 512 + head * WIDTH, WIDTH), WIDTH)
        gathered_ref[:, columns] = normed_ref[head, rows, :]

    def finish_group(group):
        for turn in range(2):
            @pl.when(core == 0)
            def _():
                finish_step(group, 2 * group + turn)

            @pl.when(core == 1)
            def _():
                finish_step(group, 2 * group + 1 - turn)

    def project_group(group):
        for head in (2 * group, 2 * group + 1):
            for d in (1, 2, 3):
                spread_copy(head, d).wait_recv()

        def tile(n, carry):
            columns = pl.ds(pl.multiple_of(n * 256, 256), 256)
            rows = slice(group * 256, (group + 1) * 256)
            total = sum(
                dot(gathered_ref[:, shard * 512 + group * 256 : shard * 512 + (group + 1) * 256], whole_ref[shard, rows, columns])
                for shard in range(4)
            )
            if group == 0:
                sum_ref[:, columns] = total
            else:
                result_ref[:, columns] = (total + sum_ref[:, columns]).astype(BF16)
            return carry

        lax.fori_loop(0, 8, tile, 0)

    for copy in smalls[:3]:
        copy.start()
    for head in range(HEADS_HERE):
        for which in range(2):
            load(which, head).start()
    for copy in smalls[3:]:
        copy.start()
    for head in range(HEADS_HERE):
        for which in (2, 3):
            load(which, head).start()
    own_w.start()
    for group in range(GROUPS):
        for n in range(8):
            oct_ref[group, n, :BLOCK, :] = jnp.zeros((BLOCK, 2 * WIDTH), BF16)
            oct_ref[group, n, BLOCK:, :] = keep_rows(jnp.ones((1, 2 * WIDTH), F32))
    barrier = pltpu.get_barrier_semaphore()
    for axis, to in partners:
        pl.semaphore_signal(barrier, inc=1, device_id={axis: to}, device_id_type=MESH)
    smalls[0].wait()
    segs_ref[...] = seg_ref[...].astype(F32)
    prepare_masks(seg_ref, far_ref, pair_ref)
    for source, n in ((decay_ref, 0), (strength_ref, 1)):
        smalls[1 + n].wait()
        for each in range(HEADS_HERE):
            for b in range(BLOCKS):
                spread_ref[n, each, b : b + 1, :] = source[each : each + 1, rows_of(b)]
    pl.semaphore_wait(barrier, len(partners))
    seg_copy.start()
    for copy in w_first:
        copy.start()

    summary_step(0, lambda: None)
    summary_step(1, lambda: chip_step(0))
    for copy in smalls[3:]:
        copy.wait()
    for level in range(10):
        for each in range(HEADS_HERE):
            for b in range(BLOCKS):
                row = b * 16 + level
                weight_ref[each, row : row + 1, :] = weights_ref[level, each : each + 1, rows_of(b)]
    gate_step(0)
    chip_step(1)
    for n in range(2):
        w_first[n].wait_recv()
        w_relay[n].start()
    readout_step(0)
    quad_step(0)
    for head in range(1, HEADS_HERE):
        readout_step(head)
    quad_step(1)
    for n in range(2):
        w_first[2 + n].wait_recv()
        w_core[n].start()
    for head in range(1, HEADS_HERE):
        gate_step(head)
    near_step(0, 0)
    near_step(0, 1)
    oct_step(0)
    near_step(1, 2)
    near_step(1, 3)
    finish_group(0)
    for copy in w_relay:
        copy.wait_recv()
    w_core[2].start()
    oct_step(1)
    finish_group(1)
    own_w.wait()
    for copy in w_core:
        copy.wait_recv()
    project_group(0)
    project_group(1)
    seg_copy.wait_send()
    for copy in w_first + w_relay + w_core:
        copy.wait_send()
    for head in range(HEADS_HERE):
        core_copy(head).wait_send()
        for d in (1, 2, 3):
            spread_copy(head, d).wait_send()
    for group in range(GROUPS):
        for d in (1, 2, 3):
            quad_copy(group, d).wait_send()
        for part in range(2):
            chip_copy(group, part, own_head(group)).wait_send()
        for d in range(1, 8):

            @pl.when(place + d < 8)
            def _():
                oct_copy(group, d).wait_send()


def shards(queries, keys, values, log_decay, write_strength, level_weights, segment, out_gate, norm_gain, w_out):
    far = pl.BlockSpec(memory_space=pl.ANY)
    near = pl.BlockSpec(memory_space=pltpu.VMEM)
    tall = (HEADS_HERE, TOKENS_HERE, WIDTH)
    wide = (MESSAGE_ROWS, 2 * WIDTH)
    return pl.pallas_call(
        layer_kernel,
        out_shape=jax.ShapeDtypeStruct((256, 2048), BF16),
        in_specs=[far] * 10,
        out_specs=near,
        scratch_shapes=[
            pltpu.VMEM(tall, BF16),
            pltpu.VMEM(tall, BF16),
            pltpu.VMEM(tall, BF16),
            pltpu.VMEM(tall, BF16),
            pltpu.VMEM((4, 512, 2048), BF16),
            pltpu.VMEM((HEADS_HERE, TOKENS_HERE), F32),
            pltpu.VMEM((HEADS_HERE, TOKENS_HERE), F32),
            pltpu.VMEM((LEVELS, HEADS_HERE, TOKENS_HERE), F32),
            pltpu.VMEM((BLOCKS, BLOCK), jnp.int32),
            pltpu.VMEM((1, WIDTH), F32),
            pltpu.VMEM((BLOCKS, BLOCK, BLOCK), F32),
            pltpu.VMEM((7, BLOCK, BLOCK), BF16),
            pltpu.VMEM((2, HEADS_HERE, BLOCKS, BLOCK), F32),
            pltpu.VMEM((HEADS_HERE, BLOCK, BLOCK), F32),
            pltpu.VMEM(tall, BF16),
            pltpu.VMEM((HEADS_HERE, BLOCKS, BLOCK, BLOCK), F32),
            pltpu.VMEM((HEADS_HERE, BLOCKS, BLOCK, 2 * WIDTH), BF16),
            pltpu.VMEM((HEADS_HERE, 7, BLOCK, 2 * WIDTH), BF16),
            pltpu.VMEM((HEADS_HERE, 8, WIDTH), F32),
            pltpu.VMEM((HEADS_HERE, BLOCK, BLOCK), F32),
            pltpu.VMEM(tall, F32),
            pltpu.VMEM((HEADS_HERE, TOKENS_HERE, 6 * WIDTH), BF16),
            pltpu.VMEM(tall, F32),
            pltpu.VMEM(tall, BF16),
            pltpu.VMEM((256, 2048), BF16),
            pltpu.VMEM((256, 2048), F32),
            pltpu.VMEM((HEADS_HERE,) + wide, BF16),
            pltpu.VMEM((HEADS_HERE,) + wide, BF16),
            pltpu.VMEM((GROUPS, 4) + wide, BF16),
            pltpu.VMEM((GROUPS,) + wide, BF16),
            pltpu.VMEM((GROUPS, 8) + wide, BF16),
            pltpu.VMEM((HEADS_HERE, BLOCK, 2 * WIDTH), F32),
            pltpu.VMEM((HEADS_HERE, 8, 2 * WIDTH), F32),
            pltpu.VMEM((GROUPS, BLOCK, 2 * WIDTH), F32),
            pltpu.VMEM((GROUPS, 8, 2 * WIDTH), F32),
            pltpu.VMEM((HEADS_HERE, 5, BLOCK, WIDTH), BF16),
            pltpu.VMEM((BLOCKS, BLOCK), F32),
            pltpu.VMEM((BLOCKS, BLOCK), F32),
            pltpu.SemaphoreType.DMA((4, HEADS_HERE)),
            pltpu.SemaphoreType.DMA((5,)),
            pltpu.SemaphoreType.DMA,
            pltpu.SemaphoreType.DMA((2,)),
            pltpu.SemaphoreType.DMA((2, HEADS_HERE)),
            pltpu.SemaphoreType.DMA((2, GROUPS, 3)),
            pltpu.SemaphoreType.DMA((2, GROUPS, 7)),
            pltpu.SemaphoreType.DMA((2, GROUPS, 2)),
            pltpu.SemaphoreType.DMA((HEADS_HERE, 3)),
            pltpu.SemaphoreType.DMA((HEADS_HERE, 3)),
            pltpu.SemaphoreType.DMA((9,)),
            pltpu.SemaphoreType.DMA((9,)),
        ],
        compiler_params=pltpu.CompilerParams(
            collective_id=0, has_side_effects=True, vmem_limit_bytes=58 << 20
        ),
        cost_estimate=pl.CostEstimate(flops=24_000_000_000, bytes_accessed=16_000_000, transcendentals=0),
    )(
        queries,
        keys,
        values,
        out_gate,
        w_out,
        log_decay,
        write_strength,
        level_weights.transpose(1, 0, 2),
        segment.reshape(BLOCKS, BLOCK),
        norm_gain.reshape(1, WIDTH),
    )


def solution(mesh):
    placed = (
        P("ctx", "head"),
        P("ctx", "head"),
        P("ctx", "head"),
        P("head", "ctx"),
        P("head", "ctx"),
        P("head", None, "ctx"),
        P("ctx"),
        P("ctx", "head"),
        P(),
        P("head", None),
    )
    return jax.shard_map(
        shards, mesh=mesh, in_specs=placed, out_specs=P(("ctx", "head"), None), check_vma=False
    )
```

```python
import jax
import jax.numpy as jnp
from jax import lax
from jax.experimental import pallas as pl
from jax.experimental.pallas import tpu as pltpu
from jax.sharding import PartitionSpec as P

BLOCK = 128
BLOCKS = 8
TOKENS_HERE = 1024
HEADS_HERE = 4
WIDTH = 128
LEVELS = 12
EPSILON = 1e-06
FAR = -1e4
MESSAGE_ROWS = 144

F32 = jnp.float32
BF16 = jnp.bfloat16


def dot(left, right):
    return jnp.dot(left, right, preferred_element_type=F32)


def dot_rows(left, right):
    return lax.dot_general(left, right, (((1,), (1,)), ((), ())), preferred_element_type=F32)


def dot_columns(left, right):
    return lax.dot_general(left, right, (((0,), (0,)), ((), ())), preferred_element_type=F32)


def split3(value):
    first = value.astype(BF16)
    rest = value - first.astype(F32)
    second = rest.astype(BF16)
    third = (rest - second.astype(F32)).astype(BF16)
    return first, second, third


def rows_of(block):
    return slice(block * BLOCK, (block + 1) * BLOCK)


def prepare_masks(seg_ref, far_ref, pair_ref):
    row = lax.broadcasted_iota(jnp.int32, (BLOCK, BLOCK), 0)
    col = lax.broadcasted_iota(jnp.int32, (BLOCK, BLOCK), 1)
    segs = seg_ref[...].astype(F32)
    padded = jnp.concatenate([segs, jnp.zeros((BLOCK - BLOCKS, BLOCK), F32)], axis=0)
    seg_cols = padded.T
    for block in range(BLOCKS):
        same = seg_cols[:, block : block + 1] == segs[block : block + 1, :]
        far_ref[block] = jnp.where(same & (row >= col), 0.0, FAR)
    for step in range(7):
        size = 1 << step
        chosen = (row // size == col // size + 1) & (row // size % 2 == 1)
        pair_ref[step] = jnp.where(chosen, 1.0, 0.0).astype(BF16)


def unit_rows(rows, ones):
    wide = rows.astype(F32)
    total = dot((wide * wide).astype(BF16), ones)
    return (wide * lax.rsqrt(total + EPSILON)).astype(BF16)


def columns_of(rows):
    return jnp.concatenate([rows, jnp.zeros((BLOCK - rows.shape[0], BLOCK), F32)], axis=0).T


def column_at(columns, kind, block):
    at = kind * BLOCKS + block
    return columns[:, at : at + 1]


def summary_terms(heads, k_ref, v_ref, spread_ref, segs, far_ref, pair_ref, keys_ref, fading_ref, solved_ref, node_ref, keeps_ref, column_ref, between):
    row = lax.broadcasted_iota(jnp.int32, (BLOCK, BLOCK), 0)
    col = lax.broadcasted_iota(jnp.int32, (BLOCK, BLOCK), 1)
    every = range(BLOCKS)
    all_blocks = [(h, b) for h in range(len(heads)) for b in every]
    ones = jnp.ones((BLOCK, BLOCK), BF16)
    upto = jnp.where(row <= col, 1.0, 0.0).astype(BF16)
    last_seg = jnp.broadcast_to(segs[:, BLOCK - 1 :], (BLOCKS, BLOCK))
    first_seg = jnp.broadcast_to(segs[:, :1], (BLOCKS, BLOCK))
    before = jnp.concatenate([first_seg[:1], last_seg[:-1]], axis=0)
    opens = (segs == before).astype(F32)
    closes = (segs == last_seg).astype(F32)
    through = (last_seg == before).astype(F32)
    summed, columns, keep = [], [], []
    for head in heads:
        strength = spread_ref[1, head]
        total = sum(dot(part, upto) for part in split3(spread_ref[0, head]))
        last_sum = jnp.broadcast_to(total[:, BLOCK - 1 :], (BLOCKS, BLOCK))
        opening = jnp.exp(total) * opens
        closing = jnp.exp(last_sum - total) * closes
        keeps = jnp.exp(last_sum) * through
        columns.append(
            columns_of(jnp.concatenate([total, strength, opening, strength * opening, closing], axis=0))
        )
        summed.append(total)
        keep.append([keeps[b : b + 1] for b in every])
        column_ref[head] = columns[-1]
    kn = {}
    for h, head in enumerate(heads):
        unit = unit_rows(k_ref[head], ones)
        for b in every:
            kn[h, b] = unit[rows_of(b)]
    grams = {i: dot_rows(kn[i], kn[i]) for i in all_blocks}
    lower = {}
    for h, b in all_blocks:
        fading = jnp.exp(column_at(columns[h], 0, b) - summed[h][b : b + 1, :] + far_ref[b])
        fading_ref[heads[h], b] = fading
        lower[h, b] = (column_at(columns[h], 1, b) * fading * grams[h, b]).astype(BF16)
    between()
    eye = jnp.where(row == col, 1.0, 0.0).astype(BF16)
    inverse = {i: eye - lower[i] * pair_ref[0] for i in all_blocks}
    for step in range(1, 7):
        mask = pair_ref[step]
        half = {i: dot(inverse[i], lower[i] * mask).astype(BF16) for i in all_blocks}
        inverse = {i: inverse[i] - dot(half[i], inverse[i]).astype(BF16) for i in all_blocks}
    joined = {}
    for h, b in all_blocks:
        wide = kn[h, b].astype(F32)
        right = jnp.concatenate(
            [
                (column_at(columns[h], 1, b) * v_ref[heads[h], rows_of(b), :].astype(F32)).astype(BF16),
                (column_at(columns[h], 3, b) * wide).astype(BF16),
            ],
            axis=1,
        )
        solved = dot(inverse[h, b], right).astype(BF16)
        solved_ref[heads[h], b] = solved
        ended = (column_at(columns[h], 4, b) * wide).astype(BF16)
        joined[h, b] = dot_columns(ended, solved)
        keys_ref[heads[h], rows_of(b), :] = kn[h, b]
    nodes = [[joined[h, b] for b in every] for h in range(len(heads))]
    first = 0
    for level in range(3):
        many = len(nodes[0]) // 2
        for h, head in enumerate(heads):
            merged, kept = [], []
            for pair in range(many):
                early, late = nodes[h][2 * pair], nodes[h][2 * pair + 1]
                keep_e, keep_o = keep[h][2 * pair], keep[h][2 * pair + 1]
                node = early.astype(BF16)
                node_ref[head, first + pair] = node
                keeps_ref[head, first + pair : first + pair + 1, :] = keep_e
                moved = dot(late[:, WIDTH:].astype(BF16), node)
                carried = jnp.concatenate([late[:, :WIDTH], keep_e * late[:, WIDTH:]], axis=1)
                merged.append(jnp.concatenate([keep_o, keep_o], axis=1) * early + carried - moved)
                kept.append(keep_e * keep_o)
            nodes[h], keep[h] = merged, kept
        first = first + many
    return [(nodes[h][0], keep[h][0]) for h in range(len(heads))]


def readout_terms(head, q_ref, weight_ref, keys_ref, fading_ref, solved_ref, node_ref, keeps_ref, column_ref, out_ref, weighted_ref):
    every = range(BLOCKS)
    ones = jnp.ones((BLOCK, BLOCK), BF16)
    columns = column_ref[head]
    wcols = weight_ref[head].T

    def weight(level, block):
        at = block * 16 + level
        return wcols[:, at : at + 1]

    qn = unit_rows(q_ref[head], ones)
    scores = [
        (fading_ref[head, b] * dot_rows(qn[rows_of(b)], keys_ref[head, rows_of(b), :])).astype(BF16) for b in every
    ]
    both = [dot(scores[b], solved_ref[head, b]) for b in every]
    out = [weight(0, b) * both[b][:, :WIDTH] for b in every]
    reads = [column_at(columns, 2, b) * qn[rows_of(b)].astype(F32) - both[b][:, WIDTH:] for b in every]
    first = 0
    for level in range(1, 4):
        span = 1 << (level - 1)
        many = BLOCKS // (2 * span)
        for pair in range(many):
            later = [b for b in every if b // span == 2 * pair + 1]
            stack = jnp.concatenate([reads[b] for b in later], axis=0).astype(BF16)
            moved = dot(stack, node_ref[head, first + pair])
            keep = keeps_ref[head, first + pair : first + pair + 1, :]
            for at, b in enumerate(later):
                part = moved[at * BLOCK : (at + 1) * BLOCK]
                out[b] = out[b] + weight(level, b) * part[:, :WIDTH]
                reads[b] = keep * reads[b] - part[:, WIDTH:]
        first = first + many
    for b in every:
        out_ref[head, rows_of(b), :] = out[b]
        weighted_ref[head, rows_of(b), :] = jnp.concatenate(
            [(weight(level, b) * reads[b]).astype(BF16) for level in range(4, 10)], axis=1
        )

MESH = pl.DeviceIdType.MESH
GROUPS = 2


def joined(late, early):
    keep_l, body_l, first_l, last_l = late
    keep_e, body_e, first_e, last_e = early
    same = (first_l == last_e).astype(F32)
    moved = dot(body_l[:, WIDTH:].astype(BF16), body_e.astype(BF16))
    carried = jnp.concatenate([body_l[:, :WIDTH], (same * keep_e)[:, WIDTH:] * body_l[:, WIDTH:]], axis=1)
    keep_l = same * keep_l
    return keep_l * keep_e, keep_l * body_e + carried - same * moved, first_e, last_l


def without_state(summary):
    keep, body, first, last = summary
    return keep, jnp.concatenate([jnp.zeros((BLOCK, WIDTH), F32), body[:, WIDTH:]], axis=1), first, last


def chosen(use, one, other):
    use = use.astype(F32)
    return tuple(use * a + (1.0 - use) * b for a, b in zip(one, other))


def tail_rows(summary):
    keep, _, first_id, last_id = summary
    parts = [part.astype(F32) for part in split3(keep)] + [first_id, last_id]
    return jnp.concatenate(parts + [jnp.zeros((11, 2 * WIDTH), F32)], axis=0).astype(BF16)


def layer_kernel(
    q_hbm,
    k_hbm,
    v_hbm,
    gate_hbm,
    w_hbm,
    decay_hbm,
    strength_hbm,
    weights_hbm,
    seg_hbm,
    gain_hbm,
    result_ref,
    q_ref,
    k_ref,
    v_ref,
    gate_ref,
    whole_ref,
    decay_ref,
    strength_ref,
    weights_ref,
    seg_ref,
    gain_ref,
    far_ref,
    pair_ref,
    spread_ref,
    weight_ref,
    keys_ref,
    fading_ref,
    solved_ref,
    node_ref,
    keeps_ref,
    column_ref,
    out_ref,
    weighted_ref,
    silu_ref,
    normed_ref,
    gathered_ref,
    sum_ref,
    core_sent_ref,
    core_came_ref,
    quad_ref,
    half_sent_ref,
    half_ref,
    ring_sent_ref,
    ring_ref,
    total_ref,
    keep_ref,
    prefix_ref,
    prekeep_ref,
    chip_ref,
    segs_ref,
    load_sem,
    small_sem,
    own_sem,
    core_sem,
    quad_sem,
    half_sent_sem,
    half_came_sem,
    ring_sem,
    chip_sem,
    out_sem,
    in_sem,
    w_sent_sem,
    w_came_sem,
):
    ctx = lax.axis_index("ctx")
    x = lax.axis_index("head")
    core = lax.rem(ctx, 2)
    z = lax.rem(ctx // 2, 8)
    y = ctx // 16
    zq = lax.rem(z, 4)
    zh = z // 4
    right, left = lax.rem(x + 1, 4), lax.rem(x + 3, 4)
    other_core = ctx + 1 - 2 * core

    def at(y_to, z_to):
        return (y_to * 8 + z_to) * 2 + core

    def quad_to(d):
        return at(y, zh * 4 + lax.rem(zq + d, 4))

    def half_to(n):
        return at(y, 7 - z + n * (2 * (zq // 3) - 1))

    def ring_to(d):
        return at(lax.rem(y + d, 4), z)

    def remote(source, target, sent, came, axis, to):
        return pltpu.make_async_remote_copy(
            src_ref=source,
            dst_ref=target,
            send_sem=sent,
            recv_sem=came,
            device_id={axis: to},
            device_id_type=MESH,
        )

    partners = [("ctx", other_core)]
    partners += [("ctx", at(y, lax.rem(z + d, 8))) for d in range(1, 8)]
    partners += [("ctx", ring_to(d)) for d in (1, 2, 3)]
    partners += [("head", lax.rem(x + d, 4)) for d in (1, 2, 3)]

    sources = ((k_hbm, k_ref), (v_hbm, v_ref), (q_hbm, q_ref), (gate_hbm, gate_ref))

    def load(which, head):
        source, target = sources[which]
        columns = slice(head * WIDTH, (head + 1) * WIDTH)
        return pltpu.make_async_copy(source.at[:, columns], target.at[head], load_sem.at[which, head])

    smalls = [
        pltpu.make_async_copy(source, target, small_sem.at[n])
        for n, (source, target) in enumerate(
            (
                (seg_hbm, seg_ref),
                (decay_hbm, decay_ref),
                (strength_hbm, strength_ref),
                (weights_hbm, weights_ref),
                (gain_hbm, gain_ref),
            )
        )
    ]
    own_w = pltpu.make_async_copy(w_hbm, whole_ref.at[x], own_sem)
    quarters = [pl.ds(pl.multiple_of(core * 256 + part * 128, 128), 128) for part in range(2)]
    half_rows = pl.ds(pl.multiple_of(core * 256, 256), 256)

    def w_copy(n, source, shard, rows, axis, to):
        return remote(source, whole_ref.at[shard, rows], w_sent_sem.at[n], w_came_sem.at[n], axis, to)

    w_first = [
        w_copy(0, w_hbm.at[quarters[0]], x, quarters[0], "head", right),
        w_copy(1, w_hbm.at[quarters[1]], x, quarters[1], "head", left),
        w_copy(2, w_hbm.at[quarters[1]], x, quarters[1], "head", right),
        w_copy(3, w_hbm.at[quarters[0]], x, quarters[0], "head", left),
    ]
    w_relay = [
        w_copy(4, whole_ref.at[left, quarters[0]], left, quarters[0], "head", right),
        w_copy(5, whole_ref.at[right, quarters[1]], right, quarters[1], "head", left),
    ]
    w_core = [
        w_copy(6 + n, whole_ref.at[shard, half_rows], shard, half_rows, "ctx", other_core)
        for n, shard in enumerate((left, right, lax.rem(x + 2, 4)))
    ]

    def core_copy(head):
        return remote(
            core_sent_ref.at[head], core_came_ref.at[head], core_sem.at[0, head], core_sem.at[1, head], "ctx", other_core
        )

    def quad_copy(group, d):
        mine = quad_ref.at[group, zq]
        return remote(mine, mine, quad_sem.at[0, group, d - 1], quad_sem.at[1, group, d - 1], "ctx", quad_to(d))

    def half_copy(group, n):
        return remote(
            half_sent_ref.at[group],
            half_ref.at[group],
            half_sent_sem.at[group, n],
            half_came_sem.at[group],
            "ctx",
            half_to(n),
        )

    def ring_copy(group, d):
        return remote(
            ring_sent_ref.at[group],
            ring_ref.at[group, y],
            ring_sem.at[0, group, d - 1],
            ring_sem.at[1, group, d - 1],
            "ctx",
            ring_to(d),
        )

    def chip_copy(group, part, head):
        mine = chip_ref.at[head, pl.ds(2 * part, 2 + part)]
        return remote(mine, mine, chip_sem.at[0, group, part], chip_sem.at[1, group, part], "ctx", other_core)

    def spread_copy(head, d):
        to = lax.rem(x + d, 4)
        rows = pl.ds(pl.multiple_of(to * 256, 256), 256)
        columns = pl.ds(pl.multiple_of(x * 512 + head * WIDTH, WIDTH), WIDTH)
        return remote(
            normed_ref.at[head, rows],
            gathered_ref.at[:, columns],
            out_sem.at[head, d - 1],
            in_sem.at[head, d - 1],
            "head",
            to,
        )

    def own_head(group):
        return 2 * group + core

    def read(ref):
        tail = ref[BLOCK:, :].astype(F32)
        return tail[0:1] + tail[1:2] + tail[2:3], ref[:BLOCK, :].astype(F32), tail[3:4], tail[4:5]

    def write(ref, summary):
        ref[:BLOCK, :] = summary[1].astype(BF16)
        ref[BLOCK:, :] = tail_rows(summary)

    def own_ids():
        first_id = jnp.broadcast_to(segs_ref[0:1, :1], (1, 2 * WIDTH))
        last_id = jnp.broadcast_to(segs_ref[BLOCKS - 1 :, WIDTH - 1 :], (1, 2 * WIDTH))
        return first_id, last_id

    def summary_step(group, between, ready):
        heads = [2 * group, 2 * group + 1]
        for head in heads:
            for which in range(2):
                load(which, head).wait()
        found = summary_terms(
            heads,
            k_ref,
            v_ref,
            spread_ref,
            segs_ref[...],
            far_ref,
            pair_ref,
            keys_ref,
            fading_ref,
            solved_ref,
            node_ref,
            keeps_ref,
            column_ref,
            between,
        )
        ready()
        for head, (body, keep) in zip(heads, found):
            keep = jnp.concatenate([keep, keep], axis=1)
            total_ref[head] = body
            keep_ref[head] = jnp.broadcast_to(keep, (8, 2 * WIDTH))
            write(core_sent_ref.at[head], (keep, body) + own_ids())
            core_copy(head).start()

    def chip_step(group):
        for head in (2 * group, 2 * group + 1):
            core_copy(head).wait_recv()
        head = own_head(group)
        mine = (keep_ref[head, 0:1, :], total_ref[head]) + own_ids()
        other = read(core_came_ref.at[head])
        to = quad_ref.at[group, zq]

        @pl.when(core == 1)
        def _():
            write(to, joined(mine, other))

        @pl.when(core == 0)
        def _():
            write(to, joined(other, mine))

        for d in (1, 3, 2):
            quad_copy(group, d).start()

    def store_prefix(group, prefix):
        prefix_ref[group] = prefix[1]
        prekeep_ref[group, 0:1, :] = prefix[0]
        prekeep_ref[group, 1:2, :] = prefix[2]

    def load_prefix(group):
        first_id = prekeep_ref[group, 1:2, :]
        return prekeep_ref[group, 0:1, :], prefix_ref[group], first_id, first_id

    def quad_step(group):
        for d in (1, 2, 3):
            quad_copy(group, d).wait_recv()
        parts = [read(quad_ref.at[group, n]) for n in range(4)]
        first, second = joined(parts[1], parts[0]), joined(parts[3], parts[2])
        write(half_sent_ref.at[group], joined(second, first))

        @pl.when((zq == 0) | (zq == 3))
        def _():
            for n in (1, 0):
                half_copy(group, n).start()

        head = own_head(group)
        odd = lax.rem(zq, 2)
        upper = zq // 2
        own_first = read(quad_ref.at[group, zq])[2]
        none = jnp.ones((1, 2 * WIDTH), F32), jnp.zeros((BLOCK, 2 * WIDTH), F32), own_first, own_first
        keep, body, first_id, last_id = read(quad_ref.at[group, odd * (zq - odd)])
        same = (own_first == last_id).astype(F32)
        near = chosen(odd, (same * keep, same * body, first_id, first_id), none)
        chip_ref[head, 0] = near[1][:, :WIDTH].astype(BF16)
        near = without_state(near)
        far = chosen(upper, joined(near, first), near)
        chip_ref[head, 1] = far[1][:, :WIDTH].astype(BF16)
        chip_copy(group, 0, head).start()
        store_prefix(group, without_state(far))

    def ring_step(group):
        half_copy(group, 0).wait_recv()
        mine, other = read(half_sent_ref.at[group]), read(half_ref.at[group])

        @pl.when(zh == 1)
        def _():
            write(ring_sent_ref.at[group], joined(mine, other))

        @pl.when(zh == 0)
        def _():
            write(ring_sent_ref.at[group], joined(other, mine))

        for d in (2, 1, 3):

            @pl.when(y + d < 4)
            def _():
                ring_copy(group, d).start()

        prefix = load_prefix(group)
        over = chosen(zh, joined(prefix, other), prefix)
        chip_ref[own_head(group), 2] = over[1][:, :WIDTH].astype(BF16)
        store_prefix(group, without_state(over))

    def last_step(group):
        for d in range(1, 4):

            @pl.when(y >= d)
            def _():
                ring_copy(group, d).wait_recv()

        head = own_head(group)
        odd, upper = lax.rem(y, 2), y // 2

        def slot(use, n):
            return read(ring_ref.at[group, use * n + (1 - use) * 3])

        prefix = load_prefix(group)
        oldest = joined(slot(upper, 1), slot(upper, 0))
        over = chosen(odd, joined(prefix, slot(odd, y - 1)), prefix)
        chip_ref[head, 3] = over[1][:, :WIDTH].astype(BF16)
        over = joined(without_state(over), oldest)
        chip_ref[head, 4] = (upper.astype(F32) * over[1][:, :WIDTH]).astype(BF16)
        chip_copy(group, 1, head).start()

    def readout_step(head):
        load(2, head).wait()
        readout_terms(
            head,
            q_ref,
            weight_ref,
            keys_ref,
            fading_ref,
            solved_ref,
            node_ref,
            keeps_ref,
            column_ref,
            out_ref,
            weighted_ref,
        )

    def gate_step(head):
        load(3, head).wait()
        gate = gate_ref[head].astype(F32)
        silu_ref[head] = gate / (1.0 + jnp.exp(-gate)) * gain_ref[...]

    def own_states(head, first, last):
        keep, body, _, last_id = read(core_came_ref.at[head])
        joins = core.astype(F32) * (own_ids()[0] == last_id).astype(F32)[:, :WIDTH]
        keep = joins * keep[:, :WIDTH] + (1.0 - core.astype(F32))
        erase = (joins * body[:, WIDTH:]).astype(BF16)
        states = [chip_ref[head, n] for n in range(first, last)]
        moved = dot(erase, jnp.concatenate(states, axis=1))
        carried = [
            (keep * state.astype(F32) - moved[:, n * WIDTH : (n + 1) * WIDTH]).astype(BF16)
            for n, state in enumerate(states)
        ]
        if first == 0:
            carried = [(joins * body[:, :WIDTH]).astype(BF16)] + carried
        return jnp.concatenate(carried, axis=0)

    def await_states(group, part, head):
        @pl.when(head != own_head(group))
        def _():
            chip_copy(group, part, head).wait_recv()

    def near_step(group, head):
        await_states(group, 0, head)
        states = own_states(head, 0, 2)
        out_ref[head] += dot(weighted_ref[head, :, : 3 * WIDTH], states)

    def finish_step(group, head):
        await_states(group, 1, head)
        states = own_states(head, 2, 5)
        ones = jnp.ones((WIDTH, WIDTH), BF16)
        total = out_ref[head] + dot(weighted_ref[head, :, 3 * WIDTH :], states)
        mean = dot((total * total).astype(BF16), ones) * (1.0 / WIDTH)
        normed_ref[head] = (total * lax.rsqrt(mean + EPSILON) * silu_ref[head]).astype(BF16)
        for d in (2, 1, 3):
            spread_copy(head, d).start()
        rows = pl.ds(pl.multiple_of(x * 256, 256), 256)
        columns = pl.ds(pl.multiple_of(x * 512 + head * WIDTH, WIDTH), WIDTH)
        gathered_ref[:, columns] = normed_ref[head, rows, :]

    def finish_group(group):
        for turn in range(2):
            @pl.when(core == 0)
            def _():
                finish_step(group, 2 * group + turn)

            @pl.when(core == 1)
            def _():
                finish_step(group, 2 * group + 1 - turn)

    def project_group(group):
        for head in (2 * group, 2 * group + 1):
            for d in (1, 2, 3):
                spread_copy(head, d).wait_recv()

        def tile(n, carry):
            columns = pl.ds(pl.multiple_of(n * 256, 256), 256)
            rows = slice(group * 256, (group + 1) * 256)
            total = sum(
                dot(gathered_ref[:, shard * 512 + group * 256 : shard * 512 + (group + 1) * 256], whole_ref[shard, rows, columns])
                for shard in range(4)
            )
            if group == 0:
                sum_ref[:, columns] = total
            else:
                result_ref[:, columns] = (total + sum_ref[:, columns]).astype(BF16)
            return carry

        lax.fori_loop(0, 8, tile, 0)

    for group in range(GROUPS):
        ring_ref[group, 3] = jnp.zeros((MESSAGE_ROWS, 2 * WIDTH), BF16)
    barrier = pltpu.get_barrier_semaphore()
    for axis, to in partners:
        pl.semaphore_signal(barrier, inc=1, device_id={axis: to}, device_id_type=MESH)
    for copy in smalls[:3]:
        copy.start()
    for head in range(HEADS_HERE):
        for which in range(2):
            load(which, head).start()
    for copy in smalls[3:]:
        copy.start()
    for head in range(HEADS_HERE):
        for which in (2, 3):
            load(which, head).start()
    own_w.start()
    smalls[0].wait()
    segs_ref[...] = seg_ref[...].astype(F32)
    prepare_masks(seg_ref, far_ref, pair_ref)
    for source, n in ((decay_ref, 0), (strength_ref, 1)):
        smalls[1 + n].wait()
        for each in range(HEADS_HERE):
            for b in range(BLOCKS):
                spread_ref[n, each, b : b + 1, :] = source[each : each + 1, rows_of(b)]

    def all_entered():
        pl.semaphore_wait(barrier, len(partners))

    summary_step(0, lambda: None, all_entered)
    for copy in w_first:
        copy.start()
    summary_step(1, lambda: chip_step(0), lambda: None)
    for copy in smalls[3:]:
        copy.wait()
    gate_step(0)
    chip_step(1)
    quad_step(0)
    for level in range(10):
        for each in range(HEADS_HERE):
            for b in range(BLOCKS):
                row = b * 16 + level
                weight_ref[each, row : row + 1, :] = weights_ref[level, each : each + 1, rows_of(b)]
    for head in range(HEADS_HERE):
        readout_step(head)
    gate_step(1)
    quad_step(1)
    for n in range(2):
        w_first[n].wait_recv()
        w_relay[n].start()
    ring_step(0)
    near_step(0, 0)
    near_step(0, 1)
    gate_step(2)
    gate_step(3)
    for n in range(2):
        w_first[2 + n].wait_recv()
        w_core[n].start()
    near_step(1, 2)
    near_step(1, 3)
    ring_step(1)
    last_step(0)
    finish_group(0)
    for copy in w_relay:
        copy.wait_recv()
    w_core[2].start()
    last_step(1)
    finish_group(1)
    own_w.wait()
    for copy in w_core:
        copy.wait_recv()
    project_group(0)
    project_group(1)
    for copy in w_first + w_relay + w_core:
        copy.wait_send()
    for head in range(HEADS_HERE):
        core_copy(head).wait_send()
        for d in (1, 2, 3):
            spread_copy(head, d).wait_send()
    for group in range(GROUPS):
        for d in (1, 2, 3):
            quad_copy(group, d).wait_send()
        for part in range(2):
            chip_copy(group, part, own_head(group)).wait_send()
        for d in range(1, 4):

            @pl.when(y + d < 4)
            def _():
                ring_copy(group, d).wait_send()

        @pl.when((zq == 0) | (zq == 3))
        def _():
            for n in range(2):
                half_copy(group, n).wait_send()


def shards(queries, keys, values, log_decay, write_strength, level_weights, segment, out_gate, norm_gain, w_out):
    far = pl.BlockSpec(memory_space=pl.ANY)
    near = pl.BlockSpec(memory_space=pltpu.VMEM)
    tall = (HEADS_HERE, TOKENS_HERE, WIDTH)
    wide = (MESSAGE_ROWS, 2 * WIDTH)
    return pl.pallas_call(
        layer_kernel,
        out_shape=jax.ShapeDtypeStruct((256, 2048), BF16),
        in_specs=[far] * 10,
        out_specs=near,
        scratch_shapes=[
            pltpu.VMEM(tall, BF16),
            pltpu.VMEM(tall, BF16),
            pltpu.VMEM(tall, BF16),
            pltpu.VMEM(tall, BF16),
            pltpu.VMEM((4, 512, 2048), BF16),
            pltpu.VMEM((HEADS_HERE, TOKENS_HERE), F32),
            pltpu.VMEM((HEADS_HERE, TOKENS_HERE), F32),
            pltpu.VMEM((LEVELS, HEADS_HERE, TOKENS_HERE), F32),
            pltpu.VMEM((BLOCKS, BLOCK), jnp.int32),
            pltpu.VMEM((1, WIDTH), F32),
            pltpu.VMEM((BLOCKS, BLOCK, BLOCK), F32),
            pltpu.VMEM((7, BLOCK, BLOCK), BF16),
            pltpu.VMEM((2, HEADS_HERE, BLOCKS, BLOCK), F32),
            pltpu.VMEM((HEADS_HERE, BLOCK, BLOCK), F32),
            pltpu.VMEM(tall, BF16),
            pltpu.VMEM((HEADS_HERE, BLOCKS, BLOCK, BLOCK), F32),
            pltpu.VMEM((HEADS_HERE, BLOCKS, BLOCK, 2 * WIDTH), BF16),
            pltpu.VMEM((HEADS_HERE, 7, BLOCK, 2 * WIDTH), BF16),
            pltpu.VMEM((HEADS_HERE, 8, WIDTH), F32),
            pltpu.VMEM((HEADS_HERE, BLOCK, BLOCK), F32),
            pltpu.VMEM(tall, F32),
            pltpu.VMEM((HEADS_HERE, TOKENS_HERE, 6 * WIDTH), BF16),
            pltpu.VMEM(tall, F32),
            pltpu.VMEM(tall, BF16),
            pltpu.VMEM((256, 2048), BF16),
            pltpu.VMEM((256, 2048), F32),
            pltpu.VMEM((HEADS_HERE,) + wide, BF16),
            pltpu.VMEM((HEADS_HERE,) + wide, BF16),
            pltpu.VMEM((GROUPS, 4) + wide, BF16),
            pltpu.VMEM((GROUPS,) + wide, BF16),
            pltpu.VMEM((GROUPS,) + wide, BF16),
            pltpu.VMEM((GROUPS,) + wide, BF16),
            pltpu.VMEM((GROUPS, 4) + wide, BF16),
            pltpu.VMEM((HEADS_HERE, BLOCK, 2 * WIDTH), F32),
            pltpu.VMEM((HEADS_HERE, 8, 2 * WIDTH), F32),
            pltpu.VMEM((GROUPS, BLOCK, 2 * WIDTH), F32),
            pltpu.VMEM((GROUPS, 8, 2 * WIDTH), F32),
            pltpu.VMEM((HEADS_HERE, 5, BLOCK, WIDTH), BF16),
            pltpu.VMEM((BLOCKS, BLOCK), F32),
            pltpu.SemaphoreType.DMA((4, HEADS_HERE)),
            pltpu.SemaphoreType.DMA((5,)),
            pltpu.SemaphoreType.DMA,
            pltpu.SemaphoreType.DMA((2, HEADS_HERE)),
            pltpu.SemaphoreType.DMA((2, GROUPS, 3)),
            pltpu.SemaphoreType.DMA((GROUPS, 2)),
            pltpu.SemaphoreType.DMA((GROUPS,)),
            pltpu.SemaphoreType.DMA((2, GROUPS, 3)),
            pltpu.SemaphoreType.DMA((2, GROUPS, 2)),
            pltpu.SemaphoreType.DMA((HEADS_HERE, 3)),
            pltpu.SemaphoreType.DMA((HEADS_HERE, 3)),
            pltpu.SemaphoreType.DMA((9,)),
            pltpu.SemaphoreType.DMA((9,)),
        ],
        compiler_params=pltpu.CompilerParams(
            collective_id=0, has_side_effects=True, vmem_limit_bytes=50 << 20
        ),
        cost_estimate=pl.CostEstimate(flops=24_000_000_000, bytes_accessed=16_000_000, transcendentals=0),
    )(
        queries,
        keys,
        values,
        out_gate,
        w_out,
        log_decay,
        write_strength,
        level_weights.transpose(1, 0, 2),
        segment.reshape(BLOCKS, BLOCK),
        norm_gain.reshape(1, WIDTH),
    )


def solution(mesh):
    placed = (
        P("ctx", "head"),
        P("ctx", "head"),
        P("ctx", "head"),
        P("head", "ctx"),
        P("head", "ctx"),
        P("head", None, "ctx"),
        P("ctx"),
        P("ctx", "head"),
        P(),
        P("head", None),
    )
    return jax.shard_map(
        shards, mesh=mesh, in_specs=placed, out_specs=P(("ctx", "head"), None), check_vma=False
    )
```

```python
import jax
import jax.numpy as jnp
from jax import lax
from jax.experimental import pallas as pl
from jax.experimental.pallas import tpu as pltpu
from jax.sharding import PartitionSpec as P

BLOCK = 128
BLOCKS = 8
TOKENS_HERE = 1024
HEADS_HERE = 4
WIDTH = 128
LEVELS = 12
EPSILON = 1e-06
FAR = -1e4
MESSAGE_ROWS = 144

F32 = jnp.float32
BF16 = jnp.bfloat16


def dot(left, right):
    return jnp.dot(left, right, preferred_element_type=F32)


def dot_rows(left, right):
    return lax.dot_general(left, right, (((1,), (1,)), ((), ())), preferred_element_type=F32)


def dot_columns(left, right):
    return lax.dot_general(left, right, (((0,), (0,)), ((), ())), preferred_element_type=F32)


def split3(value):
    first = value.astype(BF16)
    rest = value - first.astype(F32)
    second = rest.astype(BF16)
    third = (rest - second.astype(F32)).astype(BF16)
    return first, second, third


def rows_of(block):
    return slice(block * BLOCK, (block + 1) * BLOCK)


def prepare_masks(seg_ref, far_ref, pair_ref):
    row = lax.broadcasted_iota(jnp.int32, (BLOCK, BLOCK), 0)
    col = lax.broadcasted_iota(jnp.int32, (BLOCK, BLOCK), 1)
    segs = seg_ref[...].astype(F32)
    padded = jnp.concatenate([segs, jnp.zeros((BLOCK - BLOCKS, BLOCK), F32)], axis=0)
    seg_cols = padded.T
    for block in range(BLOCKS):
        same = seg_cols[:, block : block + 1] == segs[block : block + 1, :]
        far_ref[block] = jnp.where(same & (row >= col), 0.0, FAR)
    for step in range(7):
        size = 1 << step
        chosen = (row // size == col // size + 1) & (row // size % 2 == 1)
        pair_ref[step] = jnp.where(chosen, 1.0, 0.0).astype(BF16)


def unit_rows(rows, ones):
    wide = rows.astype(F32)
    total = dot((wide * wide).astype(BF16), ones)
    return (wide * lax.rsqrt(total + EPSILON)).astype(BF16)


def columns_of(rows):
    return jnp.concatenate([rows, jnp.zeros((BLOCK - rows.shape[0], BLOCK), F32)], axis=0).T


def column_at(columns, kind, block):
    at = kind * BLOCKS + block
    return columns[:, at : at + 1]


def summary_terms(heads, k_ref, v_ref, spread_ref, segs, far_ref, pair_ref, keys_ref, fading_ref, solved_ref, node_ref, keeps_ref, column_ref, between):
    row = lax.broadcasted_iota(jnp.int32, (BLOCK, BLOCK), 0)
    col = lax.broadcasted_iota(jnp.int32, (BLOCK, BLOCK), 1)
    every = range(BLOCKS)
    all_blocks = [(h, b) for h in range(len(heads)) for b in every]
    ones = jnp.ones((BLOCK, BLOCK), BF16)
    upto = jnp.where(row <= col, 1.0, 0.0).astype(BF16)
    last_seg = jnp.broadcast_to(segs[:, BLOCK - 1 :], (BLOCKS, BLOCK))
    first_seg = jnp.broadcast_to(segs[:, :1], (BLOCKS, BLOCK))
    before = jnp.concatenate([first_seg[:1], last_seg[:-1]], axis=0)
    opens = (segs == before).astype(F32)
    closes = (segs == last_seg).astype(F32)
    through = (last_seg == before).astype(F32)
    summed, columns, keep = [], [], []
    for head in heads:
        strength = spread_ref[1, head]
        total = sum(dot(part, upto) for part in split3(spread_ref[0, head]))
        last_sum = jnp.broadcast_to(total[:, BLOCK - 1 :], (BLOCKS, BLOCK))
        opening = jnp.exp(total) * opens
        closing = jnp.exp(last_sum - total) * closes
        keeps = jnp.exp(last_sum) * through
        columns.append(
            columns_of(jnp.concatenate([total, strength, opening, strength * opening, closing], axis=0))
        )
        summed.append(total)
        keep.append([keeps[b : b + 1] for b in every])
        column_ref[head] = columns[-1]
    kn = {}
    for h, head in enumerate(heads):
        unit = unit_rows(k_ref[head], ones)
        for b in every:
            kn[h, b] = unit[rows_of(b)]
    grams = {i: dot_rows(kn[i], kn[i]) for i in all_blocks}
    lower = {}
    for h, b in all_blocks:
        fading = jnp.exp(column_at(columns[h], 0, b) - summed[h][b : b + 1, :] + far_ref[b])
        fading_ref[heads[h], b] = fading
        lower[h, b] = (column_at(columns[h], 1, b) * fading * grams[h, b]).astype(BF16)
    between()
    eye = jnp.where(row == col, 1.0, 0.0).astype(BF16)
    inverse = {i: eye - lower[i] * pair_ref[0] for i in all_blocks}
    for step in range(1, 7):
        mask = pair_ref[step]
        half = {i: dot(inverse[i], lower[i] * mask).astype(BF16) for i in all_blocks}
        inverse = {i: inverse[i] - dot(half[i], inverse[i]).astype(BF16) for i in all_blocks}
    joined = {}
    for h, b in all_blocks:
        wide = kn[h, b].astype(F32)
        right = jnp.concatenate(
            [
                (column_at(columns[h], 1, b) * v_ref[heads[h], rows_of(b), :].astype(F32)).astype(BF16),
                (column_at(columns[h], 3, b) * wide).astype(BF16),
            ],
            axis=1,
        )
        solved = dot(inverse[h, b], right).astype(BF16)
        solved_ref[heads[h], b] = solved
        ended = (column_at(columns[h], 4, b) * wide).astype(BF16)
        joined[h, b] = dot_columns(ended, solved)
        keys_ref[heads[h], rows_of(b), :] = kn[h, b]
    nodes = [[joined[h, b] for b in every] for h in range(len(heads))]
    first = 0
    for level in range(3):
        many = len(nodes[0]) // 2
        for h, head in enumerate(heads):
            merged, kept = [], []
            for pair in range(many):
                early, late = nodes[h][2 * pair], nodes[h][2 * pair + 1]
                keep_e, keep_o = keep[h][2 * pair], keep[h][2 * pair + 1]
                node = early.astype(BF16)
                node_ref[head, first + pair] = node
                keeps_ref[head, first + pair : first + pair + 1, :] = keep_e
                moved = dot(late[:, WIDTH:].astype(BF16), node)
                carried = jnp.concatenate([late[:, :WIDTH], keep_e * late[:, WIDTH:]], axis=1)
                merged.append(jnp.concatenate([keep_o, keep_o], axis=1) * early + carried - moved)
                kept.append(keep_e * keep_o)
            nodes[h], keep[h] = merged, kept
        first = first + many
    return [(nodes[h][0], keep[h][0]) for h in range(len(heads))]


def readout_terms(head, q_ref, weight_ref, keys_ref, fading_ref, solved_ref, node_ref, keeps_ref, column_ref, out_ref, weighted_ref):
    every = range(BLOCKS)
    ones = jnp.ones((BLOCK, BLOCK), BF16)
    columns = column_ref[head]
    wcols = weight_ref[head].T

    def weight(level, block):
        at = block * 16 + level
        return wcols[:, at : at + 1]

    qn = unit_rows(q_ref[head], ones)
    scores = [
        (fading_ref[head, b] * dot_rows(qn[rows_of(b)], keys_ref[head, rows_of(b), :])).astype(BF16) for b in every
    ]
    both = [dot(scores[b], solved_ref[head, b]) for b in every]
    out = [weight(0, b) * both[b][:, :WIDTH] for b in every]
    reads = [column_at(columns, 2, b) * qn[rows_of(b)].astype(F32) - both[b][:, WIDTH:] for b in every]
    first = 0
    for level in range(1, 4):
        span = 1 << (level - 1)
        many = BLOCKS // (2 * span)
        for pair in range(many):
            later = [b for b in every if b // span == 2 * pair + 1]
            stack = jnp.concatenate([reads[b] for b in later], axis=0).astype(BF16)
            moved = dot(stack, node_ref[head, first + pair])
            keep = keeps_ref[head, first + pair : first + pair + 1, :]
            for at, b in enumerate(later):
                part = moved[at * BLOCK : (at + 1) * BLOCK]
                out[b] = out[b] + weight(level, b) * part[:, :WIDTH]
                reads[b] = keep * reads[b] - part[:, WIDTH:]
        first = first + many
    for b in every:
        out_ref[head, rows_of(b), :] = out[b]
        weighted_ref[head, rows_of(b), :] = jnp.concatenate(
            [(weight(level, b) * reads[b]).astype(BF16) for level in range(4, 10)], axis=1
        )

MESH = pl.DeviceIdType.MESH
GROUPS = 2


def joined(late, early):
    keep_l, body_l, first_l, last_l = late
    keep_e, body_e, first_e, last_e = early
    same = (first_l == last_e).astype(F32)
    moved = dot(body_l[:, WIDTH:].astype(BF16), body_e.astype(BF16))
    carried = jnp.concatenate([body_l[:, :WIDTH], (same * keep_e)[:, WIDTH:] * body_l[:, WIDTH:]], axis=1)
    keep_l = same * keep_l
    return keep_l * keep_e, keep_l * body_e + carried - same * moved, first_e, last_l


def without_state(summary):
    keep, body, first, last = summary
    return keep, jnp.concatenate([jnp.zeros((BLOCK, WIDTH), F32), body[:, WIDTH:]], axis=1), first, last


def chosen(use, one, other):
    use = use.astype(F32)
    return tuple(use * a + (1.0 - use) * b for a, b in zip(one, other))


def tail_rows(summary):
    keep, _, first_id, last_id = summary
    parts = [part.astype(F32) for part in split3(keep)] + [first_id, last_id]
    return jnp.concatenate(parts + [jnp.zeros((11, 2 * WIDTH), F32)], axis=0).astype(BF16)


def layer_kernel(
    q_hbm,
    k_hbm,
    v_hbm,
    gate_hbm,
    w_hbm,
    decay_hbm,
    strength_hbm,
    weights_hbm,
    seg_hbm,
    gain_hbm,
    result_ref,
    q_ref,
    k_ref,
    v_ref,
    gate_ref,
    whole_ref,
    decay_ref,
    strength_ref,
    weights_ref,
    seg_ref,
    gain_ref,
    far_ref,
    pair_ref,
    spread_ref,
    weight_ref,
    keys_ref,
    fading_ref,
    solved_ref,
    node_ref,
    keeps_ref,
    column_ref,
    out_ref,
    weighted_ref,
    silu_ref,
    normed_ref,
    gathered_ref,
    sum_ref,
    core_sent_ref,
    core_came_ref,
    quad_ref,
    half_sent_ref,
    half_ref,
    ring_sent_ref,
    ring_ref,
    total_ref,
    keep_ref,
    prefix_ref,
    prekeep_ref,
    chip_ref,
    segs_ref,
    load_sem,
    small_sem,
    own_sem,
    core_sem,
    quad_sem,
    half_sent_sem,
    half_came_sem,
    ring_sem,
    chip_sem,
    out_sem,
    in_sem,
    w_sent_sem,
    w_came_sem,
):
    ctx = lax.axis_index("ctx")
    x = lax.axis_index("head")
    core = lax.rem(ctx, 2)
    z = lax.rem(ctx // 2, 8)
    y = ctx // 16
    zq = lax.rem(z, 4)
    zh = z // 4
    right, left = lax.rem(x + 1, 4), lax.rem(x + 3, 4)
    other_core = ctx + 1 - 2 * core

    def at(y_to, z_to):
        return (y_to * 8 + z_to) * 2 + core

    def quad_to(d):
        return at(y, zh * 4 + lax.rem(zq + d, 4))

    def half_to(n):
        return at(y, 7 - z + n * (2 * (zq // 3) - 1))

    def ring_to(d):
        return at(lax.rem(y + d, 4), z)

    def remote(source, target, sent, came, axis, to):
        return pltpu.make_async_remote_copy(
            src_ref=source,
            dst_ref=target,
            send_sem=sent,
            recv_sem=came,
            device_id={axis: to},
            device_id_type=MESH,
        )

    partners = [("ctx", other_core)]
    partners += [("ctx", at(y, lax.rem(z + d, 8))) for d in range(1, 8)]
    partners += [("ctx", ring_to(d)) for d in (1, 2, 3)]
    partners += [("head", lax.rem(x + d, 4)) for d in (1, 2, 3)]

    sources = ((k_hbm, k_ref), (v_hbm, v_ref), (q_hbm, q_ref), (gate_hbm, gate_ref))

    def load(which, head):
        source, target = sources[which]
        columns = slice(head * WIDTH, (head + 1) * WIDTH)
        return pltpu.make_async_copy(source.at[:, columns], target.at[head], load_sem.at[which, head])

    smalls = [
        pltpu.make_async_copy(source, target, small_sem.at[n])
        for n, (source, target) in enumerate(
            (
                (seg_hbm, seg_ref),
                (decay_hbm, decay_ref),
                (strength_hbm, strength_ref),
                (weights_hbm, weights_ref),
                (gain_hbm, gain_ref),
            )
        )
    ]
    own_w = pltpu.make_async_copy(w_hbm, whole_ref.at[x], own_sem)
    quarters = [pl.ds(pl.multiple_of(core * 256 + part * 128, 128), 128) for part in range(2)]
    half_rows = pl.ds(pl.multiple_of(core * 256, 256), 256)

    def w_copy(n, source, shard, rows, axis, to):
        return remote(source, whole_ref.at[shard, rows], w_sent_sem.at[n], w_came_sem.at[n], axis, to)

    w_first = [
        w_copy(0, w_hbm.at[quarters[0]], x, quarters[0], "head", right),
        w_copy(1, w_hbm.at[quarters[1]], x, quarters[1], "head", left),
        w_copy(2, w_hbm.at[quarters[1]], x, quarters[1], "head", right),
        w_copy(3, w_hbm.at[quarters[0]], x, quarters[0], "head", left),
    ]
    w_relay = [
        w_copy(4, whole_ref.at[left, quarters[0]], left, quarters[0], "head", right),
        w_copy(5, whole_ref.at[right, quarters[1]], right, quarters[1], "head", left),
    ]
    w_core = [
        w_copy(6 + n, whole_ref.at[shard, half_rows], shard, half_rows, "ctx", other_core)
        for n, shard in enumerate((left, right, lax.rem(x + 2, 4)))
    ]

    def core_copy(head):
        return remote(
            core_sent_ref.at[head], core_came_ref.at[head], core_sem.at[0, head], core_sem.at[1, head], "ctx", other_core
        )

    def quad_copy(group, d):
        mine = quad_ref.at[group, zq]
        return remote(mine, mine, quad_sem.at[0, group, d - 1], quad_sem.at[1, group, d - 1], "ctx", quad_to(d))

    def half_copy(group, n):
        return remote(
            half_sent_ref.at[group],
            half_ref.at[group],
            half_sent_sem.at[group, n],
            half_came_sem.at[group],
            "ctx",
            half_to(n),
        )

    def ring_copy(group, d):
        return remote(
            ring_sent_ref.at[group],
            ring_ref.at[group, y],
            ring_sem.at[0, group, d - 1],
            ring_sem.at[1, group, d - 1],
            "ctx",
            ring_to(d),
        )

    def chip_copy(group, part, head):
        mine = chip_ref.at[head, pl.ds(2 * part, 2 + part)]
        return remote(mine, mine, chip_sem.at[0, group, part], chip_sem.at[1, group, part], "ctx", other_core)

    def spread_copy(head, d):
        to = lax.rem(x + d, 4)
        rows = pl.ds(pl.multiple_of(to * 256, 256), 256)
        columns = pl.ds(pl.multiple_of(x * 512 + head * WIDTH, WIDTH), WIDTH)
        return remote(
            normed_ref.at[head, rows],
            gathered_ref.at[:, columns],
            out_sem.at[head, d - 1],
            in_sem.at[head, d - 1],
            "head",
            to,
        )

    def own_head(group):
        return 2 * group + core

    def read(ref):
        tail = ref[BLOCK:, :].astype(F32)
        return tail[0:1] + tail[1:2] + tail[2:3], ref[:BLOCK, :].astype(F32), tail[3:4], tail[4:5]

    def write(ref, summary):
        ref[:BLOCK, :] = summary[1].astype(BF16)
        ref[BLOCK:, :] = tail_rows(summary)

    def own_ids():
        first_id = jnp.broadcast_to(segs_ref[0:1, :1], (1, 2 * WIDTH))
        last_id = jnp.broadcast_to(segs_ref[BLOCKS - 1 :, WIDTH - 1 :], (1, 2 * WIDTH))
        return first_id, last_id

    def summary_step(group, between, ready):
        heads = [2 * group, 2 * group + 1]
        for head in heads:
            for which in range(2):
                load(which, head).wait()
        found = summary_terms(
            heads,
            k_ref,
            v_ref,
            spread_ref,
            segs_ref[...],
            far_ref,
            pair_ref,
            keys_ref,
            fading_ref,
            solved_ref,
            node_ref,
            keeps_ref,
            column_ref,
            between,
        )
        ready()
        for head, (body, keep) in zip(heads, found):
            keep = jnp.concatenate([keep, keep], axis=1)
            total_ref[head] = body
            keep_ref[head] = jnp.broadcast_to(keep, (8, 2 * WIDTH))
            write(core_sent_ref.at[head], (keep, body) + own_ids())
            core_copy(head).start()

    def chip_step(group):
        for head in (2 * group, 2 * group + 1):
            core_copy(head).wait_recv()
        head = own_head(group)
        mine = (keep_ref[head, 0:1, :], total_ref[head]) + own_ids()
        other = read(core_came_ref.at[head])
        to = quad_ref.at[group, zq]

        @pl.when(core == 1)
        def _():
            write(to, joined(mine, other))

        @pl.when(core == 0)
        def _():
            write(to, joined(other, mine))

        for d in (1, 3, 2):
            quad_copy(group, d).start()

    def store_prefix(group, prefix):
        prefix_ref[group] = prefix[1]
        prekeep_ref[group, 0:1, :] = prefix[0]
        prekeep_ref[group, 1:2, :] = prefix[2]

    def load_prefix(group):
        first_id = prekeep_ref[group, 1:2, :]
        return prekeep_ref[group, 0:1, :], prefix_ref[group], first_id, first_id

    def quad_step(group):
        for d in (1, 2, 3):
            quad_copy(group, d).wait_recv()
        parts = [read(quad_ref.at[group, n]) for n in range(4)]
        first, second = joined(parts[1], parts[0]), joined(parts[3], parts[2])
        write(half_sent_ref.at[group], joined(second, first))

        @pl.when((zq == 0) | (zq == 3))
        def _():
            for n in (1, 0):
                half_copy(group, n).start()

        head = own_head(group)
        odd = lax.rem(zq, 2)
        upper = zq // 2
        own_first = read(quad_ref.at[group, zq])[2]
        none = jnp.ones((1, 2 * WIDTH), F32), jnp.zeros((BLOCK, 2 * WIDTH), F32), own_first, own_first
        keep, body, first_id, last_id = read(quad_ref.at[group, odd * (zq - odd)])
        same = (own_first == last_id).astype(F32)
        near = chosen(odd, (same * keep, same * body, first_id, first_id), none)
        chip_ref[head, 0] = near[1][:, :WIDTH].astype(BF16)
        near = without_state(near)
        far = chosen(upper, joined(near, first), near)
        chip_ref[head, 1] = far[1][:, :WIDTH].astype(BF16)
        chip_copy(group, 0, head).start()
        store_prefix(group, without_state(far))

    def ring_step(group):
        half_copy(group, 0).wait_recv()
        mine, other = read(half_sent_ref.at[group]), read(half_ref.at[group])

        @pl.when(zh == 1)
        def _():
            write(ring_sent_ref.at[group], joined(mine, other))

        @pl.when(zh == 0)
        def _():
            write(ring_sent_ref.at[group], joined(other, mine))

        for d in (2, 1, 3):

            @pl.when(y + d < 4)
            def _():
                ring_copy(group, d).start()

        prefix = load_prefix(group)
        over = chosen(zh, joined(prefix, other), prefix)
        chip_ref[own_head(group), 2] = over[1][:, :WIDTH].astype(BF16)
        store_prefix(group, without_state(over))

    def last_step(group):
        for d in range(1, 4):

            @pl.when(y >= d)
            def _():
                ring_copy(group, d).wait_recv()

        head = own_head(group)
        odd, upper = lax.rem(y, 2), y // 2

        def slot(use, n):
            return read(ring_ref.at[group, use * n + (1 - use) * 3])

        prefix = load_prefix(group)
        oldest = joined(slot(upper, 1), slot(upper, 0))
        over = chosen(odd, joined(prefix, slot(odd, y - 1)), prefix)
        chip_ref[head, 3] = over[1][:, :WIDTH].astype(BF16)
        over = joined(without_state(over), oldest)
        chip_ref[head, 4] = (upper.astype(F32) * over[1][:, :WIDTH]).astype(BF16)
        chip_copy(group, 1, head).start()

    def readout_step(head):
        load(2, head).wait()
        readout_terms(
            head,
            q_ref,
            weight_ref,
            keys_ref,
            fading_ref,
            solved_ref,
            node_ref,
            keeps_ref,
            column_ref,
            out_ref,
            weighted_ref,
        )

    def gate_step(head):
        load(3, head).wait()
        gate = gate_ref[head].astype(F32)
        silu_ref[head] = gate / (1.0 + jnp.exp(-gate)) * gain_ref[...]

    def own_states(head, first, last):
        keep, body, _, last_id = read(core_came_ref.at[head])
        joins = core.astype(F32) * (own_ids()[0] == last_id).astype(F32)[:, :WIDTH]
        keep = joins * keep[:, :WIDTH] + (1.0 - core.astype(F32))
        erase = (joins * body[:, WIDTH:]).astype(BF16)
        states = [chip_ref[head, n] for n in range(first, last)]
        moved = dot(erase, jnp.concatenate(states, axis=1))
        carried = [
            (keep * state.astype(F32) - moved[:, n * WIDTH : (n + 1) * WIDTH]).astype(BF16)
            for n, state in enumerate(states)
        ]
        if first == 0:
            carried = [(joins * body[:, :WIDTH]).astype(BF16)] + carried
        return jnp.concatenate(carried, axis=0)

    def await_states(group, part, head):
        @pl.when(head != own_head(group))
        def _():
            chip_copy(group, part, head).wait_recv()

    def near_step(group, head):
        await_states(group, 0, head)
        states = own_states(head, 0, 2)
        out_ref[head] += dot(weighted_ref[head, :, : 3 * WIDTH], states)

    def finish_step(group, head):
        await_states(group, 1, head)
        states = own_states(head, 2, 5)
        ones = jnp.ones((WIDTH, WIDTH), BF16)
        total = out_ref[head] + dot(weighted_ref[head, :, 3 * WIDTH :], states)
        mean = dot((total * total).astype(BF16), ones) * (1.0 / WIDTH)
        normed_ref[head] = (total * lax.rsqrt(mean + EPSILON) * silu_ref[head]).astype(BF16)
        for d in (2, 1, 3):
            spread_copy(head, d).start()
        rows = pl.ds(pl.multiple_of(x * 256, 256), 256)
        columns = pl.ds(pl.multiple_of(x * 512 + head * WIDTH, WIDTH), WIDTH)
        gathered_ref[:, columns] = normed_ref[head, rows, :]

    def finish_group(group):
        for turn in range(2):
            @pl.when(core == 0)
            def _():
                finish_step(group, 2 * group + turn)

            @pl.when(core == 1)
            def _():
                finish_step(group, 2 * group + 1 - turn)

    def project_group(group):
        for head in (2 * group, 2 * group + 1):
            for d in (1, 2, 3):
                spread_copy(head, d).wait_recv()

        def tile(n, carry):
            columns = pl.ds(pl.multiple_of(n * 256, 256), 256)
            rows = slice(group * 256, (group + 1) * 256)
            total = sum(
                dot(gathered_ref[:, shard * 512 + group * 256 : shard * 512 + (group + 1) * 256], whole_ref[shard, rows, columns])
                for shard in range(4)
            )
            if group == 0:
                sum_ref[:, columns] = total
            else:
                result_ref[:, columns] = (total + sum_ref[:, columns]).astype(BF16)
            return carry

        lax.fori_loop(0, 8, tile, 0)

    for group in range(GROUPS):
        ring_ref[group, 3] = jnp.zeros((MESSAGE_ROWS, 2 * WIDTH), BF16)
    barrier = pltpu.get_barrier_semaphore()
    for axis, to in partners:
        pl.semaphore_signal(barrier, inc=1, device_id={axis: to}, device_id_type=MESH)
    for copy in smalls[:3]:
        copy.start()
    for head in range(HEADS_HERE):
        for which in range(2):
            load(which, head).start()
    for copy in smalls[3:]:
        copy.start()
    for head in range(HEADS_HERE):
        for which in (2, 3):
            load(which, head).start()
    own_w.start()
    smalls[0].wait()
    segs_ref[...] = seg_ref[...].astype(F32)
    prepare_masks(seg_ref, far_ref, pair_ref)
    for source, n in ((decay_ref, 0), (strength_ref, 1)):
        smalls[1 + n].wait()
        for each in range(HEADS_HERE):
            for b in range(BLOCKS):
                spread_ref[n, each, b : b + 1, :] = source[each : each + 1, rows_of(b)]

    pl.semaphore_wait(barrier, len(partners))
    for copy in w_first[:2]:
        copy.start()
    summary_step(0, lambda: None, lambda: None)
    summary_step(1, lambda: chip_step(0), lambda: None)
    for copy in smalls[3:]:
        copy.wait()
    for copy in w_first[2:]:
        copy.start()
    gate_step(0)
    chip_step(1)
    quad_step(0)
    for level in range(10):
        for each in range(HEADS_HERE):
            for b in range(BLOCKS):
                row = b * 16 + level
                weight_ref[each, row : row + 1, :] = weights_ref[level, each : each + 1, rows_of(b)]
    for head in range(HEADS_HERE):
        readout_step(head)
    for n in range(2):
        w_first[n].wait_recv()
        w_relay[n].start()
    gate_step(1)
    quad_step(1)
    ring_step(0)
    near_step(0, 0)
    near_step(0, 1)
    gate_step(2)
    gate_step(3)
    near_step(1, 2)
    near_step(1, 3)
    ring_step(1)
    last_step(0)
    finish_group(0)
    for n in range(2):
        w_first[2 + n].wait_recv()
        w_core[n].start()
    last_step(1)
    finish_group(1)
    for copy in w_relay:
        copy.wait_recv()
    w_core[2].start()
    own_w.wait()
    for copy in w_core:
        copy.wait_recv()
    project_group(0)
    project_group(1)
    for copy in w_first + w_relay + w_core:
        copy.wait_send()
    for head in range(HEADS_HERE):
        core_copy(head).wait_send()
        for d in (1, 2, 3):
            spread_copy(head, d).wait_send()
    for group in range(GROUPS):
        for d in (1, 2, 3):
            quad_copy(group, d).wait_send()
        for part in range(2):
            chip_copy(group, part, own_head(group)).wait_send()
        for d in range(1, 4):

            @pl.when(y + d < 4)
            def _():
                ring_copy(group, d).wait_send()

        @pl.when((zq == 0) | (zq == 3))
        def _():
            for n in range(2):
                half_copy(group, n).wait_send()


def shards(queries, keys, values, log_decay, write_strength, level_weights, segment, out_gate, norm_gain, w_out):
    far = pl.BlockSpec(memory_space=pl.ANY)
    near = pl.BlockSpec(memory_space=pltpu.VMEM)
    tall = (HEADS_HERE, TOKENS_HERE, WIDTH)
    wide = (MESSAGE_ROWS, 2 * WIDTH)
    return pl.pallas_call(
        layer_kernel,
        out_shape=jax.ShapeDtypeStruct((256, 2048), BF16),
        in_specs=[far] * 10,
        out_specs=near,
        scratch_shapes=[
            pltpu.VMEM(tall, BF16),
            pltpu.VMEM(tall, BF16),
            pltpu.VMEM(tall, BF16),
            pltpu.VMEM(tall, BF16),
            pltpu.VMEM((4, 512, 2048), BF16),
            pltpu.VMEM((HEADS_HERE, TOKENS_HERE), F32),
            pltpu.VMEM((HEADS_HERE, TOKENS_HERE), F32),
            pltpu.VMEM((LEVELS, HEADS_HERE, TOKENS_HERE), F32),
            pltpu.VMEM((BLOCKS, BLOCK), jnp.int32),
            pltpu.VMEM((1, WIDTH), F32),
            pltpu.VMEM((BLOCKS, BLOCK, BLOCK), F32),
            pltpu.VMEM((7, BLOCK, BLOCK), BF16),
            pltpu.VMEM((2, HEADS_HERE, BLOCKS, BLOCK), F32),
            pltpu.VMEM((HEADS_HERE, BLOCK, BLOCK), F32),
            pltpu.VMEM(tall, BF16),
            pltpu.VMEM((HEADS_HERE, BLOCKS, BLOCK, BLOCK), F32),
            pltpu.VMEM((HEADS_HERE, BLOCKS, BLOCK, 2 * WIDTH), BF16),
            pltpu.VMEM((HEADS_HERE, 7, BLOCK, 2 * WIDTH), BF16),
            pltpu.VMEM((HEADS_HERE, 8, WIDTH), F32),
            pltpu.VMEM((HEADS_HERE, BLOCK, BLOCK), F32),
            pltpu.VMEM(tall, F32),
            pltpu.VMEM((HEADS_HERE, TOKENS_HERE, 6 * WIDTH), BF16),
            pltpu.VMEM(tall, F32),
            pltpu.VMEM(tall, BF16),
            pltpu.VMEM((256, 2048), BF16),
            pltpu.VMEM((256, 2048), F32),
            pltpu.VMEM((HEADS_HERE,) + wide, BF16),
            pltpu.VMEM((HEADS_HERE,) + wide, BF16),
            pltpu.VMEM((GROUPS, 4) + wide, BF16),
            pltpu.VMEM((GROUPS,) + wide, BF16),
            pltpu.VMEM((GROUPS,) + wide, BF16),
            pltpu.VMEM((GROUPS,) + wide, BF16),
            pltpu.VMEM((GROUPS, 4) + wide, BF16),
            pltpu.VMEM((HEADS_HERE, BLOCK, 2 * WIDTH), F32),
            pltpu.VMEM((HEADS_HERE, 8, 2 * WIDTH), F32),
            pltpu.VMEM((GROUPS, BLOCK, 2 * WIDTH), F32),
            pltpu.VMEM((GROUPS, 8, 2 * WIDTH), F32),
            pltpu.VMEM((HEADS_HERE, 5, BLOCK, WIDTH), BF16),
            pltpu.VMEM((BLOCKS, BLOCK), F32),
            pltpu.SemaphoreType.DMA((4, HEADS_HERE)),
            pltpu.SemaphoreType.DMA((5,)),
            pltpu.SemaphoreType.DMA,
            pltpu.SemaphoreType.DMA((2, HEADS_HERE)),
            pltpu.SemaphoreType.DMA((2, GROUPS, 3)),
            pltpu.SemaphoreType.DMA((GROUPS, 2)),
            pltpu.SemaphoreType.DMA((GROUPS,)),
            pltpu.SemaphoreType.DMA((2, GROUPS, 3)),
            pltpu.SemaphoreType.DMA((2, GROUPS, 2)),
            pltpu.SemaphoreType.DMA((HEADS_HERE, 3)),
            pltpu.SemaphoreType.DMA((HEADS_HERE, 3)),
            pltpu.SemaphoreType.DMA((9,)),
            pltpu.SemaphoreType.DMA((9,)),
        ],
        compiler_params=pltpu.CompilerParams(
            collective_id=0, has_side_effects=True, vmem_limit_bytes=58 << 20
        ),
        cost_estimate=pl.CostEstimate(flops=24_000_000_000, bytes_accessed=16_000_000, transcendentals=0),
    )(
        queries,
        keys,
        values,
        out_gate,
        w_out,
        log_decay,
        write_strength,
        level_weights.transpose(1, 0, 2),
        segment.reshape(BLOCKS, BLOCK),
        norm_gain.reshape(1, WIDTH),
    )


def solution(mesh):
    placed = (
        P("ctx", "head"),
        P("ctx", "head"),
        P("ctx", "head"),
        P("head", "ctx"),
        P("head", "ctx"),
        P("head", None, "ctx"),
        P("ctx"),
        P("ctx", "head"),
        P(),
        P("head", None),
    )
    return jax.shard_map(
        shards, mesh=mesh, in_specs=placed, out_specs=P(("ctx", "head"), None), check_vma=False
    )
```

```python
import jax
import jax.numpy as jnp
from jax import lax
from jax.experimental import pallas as pl
from jax.experimental.pallas import tpu as pltpu
from jax.sharding import PartitionSpec as P

BLOCK = 128
BLOCKS = 8
TOKENS_HERE = 1024
HEADS_HERE = 4
WIDTH = 128
LEVELS = 12
EPSILON = 1e-06
FAR = -1e4
MESSAGE_ROWS = 144

F32 = jnp.float32
BF16 = jnp.bfloat16


def dot(left, right):
    return jnp.dot(left, right, preferred_element_type=F32)


def dot_rows(left, right):
    return lax.dot_general(left, right, (((1,), (1,)), ((), ())), preferred_element_type=F32)


def dot_columns(left, right):
    return lax.dot_general(left, right, (((0,), (0,)), ((), ())), preferred_element_type=F32)


def split3(value):
    first = value.astype(BF16)
    rest = value - first.astype(F32)
    second = rest.astype(BF16)
    third = (rest - second.astype(F32)).astype(BF16)
    return first, second, third


def rows_of(block):
    return slice(block * BLOCK, (block + 1) * BLOCK)


def prepare_masks(seg_ref, far_ref, pair_ref):
    row = lax.broadcasted_iota(jnp.int32, (BLOCK, BLOCK), 0)
    col = lax.broadcasted_iota(jnp.int32, (BLOCK, BLOCK), 1)
    segs = seg_ref[...].astype(F32)
    padded = jnp.concatenate([segs, jnp.zeros((BLOCK - BLOCKS, BLOCK), F32)], axis=0)
    seg_cols = padded.T
    for block in range(BLOCKS):
        same = seg_cols[:, block : block + 1] == segs[block : block + 1, :]
        far_ref[block] = jnp.where(same & (row >= col), 0.0, FAR)
    for step in range(7):
        size = 1 << step
        chosen = (row // size == col // size + 1) & (row // size % 2 == 1)
        pair_ref[step] = jnp.where(chosen, 1.0, 0.0).astype(BF16)


def unit_rows(rows, ones):
    wide = rows.astype(F32)
    total = dot((wide * wide).astype(BF16), ones)
    return (wide * lax.rsqrt(total + EPSILON)).astype(BF16)


def columns_of(rows):
    return jnp.concatenate([rows, jnp.zeros((BLOCK - rows.shape[0], BLOCK), F32)], axis=0).T


def column_at(columns, kind, block):
    at = kind * BLOCKS + block
    return columns[:, at : at + 1]


def summary_terms(heads, k_ref, v_ref, spread_ref, segs, far_ref, pair_ref, keys_ref, fading_ref, solved_ref, node_ref, keeps_ref, column_ref, between):
    row = lax.broadcasted_iota(jnp.int32, (BLOCK, BLOCK), 0)
    col = lax.broadcasted_iota(jnp.int32, (BLOCK, BLOCK), 1)
    every = range(BLOCKS)
    all_blocks = [(h, b) for h in range(len(heads)) for b in every]
    ones = jnp.ones((BLOCK, BLOCK), BF16)
    upto = jnp.where(row <= col, 1.0, 0.0).astype(BF16)
    last_seg = jnp.broadcast_to(segs[:, BLOCK - 1 :], (BLOCKS, BLOCK))
    first_seg = jnp.broadcast_to(segs[:, :1], (BLOCKS, BLOCK))
    before = jnp.concatenate([first_seg[:1], last_seg[:-1]], axis=0)
    opens = (segs == before).astype(F32)
    closes = (segs == last_seg).astype(F32)
    through = (last_seg == before).astype(F32)
    summed, columns, keep = [], [], []
    for head in heads:
        strength = spread_ref[1, head]
        total = sum(dot(part, upto) for part in split3(spread_ref[0, head]))
        last_sum = jnp.broadcast_to(total[:, BLOCK - 1 :], (BLOCKS, BLOCK))
        opening = jnp.exp(total) * opens
        closing = jnp.exp(last_sum - total) * closes
        keeps = jnp.exp(last_sum) * through
        columns.append(
            columns_of(jnp.concatenate([total, strength, opening, strength * opening, closing], axis=0))
        )
        summed.append(total)
        keep.append([keeps[b : b + 1] for b in every])
        column_ref[head] = columns[-1]
    kn = {}
    for h, head in enumerate(heads):
        unit = unit_rows(k_ref[head], ones)
        for b in every:
            kn[h, b] = unit[rows_of(b)]
    grams = {i: dot_rows(kn[i], kn[i]) for i in all_blocks}
    lower = {}
    for h, b in all_blocks:
        fading = jnp.exp(column_at(columns[h], 0, b) - summed[h][b : b + 1, :] + far_ref[b])
        fading_ref[heads[h], b] = fading
        lower[h, b] = (column_at(columns[h], 1, b) * fading * grams[h, b]).astype(BF16)
    between()
    eye = jnp.where(row == col, 1.0, 0.0).astype(BF16)
    inverse = {i: eye - lower[i] * pair_ref[0] for i in all_blocks}
    for step in range(1, 7):
        mask = pair_ref[step]
        half = {i: dot(inverse[i], lower[i] * mask).astype(BF16) for i in all_blocks}
        inverse = {i: inverse[i] - dot(half[i], inverse[i]).astype(BF16) for i in all_blocks}
    joined = {}
    for h, b in all_blocks:
        wide = kn[h, b].astype(F32)
        right = jnp.concatenate(
            [
                (column_at(columns[h], 1, b) * v_ref[heads[h], rows_of(b), :].astype(F32)).astype(BF16),
                (column_at(columns[h], 3, b) * wide).astype(BF16),
            ],
            axis=1,
        )
        solved = dot(inverse[h, b], right).astype(BF16)
        solved_ref[heads[h], b] = solved
        ended = (column_at(columns[h], 4, b) * wide).astype(BF16)
        joined[h, b] = dot_columns(ended, solved)
        keys_ref[heads[h], rows_of(b), :] = kn[h, b]
    nodes = [[joined[h, b] for b in every] for h in range(len(heads))]
    first = 0
    for level in range(3):
        many = len(nodes[0]) // 2
        for h, head in enumerate(heads):
            merged, kept = [], []
            for pair in range(many):
                early, late = nodes[h][2 * pair], nodes[h][2 * pair + 1]
                keep_e, keep_o = keep[h][2 * pair], keep[h][2 * pair + 1]
                node = early.astype(BF16)
                node_ref[head, first + pair] = node
                keeps_ref[head, first + pair : first + pair + 1, :] = keep_e
                moved = dot(late[:, WIDTH:].astype(BF16), node)
                carried = jnp.concatenate([late[:, :WIDTH], keep_e * late[:, WIDTH:]], axis=1)
                merged.append(jnp.concatenate([keep_o, keep_o], axis=1) * early + carried - moved)
                kept.append(keep_e * keep_o)
            nodes[h], keep[h] = merged, kept
        first = first + many
    return [(nodes[h][0], keep[h][0]) for h in range(len(heads))]


def readout_terms(head, q_ref, weight_ref, keys_ref, fading_ref, solved_ref, node_ref, keeps_ref, column_ref, out_ref, weighted_ref):
    every = range(BLOCKS)
    ones = jnp.ones((BLOCK, BLOCK), BF16)
    columns = column_ref[head]
    wcols = weight_ref[head].T

    def weight(level, block):
        at = block * 16 + level
        return wcols[:, at : at + 1]

    qn = unit_rows(q_ref[head], ones)
    scores = [
        (fading_ref[head, b] * dot_rows(qn[rows_of(b)], keys_ref[head, rows_of(b), :])).astype(BF16) for b in every
    ]
    both = [dot(scores[b], solved_ref[head, b]) for b in every]
    out = [weight(0, b) * both[b][:, :WIDTH] for b in every]
    reads = [column_at(columns, 2, b) * qn[rows_of(b)].astype(F32) - both[b][:, WIDTH:] for b in every]
    first = 0
    for level in range(1, 4):
        span = 1 << (level - 1)
        many = BLOCKS // (2 * span)
        for pair in range(many):
            later = [b for b in every if b // span == 2 * pair + 1]
            stack = jnp.concatenate([reads[b] for b in later], axis=0).astype(BF16)
            moved = dot(stack, node_ref[head, first + pair])
            keep = keeps_ref[head, first + pair : first + pair + 1, :]
            for at, b in enumerate(later):
                part = moved[at * BLOCK : (at + 1) * BLOCK]
                out[b] = out[b] + weight(level, b) * part[:, :WIDTH]
                reads[b] = keep * reads[b] - part[:, WIDTH:]
        first = first + many
    for b in every:
        out_ref[head, rows_of(b), :] = out[b]
        weighted_ref[head, rows_of(b), :] = jnp.concatenate(
            [(weight(level, b) * reads[b]).astype(BF16) for level in range(4, 10)], axis=1
        )

MESH = pl.DeviceIdType.MESH
GROUPS = 2


def joined(late, early):
    keep_l, body_l, first_l, last_l = late
    keep_e, body_e, first_e, last_e = early
    same = (first_l == last_e).astype(F32)
    moved = dot(body_l[:, WIDTH:].astype(BF16), body_e.astype(BF16))
    carried = jnp.concatenate([body_l[:, :WIDTH], (same * keep_e)[:, WIDTH:] * body_l[:, WIDTH:]], axis=1)
    keep_l = same * keep_l
    return keep_l * keep_e, keep_l * body_e + carried - same * moved, first_e, last_l


def without_state(summary):
    keep, body, first, last = summary
    return keep, jnp.concatenate([jnp.zeros((BLOCK, WIDTH), F32), body[:, WIDTH:]], axis=1), first, last


def chosen(use, one, other):
    use = use.astype(F32)
    return tuple(use * a + (1.0 - use) * b for a, b in zip(one, other))


def tail_rows(summary):
    keep, _, first_id, last_id = summary
    parts = [part.astype(F32) for part in split3(keep)] + [first_id, last_id]
    return jnp.concatenate(parts + [jnp.zeros((11, 2 * WIDTH), F32)], axis=0).astype(BF16)


def layer_kernel(
    q_hbm,
    k_hbm,
    v_hbm,
    gate_hbm,
    w_hbm,
    decay_hbm,
    strength_hbm,
    weights_hbm,
    seg_hbm,
    gain_hbm,
    result_ref,
    q_ref,
    k_ref,
    v_ref,
    gate_ref,
    whole_ref,
    decay_ref,
    strength_ref,
    weights_ref,
    seg_ref,
    gain_ref,
    far_ref,
    pair_ref,
    spread_ref,
    weight_ref,
    keys_ref,
    fading_ref,
    solved_ref,
    node_ref,
    keeps_ref,
    column_ref,
    out_ref,
    weighted_ref,
    silu_ref,
    normed_ref,
    gathered_ref,
    sum_ref,
    core_sent_ref,
    core_came_ref,
    quad_ref,
    half_sent_ref,
    half_ref,
    ring_sent_ref,
    ring_ref,
    total_ref,
    keep_ref,
    prefix_ref,
    prekeep_ref,
    chip_ref,
    segs_ref,
    load_sem,
    small_sem,
    own_sem,
    core_sem,
    quad_sem,
    half_sent_sem,
    half_came_sem,
    ring_sem,
    chip_sem,
    out_sem,
    in_sem,
    w_sent_sem,
    w_came_sem,
):
    ctx = lax.axis_index("ctx")
    x = lax.axis_index("head")
    core = lax.rem(ctx, 2)
    z = lax.rem(ctx // 2, 8)
    y = ctx // 16
    zq = lax.rem(z, 4)
    zh = z // 4
    right, left, opposite = lax.rem(x + 1, 4), lax.rem(x + 3, 4), lax.rem(x + 2, 4)
    other_core = ctx + 1 - 2 * core

    def at(y_to, z_to):
        return (y_to * 8 + z_to) * 2 + core

    def quad_to(d):
        return at(y, zh * 4 + lax.rem(zq + d, 4))

    def half_to(n):
        return at(y, 7 - z + n * (2 * (zq // 3) - 1))

    def ring_to(d):
        return at(lax.rem(y + d, 4), z)

    def remote(source, target, sent, came, axis, to):
        return pltpu.make_async_remote_copy(
            src_ref=source,
            dst_ref=target,
            send_sem=sent,
            recv_sem=came,
            device_id={axis: to},
            device_id_type=MESH,
        )

    partners = [("ctx", other_core)]
    partners += [("ctx", at(y, lax.rem(z + d, 8))) for d in range(1, 8)]
    partners += [("ctx", ring_to(d)) for d in (1, 2, 3)]
    partners += [("head", lax.rem(x + d, 4)) for d in (1, 2, 3)]

    sources = ((k_hbm, k_ref), (v_hbm, v_ref), (q_hbm, q_ref), (gate_hbm, gate_ref))

    def load(which, head):
        source, target = sources[which]
        columns = slice(head * WIDTH, (head + 1) * WIDTH)
        return pltpu.make_async_copy(source.at[:, columns], target.at[head], load_sem.at[which, head])

    smalls = [
        pltpu.make_async_copy(source, target, small_sem.at[n])
        for n, (source, target) in enumerate(
            (
                (seg_hbm, seg_ref),
                (decay_hbm, decay_ref),
                (strength_hbm, strength_ref),
                (weights_hbm, weights_ref),
                (gain_hbm, gain_ref),
            )
        )
    ]
    own_w = pltpu.make_async_copy(w_hbm, whole_ref.at[x], own_sem)
    quarters = [pl.ds(pl.multiple_of(core * 256 + part * 128, 128), 128) for part in range(2)]
    pieces = [
        pl.ds(pl.multiple_of(core * 256 + part * 128 + lax.rem(y, 2) * 64, 64), 64) for part in range(2)
    ]
    half_rows = pl.ds(pl.multiple_of(core * 256, 256), 256)

    def w_copy(n, source, shard, rows, axis, to):
        return remote(source, whole_ref.at[shard, rows], w_sent_sem.at[n], w_came_sem.at[n], axis, to)

    w_first = [
        w_copy(0, w_hbm.at[quarters[0]], x, quarters[0], "head", right),
        w_copy(1, w_hbm.at[quarters[1]], x, quarters[1], "head", left),
        w_copy(2, w_hbm.at[quarters[1]], x, quarters[1], "head", right),
        w_copy(3, w_hbm.at[quarters[0]], x, quarters[0], "head", left),
    ]
    w_relay = [
        w_copy(4, whole_ref.at[left, pieces[0]], left, pieces[0], "head", right),
        w_copy(5, whole_ref.at[right, pieces[1]], right, pieces[1], "head", left),
    ]
    w_share = [
        w_copy(9, whole_ref.at[opposite, pieces[0]], opposite, pieces[0], "ctx", at(y + 1 - 2 * lax.rem(y, 2), z)),
        w_copy(10, whole_ref.at[opposite, pieces[1]], opposite, pieces[1], "ctx", at(3 - y, z)),
    ]
    w_core = [
        w_copy(6 + n, whole_ref.at[shard, half_rows], shard, half_rows, "ctx", other_core)
        for n, shard in enumerate((left, right, opposite))
    ]

    def core_copy(head):
        return remote(
            core_sent_ref.at[head], core_came_ref.at[head], core_sem.at[0, head], core_sem.at[1, head], "ctx", other_core
        )

    def quad_copy(group, d):
        mine = quad_ref.at[group, zq]
        return remote(mine, mine, quad_sem.at[0, group, d - 1], quad_sem.at[1, group, d - 1], "ctx", quad_to(d))

    def half_copy(group, n):
        return remote(
            half_sent_ref.at[group],
            half_ref.at[group],
            half_sent_sem.at[group, n],
            half_came_sem.at[group],
            "ctx",
            half_to(n),
        )

    def ring_copy(group, d):
        return remote(
            ring_sent_ref.at[group],
            ring_ref.at[group, y],
            ring_sem.at[0, group, d - 1],
            ring_sem.at[1, group, d - 1],
            "ctx",
            ring_to(d),
        )

    def chip_copy(group, part, head):
        mine = chip_ref.at[head, pl.ds(2 * part, 2 + part)]
        return remote(mine, mine, chip_sem.at[0, group, part], chip_sem.at[1, group, part], "ctx", other_core)

    def spread_copy(head, d):
        to = lax.rem(x + d, 4)
        rows = pl.ds(pl.multiple_of(to * 256, 256), 256)
        columns = pl.ds(pl.multiple_of(x * 512 + head * WIDTH, WIDTH), WIDTH)
        return remote(
            normed_ref.at[head, rows],
            gathered_ref.at[:, columns],
            out_sem.at[head, d - 1],
            in_sem.at[head, d - 1],
            "head",
            to,
        )

    def own_head(group):
        return 2 * group + core

    def read(ref):
        tail = ref[BLOCK:, :].astype(F32)
        return tail[0:1] + tail[1:2] + tail[2:3], ref[:BLOCK, :].astype(F32), tail[3:4], tail[4:5]

    def write(ref, summary):
        ref[:BLOCK, :] = summary[1].astype(BF16)
        ref[BLOCK:, :] = tail_rows(summary)

    def own_ids():
        first_id = jnp.broadcast_to(segs_ref[0:1, :1], (1, 2 * WIDTH))
        last_id = jnp.broadcast_to(segs_ref[BLOCKS - 1 :, WIDTH - 1 :], (1, 2 * WIDTH))
        return first_id, last_id

    def summary_step(group, between, ready):
        heads = [2 * group, 2 * group + 1]
        for head in heads:
            for which in range(2):
                load(which, head).wait()
        found = summary_terms(
            heads,
            k_ref,
            v_ref,
            spread_ref,
            segs_ref[...],
            far_ref,
            pair_ref,
            keys_ref,
            fading_ref,
            solved_ref,
            node_ref,
            keeps_ref,
            column_ref,
            between,
        )
        ready()
        for head, (body, keep) in zip(heads, found):
            keep = jnp.concatenate([keep, keep], axis=1)
            total_ref[head] = body
            keep_ref[head] = jnp.broadcast_to(keep, (8, 2 * WIDTH))
            write(core_sent_ref.at[head], (keep, body) + own_ids())
            core_copy(head).start()

    def chip_step(group):
        for head in (2 * group, 2 * group + 1):
            core_copy(head).wait_recv()
        head = own_head(group)
        mine = (keep_ref[head, 0:1, :], total_ref[head]) + own_ids()
        other = read(core_came_ref.at[head])
        to = quad_ref.at[group, zq]

        @pl.when(core == 1)
        def _():
            write(to, joined(mine, other))

        @pl.when(core == 0)
        def _():
            write(to, joined(other, mine))

        for d in (1, 3, 2):
            quad_copy(group, d).start()

    def store_prefix(group, prefix):
        prefix_ref[group] = prefix[1]
        prekeep_ref[group, 0:1, :] = prefix[0]
        prekeep_ref[group, 1:2, :] = prefix[2]

    def load_prefix(group):
        first_id = prekeep_ref[group, 1:2, :]
        return prekeep_ref[group, 0:1, :], prefix_ref[group], first_id, first_id

    def quad_step(group):
        for d in (1, 2, 3):
            quad_copy(group, d).wait_recv()
        parts = [read(quad_ref.at[group, n]) for n in range(4)]
        first, second = joined(parts[1], parts[0]), joined(parts[3], parts[2])
        write(half_sent_ref.at[group], joined(second, first))

        @pl.when((zq == 0) | (zq == 3))
        def _():
            for n in (1, 0):
                half_copy(group, n).start()

        head = own_head(group)
        odd = lax.rem(zq, 2)
        upper = zq // 2
        own_first = read(quad_ref.at[group, zq])[2]
        none = jnp.ones((1, 2 * WIDTH), F32), jnp.zeros((BLOCK, 2 * WIDTH), F32), own_first, own_first
        keep, body, first_id, last_id = read(quad_ref.at[group, odd * (zq - odd)])
        same = (own_first == last_id).astype(F32)
        near = chosen(odd, (same * keep, same * body, first_id, first_id), none)
        chip_ref[head, 0] = near[1][:, :WIDTH].astype(BF16)
        near = without_state(near)
        far = chosen(upper, joined(near, first), near)
        chip_ref[head, 1] = far[1][:, :WIDTH].astype(BF16)
        chip_copy(group, 0, head).start()
        store_prefix(group, without_state(far))

    def ring_step(group):
        half_copy(group, 0).wait_recv()
        mine, other = read(half_sent_ref.at[group]), read(half_ref.at[group])

        @pl.when(zh == 1)
        def _():
            write(ring_sent_ref.at[group], joined(mine, other))

        @pl.when(zh == 0)
        def _():
            write(ring_sent_ref.at[group], joined(other, mine))

        for d in (2, 1, 3):

            @pl.when(y + d < 4)
            def _():
                ring_copy(group, d).start()

        prefix = load_prefix(group)
        over = chosen(zh, joined(prefix, other), prefix)
        chip_ref[own_head(group), 2] = over[1][:, :WIDTH].astype(BF16)
        store_prefix(group, without_state(over))

    def last_step(group):
        for d in range(1, 4):

            @pl.when(y >= d)
            def _():
                ring_copy(group, d).wait_recv()

        head = own_head(group)
        odd, upper = lax.rem(y, 2), y // 2

        def slot(use, n):
            return read(ring_ref.at[group, use * n + (1 - use) * 3])

        prefix = load_prefix(group)
        oldest = joined(slot(upper, 1), slot(upper, 0))
        over = chosen(odd, joined(prefix, slot(odd, y - 1)), prefix)
        chip_ref[head, 3] = over[1][:, :WIDTH].astype(BF16)
        over = joined(without_state(over), oldest)
        chip_ref[head, 4] = (upper.astype(F32) * over[1][:, :WIDTH]).astype(BF16)
        chip_copy(group, 1, head).start()

    def readout_step(head):
        load(2, head).wait()
        readout_terms(
            head,
            q_ref,
            weight_ref,
            keys_ref,
            fading_ref,
            solved_ref,
            node_ref,
            keeps_ref,
            column_ref,
            out_ref,
            weighted_ref,
        )

    def gate_step(head):
        load(3, head).wait()
        gate = gate_ref[head].astype(F32)
        silu_ref[head] = gate / (1.0 + jnp.exp(-gate)) * gain_ref[...]

    def own_states(head, first, last):
        keep, body, _, last_id = read(core_came_ref.at[head])
        joins = core.astype(F32) * (own_ids()[0] == last_id).astype(F32)[:, :WIDTH]
        keep = joins * keep[:, :WIDTH] + (1.0 - core.astype(F32))
        erase = (joins * body[:, WIDTH:]).astype(BF16)
        states = [chip_ref[head, n] for n in range(first, last)]
        moved = dot(erase, jnp.concatenate(states, axis=1))
        carried = [
            (keep * state.astype(F32) - moved[:, n * WIDTH : (n + 1) * WIDTH]).astype(BF16)
            for n, state in enumerate(states)
        ]
        if first == 0:
            carried = [(joins * body[:, :WIDTH]).astype(BF16)] + carried
        return jnp.concatenate(carried, axis=0)

    def await_states(group, part, head):
        @pl.when(head != own_head(group))
        def _():
            chip_copy(group, part, head).wait_recv()

    def near_step(group, head):
        await_states(group, 0, head)
        states = own_states(head, 0, 2)
        out_ref[head] += dot(weighted_ref[head, :, : 3 * WIDTH], states)

    def finish_step(group, head):
        await_states(group, 1, head)
        states = own_states(head, 2, 5)
        ones = jnp.ones((WIDTH, WIDTH), BF16)
        total = out_ref[head] + dot(weighted_ref[head, :, 3 * WIDTH :], states)
        mean = dot((total * total).astype(BF16), ones) * (1.0 / WIDTH)
        normed_ref[head] = (total * lax.rsqrt(mean + EPSILON) * silu_ref[head]).astype(BF16)
        for d in (2, 1, 3):
            spread_copy(head, d).start()
        rows = pl.ds(pl.multiple_of(x * 256, 256), 256)
        columns = pl.ds(pl.multiple_of(x * 512 + head * WIDTH, WIDTH), WIDTH)
        gathered_ref[:, columns] = normed_ref[head, rows, :]

    def finish_group(group):
        for turn in range(2):
            @pl.when(core == 0)
            def _():
                finish_step(group, 2 * group + turn)

            @pl.when(core == 1)
            def _():
                finish_step(group, 2 * group + 1 - turn)

    def part_of(group, shard, columns):
        mine = pl.ds(pl.multiple_of(shard * 512 + group * 256, 256), 256)
        return dot(gathered_ref[:, mine], whole_ref[shard, group * 256 : (group + 1) * 256, columns])

    def arrived(group, ways):
        for head in (2 * group, 2 * group + 1):
            for d in ways:
                spread_copy(head, d).wait_recv()

    def by_tiles(work):
        def tile(n, carry):
            work(pl.ds(pl.multiple_of(n * 512, 512), 512))
            return carry

        lax.fori_loop(0, 4, tile, 0)

    def project_near(columns):
        sum_ref[:, columns] = part_of(0, x, columns) + part_of(0, left, columns) + part_of(0, right, columns)

    def project_far(columns):
        sum_ref[:, columns] += part_of(0, opposite, columns)

    def project_rest(columns):
        total = sum(part_of(1, shard, columns) for shard in (x, left, right, opposite))
        result_ref[:, columns] = (sum_ref[:, columns] + total).astype(BF16)

    for group in range(GROUPS):
        ring_ref[group, 3] = jnp.zeros((MESSAGE_ROWS, 2 * WIDTH), BF16)
    barrier = pltpu.get_barrier_semaphore()
    for axis, to in partners:
        pl.semaphore_signal(barrier, inc=1, device_id={axis: to}, device_id_type=MESH)
    for copy in smalls[:3]:
        copy.start()
    for head in range(HEADS_HERE):
        for which in range(2):
            load(which, head).start()
    for copy in smalls[3:]:
        copy.start()
    for head in range(HEADS_HERE):
        for which in (2, 3):
            load(which, head).start()
    own_w.start()
    smalls[0].wait()
    segs_ref[...] = seg_ref[...].astype(F32)
    prepare_masks(seg_ref, far_ref, pair_ref)
    for source, n in ((decay_ref, 0), (strength_ref, 1)):
        smalls[1 + n].wait()
        for each in range(HEADS_HERE):
            for b in range(BLOCKS):
                spread_ref[n, each, b : b + 1, :] = source[each : each + 1, rows_of(b)]

    pl.semaphore_wait(barrier, len(partners))
    for copy in w_first[:2]:
        copy.start()
    summary_step(0, lambda: None, lambda: None)
    summary_step(1, lambda: chip_step(0), lambda: None)
    for copy in smalls[3:]:
        copy.wait()
    for copy in w_first[2:]:
        copy.start()
    gate_step(0)
    chip_step(1)
    quad_step(0)
    for level in range(10):
        for each in range(HEADS_HERE):
            for b in range(BLOCKS):
                row = b * 16 + level
                weight_ref[each, row : row + 1, :] = weights_ref[level, each : each + 1, rows_of(b)]
    for head in range(HEADS_HERE):
        readout_step(head)
    for n in range(2):
        w_first[n].wait_recv()
        w_relay[n].start()
    gate_step(1)
    quad_step(1)
    ring_step(0)
    near_step(0, 0)
    near_step(0, 1)
    gate_step(2)
    gate_step(3)
    near_step(1, 2)
    near_step(1, 3)
    ring_step(1)
    for n in range(2):
        w_relay[n].wait_recv()
        w_share[n].start()
    last_step(0)
    finish_group(0)
    for n in range(2):
        w_first[2 + n].wait_recv()
        w_core[n].start()
    last_step(1)
    finish_group(1)
    for copy in w_share:
        copy.wait_recv()
    w_core[2].start()
    own_w.wait()
    for copy in w_core[:2]:
        copy.wait_recv()
    arrived(0, (1, 3))
    by_tiles(project_near)
    w_core[2].wait_recv()
    arrived(0, (2,))
    by_tiles(project_far)
    arrived(1, (1, 3, 2))
    by_tiles(project_rest)
    for copy in w_first + w_relay + w_share + w_core:
        copy.wait_send()
    for head in range(HEADS_HERE):
        core_copy(head).wait_send()
        for d in (1, 2, 3):
            spread_copy(head, d).wait_send()
    for group in range(GROUPS):
        for d in (1, 2, 3):
            quad_copy(group, d).wait_send()
        for part in range(2):
            chip_copy(group, part, own_head(group)).wait_send()
        for d in range(1, 4):

            @pl.when(y + d < 4)
            def _():
                ring_copy(group, d).wait_send()

        @pl.when((zq == 0) | (zq == 3))
        def _():
            for n in range(2):
                half_copy(group, n).wait_send()


def shards(queries, keys, values, log_decay, write_strength, level_weights, segment, out_gate, norm_gain, w_out):
    far = pl.BlockSpec(memory_space=pl.ANY)
    near = pl.BlockSpec(memory_space=pltpu.VMEM)
    tall = (HEADS_HERE, TOKENS_HERE, WIDTH)
    wide = (MESSAGE_ROWS, 2 * WIDTH)
    return pl.pallas_call(
        layer_kernel,
        out_shape=jax.ShapeDtypeStruct((256, 2048), BF16),
        in_specs=[far] * 10,
        out_specs=near,
        scratch_shapes=[
            pltpu.VMEM(tall, BF16),
            pltpu.VMEM(tall, BF16),
            pltpu.VMEM(tall, BF16),
            pltpu.VMEM(tall, BF16),
            pltpu.VMEM((4, 512, 2048), BF16),
            pltpu.VMEM((HEADS_HERE, TOKENS_HERE), F32),
            pltpu.VMEM((HEADS_HERE, TOKENS_HERE), F32),
            pltpu.VMEM((LEVELS, HEADS_HERE, TOKENS_HERE), F32),
            pltpu.VMEM((BLOCKS, BLOCK), jnp.int32),
            pltpu.VMEM((1, WIDTH), F32),
            pltpu.VMEM((BLOCKS, BLOCK, BLOCK), F32),
            pltpu.VMEM((7, BLOCK, BLOCK), BF16),
            pltpu.VMEM((2, HEADS_HERE, BLOCKS, BLOCK), F32),
            pltpu.VMEM((HEADS_HERE, BLOCK, BLOCK), F32),
            pltpu.VMEM(tall, BF16),
            pltpu.VMEM((HEADS_HERE, BLOCKS, BLOCK, BLOCK), F32),
            pltpu.VMEM((HEADS_HERE, BLOCKS, BLOCK, 2 * WIDTH), BF16),
            pltpu.VMEM((HEADS_HERE, 7, BLOCK, 2 * WIDTH), BF16),
            pltpu.VMEM((HEADS_HERE, 8, WIDTH), F32),
            pltpu.VMEM((HEADS_HERE, BLOCK, BLOCK), F32),
            pltpu.VMEM(tall, F32),
            pltpu.VMEM((HEADS_HERE, TOKENS_HERE, 6 * WIDTH), BF16),
            pltpu.VMEM(tall, F32),
            pltpu.VMEM(tall, BF16),
            pltpu.VMEM((256, 2048), BF16),
            pltpu.VMEM((256, 2048), F32),
            pltpu.VMEM((HEADS_HERE,) + wide, BF16),
            pltpu.VMEM((HEADS_HERE,) + wide, BF16),
            pltpu.VMEM((GROUPS, 4) + wide, BF16),
            pltpu.VMEM((GROUPS,) + wide, BF16),
            pltpu.VMEM((GROUPS,) + wide, BF16),
            pltpu.VMEM((GROUPS,) + wide, BF16),
            pltpu.VMEM((GROUPS, 4) + wide, BF16),
            pltpu.VMEM((HEADS_HERE, BLOCK, 2 * WIDTH), F32),
            pltpu.VMEM((HEADS_HERE, 8, 2 * WIDTH), F32),
            pltpu.VMEM((GROUPS, BLOCK, 2 * WIDTH), F32),
            pltpu.VMEM((GROUPS, 8, 2 * WIDTH), F32),
            pltpu.VMEM((HEADS_HERE, 5, BLOCK, WIDTH), BF16),
            pltpu.VMEM((BLOCKS, BLOCK), F32),
            pltpu.SemaphoreType.DMA((4, HEADS_HERE)),
            pltpu.SemaphoreType.DMA((5,)),
            pltpu.SemaphoreType.DMA,
            pltpu.SemaphoreType.DMA((2, HEADS_HERE)),
            pltpu.SemaphoreType.DMA((2, GROUPS, 3)),
            pltpu.SemaphoreType.DMA((GROUPS, 2)),
            pltpu.SemaphoreType.DMA((GROUPS,)),
            pltpu.SemaphoreType.DMA((2, GROUPS, 3)),
            pltpu.SemaphoreType.DMA((2, GROUPS, 2)),
            pltpu.SemaphoreType.DMA((HEADS_HERE, 3)),
            pltpu.SemaphoreType.DMA((HEADS_HERE, 3)),
            pltpu.SemaphoreType.DMA((11,)),
            pltpu.SemaphoreType.DMA((11,)),
        ],
        compiler_params=pltpu.CompilerParams(
            collective_id=0, has_side_effects=True, vmem_limit_bytes=58 << 20
        ),
        cost_estimate=pl.CostEstimate(flops=24_000_000_000, bytes_accessed=16_000_000, transcendentals=0),
    )(
        queries,
        keys,
        values,
        out_gate,
        w_out,
        log_decay,
        write_strength,
        level_weights.transpose(1, 0, 2),
        segment.reshape(BLOCKS, BLOCK),
        norm_gain.reshape(1, WIDTH),
    )


def solution(mesh):
    placed = (
        P("ctx", "head"),
        P("ctx", "head"),
        P("ctx", "head"),
        P("head", "ctx"),
        P("head", "ctx"),
        P("head", None, "ctx"),
        P("ctx"),
        P("ctx", "head"),
        P(),
        P("head", None),
    )
    return jax.shard_map(
        shards, mesh=mesh, in_specs=placed, out_specs=P(("ctx", "head"), None), check_vma=False
    )
```

```python
import jax
import jax.numpy as jnp
from jax import lax
from jax.experimental import pallas as pl
from jax.experimental.pallas import tpu as pltpu
from jax.sharding import PartitionSpec as P

BLOCK = 128
BLOCKS = 8
TOKENS_HERE = 1024
HEADS_HERE = 4
WIDTH = 128
LEVELS = 12
EPSILON = 1e-06
FAR = -1e4
MESSAGE_ROWS = 144

F32 = jnp.float32
BF16 = jnp.bfloat16


def dot(left, right):
    return jnp.dot(left, right, preferred_element_type=F32)


def dot_rows(left, right):
    return lax.dot_general(left, right, (((1,), (1,)), ((), ())), preferred_element_type=F32)


def dot_columns(left, right):
    return lax.dot_general(left, right, (((0,), (0,)), ((), ())), preferred_element_type=F32)


def split3(value):
    first = value.astype(BF16)
    rest = value - first.astype(F32)
    second = rest.astype(BF16)
    third = (rest - second.astype(F32)).astype(BF16)
    return first, second, third


def rows_of(block):
    return slice(block * BLOCK, (block + 1) * BLOCK)


def prepare_masks(seg_ref, far_ref, pair_ref):
    row = lax.broadcasted_iota(jnp.int32, (BLOCK, BLOCK), 0)
    col = lax.broadcasted_iota(jnp.int32, (BLOCK, BLOCK), 1)
    segs = seg_ref[...].astype(F32)
    padded = jnp.concatenate([segs, jnp.zeros((BLOCK - BLOCKS, BLOCK), F32)], axis=0)
    seg_cols = padded.T
    for block in range(BLOCKS):
        same = seg_cols[:, block : block + 1] == segs[block : block + 1, :]
        far_ref[block] = jnp.where(same & (row >= col), 0.0, FAR)
    for step in range(7):
        size = 1 << step
        chosen = (row // size == col // size + 1) & (row // size % 2 == 1)
        pair_ref[step] = jnp.where(chosen, 1.0, 0.0).astype(BF16)


def unit_rows(rows, ones):
    wide = rows.astype(F32)
    total = dot((wide * wide).astype(BF16), ones)
    return (wide * lax.rsqrt(total + EPSILON)).astype(BF16)


def columns_of(rows):
    return jnp.concatenate([rows, jnp.zeros((BLOCK - rows.shape[0], BLOCK), F32)], axis=0).T


def column_at(columns, kind, block):
    at = kind * BLOCKS + block
    return columns[:, at : at + 1]


def summary_terms(heads, k_ref, v_ref, spread_ref, segs, far_ref, pair_ref, keys_ref, fading_ref, solved_ref, node_ref, keeps_ref, column_ref, between):
    row = lax.broadcasted_iota(jnp.int32, (BLOCK, BLOCK), 0)
    col = lax.broadcasted_iota(jnp.int32, (BLOCK, BLOCK), 1)
    every = range(BLOCKS)
    all_blocks = [(h, b) for h in range(len(heads)) for b in every]
    ones = jnp.ones((BLOCK, BLOCK), BF16)
    upto = jnp.where(row <= col, 1.0, 0.0).astype(BF16)
    last_seg = jnp.broadcast_to(segs[:, BLOCK - 1 :], (BLOCKS, BLOCK))
    first_seg = jnp.broadcast_to(segs[:, :1], (BLOCKS, BLOCK))
    before = jnp.concatenate([first_seg[:1], last_seg[:-1]], axis=0)
    opens = (segs == before).astype(F32)
    closes = (segs == last_seg).astype(F32)
    through = (last_seg == before).astype(F32)
    summed, columns, keep = [], [], []
    for head in heads:
        strength = spread_ref[1, head]
        total = sum(dot(part, upto) for part in split3(spread_ref[0, head]))
        last_sum = jnp.broadcast_to(total[:, BLOCK - 1 :], (BLOCKS, BLOCK))
        opening = jnp.exp(total) * opens
        closing = jnp.exp(last_sum - total) * closes
        keeps = jnp.exp(last_sum) * through
        columns.append(
            columns_of(jnp.concatenate([total, strength, opening, strength * opening, closing], axis=0))
        )
        summed.append(total)
        keep.append([keeps[b : b + 1] for b in every])
        column_ref[head] = columns[-1]
    kn = {}
    for h, head in enumerate(heads):
        unit = unit_rows(k_ref[head], ones)
        for b in every:
            kn[h, b] = unit[rows_of(b)]
    grams = {i: dot_rows(kn[i], kn[i]) for i in all_blocks}
    lower = {}
    for h, b in all_blocks:
        fading = jnp.exp(column_at(columns[h], 0, b) - summed[h][b : b + 1, :] + far_ref[b])
        fading_ref[heads[h], b] = fading
        lower[h, b] = (column_at(columns[h], 1, b) * fading * grams[h, b]).astype(BF16)
    between()
    eye = jnp.where(row == col, 1.0, 0.0).astype(BF16)
    inverse = {i: eye - lower[i] * pair_ref[0] for i in all_blocks}
    for step in range(1, 7):
        mask = pair_ref[step]
        half = {i: dot(inverse[i], lower[i] * mask).astype(BF16) for i in all_blocks}
        inverse = {i: inverse[i] - dot(half[i], inverse[i]).astype(BF16) for i in all_blocks}
    joined = {}
    for h, b in all_blocks:
        wide = kn[h, b].astype(F32)
        right = jnp.concatenate(
            [
                (column_at(columns[h], 1, b) * v_ref[heads[h], rows_of(b), :].astype(F32)).astype(BF16),
                (column_at(columns[h], 3, b) * wide).astype(BF16),
            ],
            axis=1,
        )
        solved = dot(inverse[h, b], right).astype(BF16)
        solved_ref[heads[h], b] = solved
        ended = (column_at(columns[h], 4, b) * wide).astype(BF16)
        joined[h, b] = dot_columns(ended, solved)
        keys_ref[heads[h], rows_of(b), :] = kn[h, b]
    nodes = [[joined[h, b] for b in every] for h in range(len(heads))]
    first = 0
    for level in range(3):
        many = len(nodes[0]) // 2
        for h, head in enumerate(heads):
            merged, kept = [], []
            for pair in range(many):
                early, late = nodes[h][2 * pair], nodes[h][2 * pair + 1]
                keep_e, keep_o = keep[h][2 * pair], keep[h][2 * pair + 1]
                node = early.astype(BF16)
                node_ref[head, first + pair] = node
                keeps_ref[head, first + pair : first + pair + 1, :] = keep_e
                moved = dot(late[:, WIDTH:].astype(BF16), node)
                carried = jnp.concatenate([late[:, :WIDTH], keep_e * late[:, WIDTH:]], axis=1)
                merged.append(jnp.concatenate([keep_o, keep_o], axis=1) * early + carried - moved)
                kept.append(keep_e * keep_o)
            nodes[h], keep[h] = merged, kept
        first = first + many
    return [(nodes[h][0], keep[h][0]) for h in range(len(heads))]


def readout_terms(head, q_ref, weight_ref, keys_ref, fading_ref, solved_ref, node_ref, keeps_ref, column_ref, out_ref, weighted_ref):
    every = range(BLOCKS)
    ones = jnp.ones((BLOCK, BLOCK), BF16)
    columns = column_ref[head]
    wcols = weight_ref[head].T

    def weight(level, block):
        at = block * 16 + level
        return wcols[:, at : at + 1]

    qn = unit_rows(q_ref[head], ones)
    scores = [
        (fading_ref[head, b] * dot_rows(qn[rows_of(b)], keys_ref[head, rows_of(b), :])).astype(BF16) for b in every
    ]
    both = [dot(scores[b], solved_ref[head, b]) for b in every]
    out = [weight(0, b) * both[b][:, :WIDTH] for b in every]
    reads = [column_at(columns, 2, b) * qn[rows_of(b)].astype(F32) - both[b][:, WIDTH:] for b in every]
    first = 0
    for level in range(1, 4):
        span = 1 << (level - 1)
        many = BLOCKS // (2 * span)
        for pair in range(many):
            later = [b for b in every if b // span == 2 * pair + 1]
            stack = jnp.concatenate([reads[b] for b in later], axis=0).astype(BF16)
            moved = dot(stack, node_ref[head, first + pair])
            keep = keeps_ref[head, first + pair : first + pair + 1, :]
            for at, b in enumerate(later):
                part = moved[at * BLOCK : (at + 1) * BLOCK]
                out[b] = out[b] + weight(level, b) * part[:, :WIDTH]
                reads[b] = keep * reads[b] - part[:, WIDTH:]
        first = first + many
    for b in every:
        out_ref[head, rows_of(b), :] = out[b]
        weighted_ref[head, rows_of(b), :] = jnp.concatenate(
            [(weight(level, b) * reads[b]).astype(BF16) for level in range(4, 10)], axis=1
        )

MESH = pl.DeviceIdType.MESH
GROUPS = 2


def joined(late, early):
    keep_l, body_l, first_l, last_l = late
    keep_e, body_e, first_e, last_e = early
    same = (first_l == last_e).astype(F32)
    moved = dot(body_l[:, WIDTH:].astype(BF16), body_e.astype(BF16))
    carried = jnp.concatenate([body_l[:, :WIDTH], (same * keep_e)[:, WIDTH:] * body_l[:, WIDTH:]], axis=1)
    keep_l = same * keep_l
    return keep_l * keep_e, keep_l * body_e + carried - same * moved, first_e, last_l


def without_state(summary):
    keep, body, first, last = summary
    return keep, jnp.concatenate([jnp.zeros((BLOCK, WIDTH), F32), body[:, WIDTH:]], axis=1), first, last


def chosen(use, one, other):
    use = use.astype(F32)
    return tuple(use * a + (1.0 - use) * b for a, b in zip(one, other))


def tail_rows(summary):
    keep, _, first_id, last_id = summary
    parts = [part.astype(F32) for part in split3(keep)] + [first_id, last_id]
    return jnp.concatenate(parts + [jnp.zeros((11, 2 * WIDTH), F32)], axis=0).astype(BF16)


def layer_kernel(
    q_hbm,
    k_hbm,
    v_hbm,
    gate_hbm,
    w_hbm,
    decay_hbm,
    strength_hbm,
    weights_hbm,
    seg_hbm,
    gain_hbm,
    result_ref,
    q_ref,
    k_ref,
    v_ref,
    gate_ref,
    whole_ref,
    decay_ref,
    strength_ref,
    weights_ref,
    seg_ref,
    gain_ref,
    far_ref,
    pair_ref,
    spread_ref,
    weight_ref,
    keys_ref,
    fading_ref,
    solved_ref,
    node_ref,
    keeps_ref,
    column_ref,
    out_ref,
    weighted_ref,
    silu_ref,
    normed_ref,
    gathered_ref,
    sum_ref,
    core_sent_ref,
    core_came_ref,
    quad_ref,
    half_sent_ref,
    half_ref,
    ring_sent_ref,
    ring_ref,
    total_ref,
    keep_ref,
    prefix_ref,
    prekeep_ref,
    chip_ref,
    segs_ref,
    load_sem,
    small_sem,
    own_sem,
    core_sem,
    quad_sem,
    half_sent_sem,
    half_came_sem,
    ring_sem,
    chip_sem,
    out_sem,
    in_sem,
    w_sent_sem,
    w_came_sem,
):
    ctx = lax.axis_index("ctx")
    x = lax.axis_index("head")
    core = lax.rem(ctx, 2)
    z = lax.rem(ctx // 2, 8)
    y = ctx // 16
    zq = lax.rem(z, 4)
    zh = z // 4
    right, left, opposite = lax.rem(x + 1, 4), lax.rem(x + 3, 4), lax.rem(x + 2, 4)
    other_core = ctx + 1 - 2 * core

    def at(y_to, z_to):
        return (y_to * 8 + z_to) * 2 + core

    def quad_to(d):
        return at(y, zh * 4 + lax.rem(zq + d, 4))

    def half_to(n):
        return at(y, 7 - z + n * (2 * (zq // 3) - 1))

    def ring_to(d):
        return at(lax.rem(y + d, 4), z)

    def remote(source, target, sent, came, axis, to):
        return pltpu.make_async_remote_copy(
            src_ref=source,
            dst_ref=target,
            send_sem=sent,
            recv_sem=came,
            device_id={axis: to},
            device_id_type=MESH,
        )

    partners = [("ctx", other_core)]
    partners += [("ctx", at(y, lax.rem(z + d, 8))) for d in range(1, 8)]
    partners += [("ctx", ring_to(d)) for d in (1, 2, 3)]
    partners += [("head", lax.rem(x + d, 4)) for d in (1, 2, 3)]

    sources = ((k_hbm, k_ref), (v_hbm, v_ref), (q_hbm, q_ref), (gate_hbm, gate_ref))

    def load(which, head):
        source, target = sources[which]
        columns = slice(head * WIDTH, (head + 1) * WIDTH)
        return pltpu.make_async_copy(source.at[:, columns], target.at[head], load_sem.at[which, head])

    smalls = [
        pltpu.make_async_copy(source, target, small_sem.at[n])
        for n, (source, target) in enumerate(
            (
                (seg_hbm, seg_ref),
                (decay_hbm, decay_ref),
                (strength_hbm, strength_ref),
                (weights_hbm, weights_ref),
                (gain_hbm, gain_ref),
            )
        )
    ]
    own_w = pltpu.make_async_copy(w_hbm, whole_ref.at[x], own_sem)
    quarters = [pl.ds(pl.multiple_of(core * 256 + part * 128, 128), 128) for part in range(2)]
    pieces = [
        pl.ds(pl.multiple_of(core * 256 + part * 128 + lax.rem(y, 2) * 64, 64), 64) for part in range(2)
    ]
    half_rows = pl.ds(pl.multiple_of(core * 256, 256), 256)

    def w_copy(n, source, shard, rows, axis, to):
        return remote(source, whole_ref.at[shard, rows], w_sent_sem.at[n], w_came_sem.at[n], axis, to)

    w_first = [
        w_copy(0, w_hbm.at[quarters[0]], x, quarters[0], "head", right),
        w_copy(1, w_hbm.at[quarters[1]], x, quarters[1], "head", left),
        w_copy(2, w_hbm.at[quarters[1]], x, quarters[1], "head", right),
        w_copy(3, w_hbm.at[quarters[0]], x, quarters[0], "head", left),
    ]
    w_relay = [
        w_copy(4, whole_ref.at[left, pieces[0]], left, pieces[0], "head", right),
        w_copy(5, whole_ref.at[right, pieces[1]], right, pieces[1], "head", left),
    ]
    w_share = [
        w_copy(9, whole_ref.at[opposite, pieces[0]], opposite, pieces[0], "ctx", at(y + 1 - 2 * lax.rem(y, 2), z)),
        w_copy(10, whole_ref.at[opposite, pieces[1]], opposite, pieces[1], "ctx", at(3 - y, z)),
    ]
    w_core = [
        w_copy(6 + n, whole_ref.at[shard, half_rows], shard, half_rows, "ctx", other_core)
        for n, shard in enumerate((left, right, opposite))
    ]

    def core_copy(head):
        return remote(
            core_sent_ref.at[head], core_came_ref.at[head], core_sem.at[0, head], core_sem.at[1, head], "ctx", other_core
        )

    def quad_copy(group, d):
        mine = quad_ref.at[group, zq]
        return remote(mine, mine, quad_sem.at[0, group, d - 1], quad_sem.at[1, group, d - 1], "ctx", quad_to(d))

    def half_copy(group, n):
        return remote(
            half_sent_ref.at[group],
            half_ref.at[group],
            half_sent_sem.at[group, n],
            half_came_sem.at[group],
            "ctx",
            half_to(n),
        )

    def ring_copy(group, d):
        return remote(
            ring_sent_ref.at[group],
            ring_ref.at[group, y],
            ring_sem.at[0, group, d - 1],
            ring_sem.at[1, group, d - 1],
            "ctx",
            ring_to(d),
        )

    def chip_copy(group, part, head):
        mine = chip_ref.at[head, pl.ds(2 * part, 2 + part)]
        return remote(mine, mine, chip_sem.at[0, group, part], chip_sem.at[1, group, part], "ctx", other_core)

    def spread_copy(head, d):
        to = lax.rem(x + d, 4)
        rows = pl.ds(pl.multiple_of(to * 256, 256), 256)
        columns = pl.ds(pl.multiple_of(x * 512 + head * WIDTH, WIDTH), WIDTH)
        return remote(
            normed_ref.at[head, rows],
            gathered_ref.at[:, columns],
            out_sem.at[head, d - 1],
            in_sem.at[head, d - 1],
            "head",
            to,
        )

    def own_head(group):
        return 2 * group + core

    def read(ref):
        tail = ref[BLOCK:, :].astype(F32)
        return tail[0:1] + tail[1:2] + tail[2:3], ref[:BLOCK, :].astype(F32), tail[3:4], tail[4:5]

    def write(ref, summary):
        ref[:BLOCK, :] = summary[1].astype(BF16)
        ref[BLOCK:, :] = tail_rows(summary)

    def own_ids():
        first_id = jnp.broadcast_to(segs_ref[0:1, :1], (1, 2 * WIDTH))
        last_id = jnp.broadcast_to(segs_ref[BLOCKS - 1 :, WIDTH - 1 :], (1, 2 * WIDTH))
        return first_id, last_id

    def summary_step(group, between, ready):
        heads = [2 * group, 2 * group + 1]
        for head in heads:
            for which in range(2):
                load(which, head).wait()
        found = summary_terms(
            heads,
            k_ref,
            v_ref,
            spread_ref,
            segs_ref[...],
            far_ref,
            pair_ref,
            keys_ref,
            fading_ref,
            solved_ref,
            node_ref,
            keeps_ref,
            column_ref,
            between,
        )
        ready()
        for head, (body, keep) in zip(heads, found):
            keep = jnp.concatenate([keep, keep], axis=1)
            total_ref[head] = body
            keep_ref[head] = jnp.broadcast_to(keep, (8, 2 * WIDTH))
            write(core_sent_ref.at[head], (keep, body) + own_ids())
            core_copy(head).start()

    def chip_step(group):
        for head in (2 * group, 2 * group + 1):
            core_copy(head).wait_recv()
        head = own_head(group)
        mine = (keep_ref[head, 0:1, :], total_ref[head]) + own_ids()
        other = read(core_came_ref.at[head])
        to = quad_ref.at[group, zq]

        @pl.when(core == 1)
        def _():
            write(to, joined(mine, other))

        @pl.when(core == 0)
        def _():
            write(to, joined(other, mine))

        for d in (1, 3, 2):
            quad_copy(group, d).start()

    def store_prefix(group, prefix):
        prefix_ref[group] = prefix[1]
        prekeep_ref[group, 0:1, :] = prefix[0]
        prekeep_ref[group, 1:2, :] = prefix[2]

    def load_prefix(group):
        first_id = prekeep_ref[group, 1:2, :]
        return prekeep_ref[group, 0:1, :], prefix_ref[group], first_id, first_id

    def quad_step(group):
        for d in (1, 2, 3):
            quad_copy(group, d).wait_recv()
        parts = [read(quad_ref.at[group, n]) for n in range(4)]
        first, second = joined(parts[1], parts[0]), joined(parts[3], parts[2])
        write(half_sent_ref.at[group], joined(second, first))

        @pl.when((zq == 0) | (zq == 3))
        def _():
            for n in (1, 0):
                half_copy(group, n).start()

        head = own_head(group)
        odd = lax.rem(zq, 2)
        upper = zq // 2
        own_first = read(quad_ref.at[group, zq])[2]
        none = jnp.ones((1, 2 * WIDTH), F32), jnp.zeros((BLOCK, 2 * WIDTH), F32), own_first, own_first
        keep, body, first_id, last_id = read(quad_ref.at[group, odd * (zq - odd)])
        same = (own_first == last_id).astype(F32)
        near = chosen(odd, (same * keep, same * body, first_id, first_id), none)
        chip_ref[head, 0] = near[1][:, :WIDTH].astype(BF16)
        near = without_state(near)
        far = chosen(upper, joined(near, first), near)
        chip_ref[head, 1] = far[1][:, :WIDTH].astype(BF16)
        chip_copy(group, 0, head).start()
        store_prefix(group, without_state(far))

    def ring_step(group):
        half_copy(group, 0).wait_recv()
        mine, other = read(half_sent_ref.at[group]), read(half_ref.at[group])

        @pl.when(zh == 1)
        def _():
            write(ring_sent_ref.at[group], joined(mine, other))

        @pl.when(zh == 0)
        def _():
            write(ring_sent_ref.at[group], joined(other, mine))

        for d in (2, 1, 3):

            @pl.when(y + d < 4)
            def _():
                ring_copy(group, d).start()

        prefix = load_prefix(group)
        over = chosen(zh, joined(prefix, other), prefix)
        chip_ref[own_head(group), 2] = over[1][:, :WIDTH].astype(BF16)
        store_prefix(group, without_state(over))

    def last_step(group):
        for d in range(1, 4):

            @pl.when(y >= d)
            def _():
                ring_copy(group, d).wait_recv()

        head = own_head(group)
        odd, upper = lax.rem(y, 2), y // 2

        def slot(use, n):
            return read(ring_ref.at[group, use * n + (1 - use) * 3])

        prefix = load_prefix(group)
        oldest = joined(slot(upper, 1), slot(upper, 0))
        over = chosen(odd, joined(prefix, slot(odd, y - 1)), prefix)
        chip_ref[head, 3] = over[1][:, :WIDTH].astype(BF16)
        over = joined(without_state(over), oldest)
        chip_ref[head, 4] = (upper.astype(F32) * over[1][:, :WIDTH]).astype(BF16)
        chip_copy(group, 1, head).start()

    def readout_step(head):
        load(2, head).wait()
        readout_terms(
            head,
            q_ref,
            weight_ref,
            keys_ref,
            fading_ref,
            solved_ref,
            node_ref,
            keeps_ref,
            column_ref,
            out_ref,
            weighted_ref,
        )

    def gate_step(head):
        load(3, head).wait()
        gate = gate_ref[head].astype(F32)
        silu_ref[head] = gate / (1.0 + jnp.exp(-gate)) * gain_ref[...]

    def own_states(head, first, last):
        keep, body, _, last_id = read(core_came_ref.at[head])
        joins = core.astype(F32) * (own_ids()[0] == last_id).astype(F32)[:, :WIDTH]
        keep = joins * keep[:, :WIDTH] + (1.0 - core.astype(F32))
        erase = (joins * body[:, WIDTH:]).astype(BF16)
        states = [chip_ref[head, n] for n in range(first, last)]
        moved = dot(erase, jnp.concatenate(states, axis=1))
        carried = [
            (keep * state.astype(F32) - moved[:, n * WIDTH : (n + 1) * WIDTH]).astype(BF16)
            for n, state in enumerate(states)
        ]
        if first == 0:
            carried = [(joins * body[:, :WIDTH]).astype(BF16)] + carried
        return jnp.concatenate(carried, axis=0)

    def await_states(group, part, head):
        @pl.when(head != own_head(group))
        def _():
            chip_copy(group, part, head).wait_recv()

    def near_step(group, head):
        await_states(group, 0, head)
        states = own_states(head, 0, 2)
        out_ref[head] += dot(weighted_ref[head, :, : 3 * WIDTH], states)

    def finish_step(group, head):
        await_states(group, 1, head)
        states = own_states(head, 2, 5)
        ones = jnp.ones((WIDTH, WIDTH), BF16)
        total = out_ref[head] + dot(weighted_ref[head, :, 3 * WIDTH :], states)
        mean = dot((total * total).astype(BF16), ones) * (1.0 / WIDTH)
        normed_ref[head] = (total * lax.rsqrt(mean + EPSILON) * silu_ref[head]).astype(BF16)
        for d in (2, 1, 3):
            spread_copy(head, d).start()
        rows = pl.ds(pl.multiple_of(x * 256, 256), 256)
        columns = pl.ds(pl.multiple_of(x * 512 + head * WIDTH, WIDTH), WIDTH)
        gathered_ref[:, columns] = normed_ref[head, rows, :]

    def finish_group(group):
        for turn in range(2):
            @pl.when(core == 0)
            def _():
                finish_step(group, 2 * group + turn)

            @pl.when(core == 1)
            def _():
                finish_step(group, 2 * group + 1 - turn)

    def part_of(group, shard, columns):
        mine = pl.ds(pl.multiple_of(shard * 512 + group * 256, 256), 256)
        return dot(gathered_ref[:, mine], whole_ref[shard, group * 256 : (group + 1) * 256, columns])

    def arrived(group, ways):
        for head in (2 * group, 2 * group + 1):
            for d in ways:
                spread_copy(head, d).wait_recv()

    def by_tiles(work):
        def tile(n, carry):
            work(pl.ds(pl.multiple_of(n * 512, 512), 512))
            return carry

        lax.fori_loop(0, 4, tile, 0)

    def project_near(columns):
        sum_ref[:, columns] = part_of(0, x, columns) + part_of(0, left, columns) + part_of(0, right, columns)

    def project_far(columns):
        sum_ref[:, columns] += part_of(0, opposite, columns)

    def project_rest(columns):
        total = sum(part_of(1, shard, columns) for shard in (x, left, right, opposite))
        result_ref[:, columns] = (sum_ref[:, columns] + total).astype(BF16)

    for group in range(GROUPS):
        ring_ref[group, 3] = jnp.zeros((MESSAGE_ROWS, 2 * WIDTH), BF16)
    barrier = pltpu.get_barrier_semaphore()
    for axis, to in partners:
        pl.semaphore_signal(barrier, inc=1, device_id={axis: to}, device_id_type=MESH)
    for copy in smalls[:3]:
        copy.start()
    for head in range(HEADS_HERE):
        for which in range(2):
            load(which, head).start()
    for copy in smalls[3:]:
        copy.start()
    for head in range(HEADS_HERE):
        for which in (2, 3):
            load(which, head).start()
    own_w.start()
    smalls[0].wait()
    segs_ref[...] = seg_ref[...].astype(F32)
    prepare_masks(seg_ref, far_ref, pair_ref)
    for source, n in ((decay_ref, 0), (strength_ref, 1)):
        smalls[1 + n].wait()
        for each in range(HEADS_HERE):
            for b in range(BLOCKS):
                spread_ref[n, each, b : b + 1, :] = source[each : each + 1, rows_of(b)]


    def enter():
        pl.semaphore_wait(barrier, len(partners))
        for copy in w_first[:2]:
            copy.start()

    summary_step(0, enter, lambda: None)
    summary_step(1, lambda: chip_step(0), lambda: None)
    for copy in smalls[3:]:
        copy.wait()
    for copy in w_first[2:]:
        copy.start()
    gate_step(0)
    chip_step(1)
    quad_step(0)
    for level in range(10):
        for each in range(HEADS_HERE):
            for b in range(BLOCKS):
                row = b * 16 + level
                weight_ref[each, row : row + 1, :] = weights_ref[level, each : each + 1, rows_of(b)]
    for head in range(HEADS_HERE):
        readout_step(head)
    for n in range(2):
        w_first[n].wait_recv()
        w_relay[n].start()
    gate_step(1)
    quad_step(1)
    ring_step(0)
    near_step(0, 0)
    near_step(0, 1)
    gate_step(2)
    gate_step(3)
    near_step(1, 2)
    near_step(1, 3)
    ring_step(1)
    for n in range(2):
        w_relay[n].wait_recv()
        w_share[n].start()
    last_step(0)
    finish_group(0)
    for n in range(2):
        w_first[2 + n].wait_recv()
        w_core[n].start()
    last_step(1)
    finish_group(1)
    for copy in w_share:
        copy.wait_recv()
    w_core[2].start()
    own_w.wait()
    for copy in w_core[:2]:
        copy.wait_recv()
    arrived(0, (1, 3))
    by_tiles(project_near)
    w_core[2].wait_recv()
    arrived(0, (2,))
    by_tiles(project_far)
    arrived(1, (1, 3, 2))
    by_tiles(project_rest)
    for copy in w_first + w_relay + w_share + w_core:
        copy.wait_send()
    for head in range(HEADS_HERE):
        core_copy(head).wait_send()
        for d in (1, 2, 3):
            spread_copy(head, d).wait_send()
    for group in range(GROUPS):
        for d in (1, 2, 3):
            quad_copy(group, d).wait_send()
        for part in range(2):
            chip_copy(group, part, own_head(group)).wait_send()
        for d in range(1, 4):

            @pl.when(y + d < 4)
            def _():
                ring_copy(group, d).wait_send()

        @pl.when((zq == 0) | (zq == 3))
        def _():
            for n in range(2):
                half_copy(group, n).wait_send()


def shards(queries, keys, values, log_decay, write_strength, level_weights, segment, out_gate, norm_gain, w_out):
    far = pl.BlockSpec(memory_space=pl.ANY)
    near = pl.BlockSpec(memory_space=pltpu.VMEM)
    tall = (HEADS_HERE, TOKENS_HERE, WIDTH)
    wide = (MESSAGE_ROWS, 2 * WIDTH)
    return pl.pallas_call(
        layer_kernel,
        out_shape=jax.ShapeDtypeStruct((256, 2048), BF16),
        in_specs=[far] * 10,
        out_specs=near,
        scratch_shapes=[
            pltpu.VMEM(tall, BF16),
            pltpu.VMEM(tall, BF16),
            pltpu.VMEM(tall, BF16),
            pltpu.VMEM(tall, BF16),
            pltpu.VMEM((4, 512, 2048), BF16),
            pltpu.VMEM((HEADS_HERE, TOKENS_HERE), F32),
            pltpu.VMEM((HEADS_HERE, TOKENS_HERE), F32),
            pltpu.VMEM((LEVELS, HEADS_HERE, TOKENS_HERE), F32),
            pltpu.VMEM((BLOCKS, BLOCK), jnp.int32),
            pltpu.VMEM((1, WIDTH), F32),
            pltpu.VMEM((BLOCKS, BLOCK, BLOCK), F32),
            pltpu.VMEM((7, BLOCK, BLOCK), BF16),
            pltpu.VMEM((2, HEADS_HERE, BLOCKS, BLOCK), F32),
            pltpu.VMEM((HEADS_HERE, BLOCK, BLOCK), F32),
            pltpu.VMEM(tall, BF16),
            pltpu.VMEM((HEADS_HERE, BLOCKS, BLOCK, BLOCK), F32),
            pltpu.VMEM((HEADS_HERE, BLOCKS, BLOCK, 2 * WIDTH), BF16),
            pltpu.VMEM((HEADS_HERE, 7, BLOCK, 2 * WIDTH), BF16),
            pltpu.VMEM((HEADS_HERE, 8, WIDTH), F32),
            pltpu.VMEM((HEADS_HERE, BLOCK, BLOCK), F32),
            pltpu.VMEM(tall, F32),
            pltpu.VMEM((HEADS_HERE, TOKENS_HERE, 6 * WIDTH), BF16),
            pltpu.VMEM(tall, F32),
            pltpu.VMEM(tall, BF16),
            pltpu.VMEM((256, 2048), BF16),
            pltpu.VMEM((256, 2048), F32),
            pltpu.VMEM((HEADS_HERE,) + wide, BF16),
            pltpu.VMEM((HEADS_HERE,) + wide, BF16),
            pltpu.VMEM((GROUPS, 4) + wide, BF16),
            pltpu.VMEM((GROUPS,) + wide, BF16),
            pltpu.VMEM((GROUPS,) + wide, BF16),
            pltpu.VMEM((GROUPS,) + wide, BF16),
            pltpu.VMEM((GROUPS, 4) + wide, BF16),
            pltpu.VMEM((HEADS_HERE, BLOCK, 2 * WIDTH), F32),
            pltpu.VMEM((HEADS_HERE, 8, 2 * WIDTH), F32),
            pltpu.VMEM((GROUPS, BLOCK, 2 * WIDTH), F32),
            pltpu.VMEM((GROUPS, 8, 2 * WIDTH), F32),
            pltpu.VMEM((HEADS_HERE, 5, BLOCK, WIDTH), BF16),
            pltpu.VMEM((BLOCKS, BLOCK), F32),
            pltpu.SemaphoreType.DMA((4, HEADS_HERE)),
            pltpu.SemaphoreType.DMA((5,)),
            pltpu.SemaphoreType.DMA,
            pltpu.SemaphoreType.DMA((2, HEADS_HERE)),
            pltpu.SemaphoreType.DMA((2, GROUPS, 3)),
            pltpu.SemaphoreType.DMA((GROUPS, 2)),
            pltpu.SemaphoreType.DMA((GROUPS,)),
            pltpu.SemaphoreType.DMA((2, GROUPS, 3)),
            pltpu.SemaphoreType.DMA((2, GROUPS, 2)),
            pltpu.SemaphoreType.DMA((HEADS_HERE, 3)),
            pltpu.SemaphoreType.DMA((HEADS_HERE, 3)),
            pltpu.SemaphoreType.DMA((11,)),
            pltpu.SemaphoreType.DMA((11,)),
        ],
        compiler_params=pltpu.CompilerParams(
            collective_id=0, has_side_effects=True, vmem_limit_bytes=58 << 20
        ),
        cost_estimate=pl.CostEstimate(flops=24_000_000_000, bytes_accessed=16_000_000, transcendentals=0),
    )(
        queries,
        keys,
        values,
        out_gate,
        w_out,
        log_decay,
        write_strength,
        level_weights.transpose(1, 0, 2),
        segment.reshape(BLOCKS, BLOCK),
        norm_gain.reshape(1, WIDTH),
    )


def solution(mesh):
    placed = (
        P("ctx", "head"),
        P("ctx", "head"),
        P("ctx", "head"),
        P("head", "ctx"),
        P("head", "ctx"),
        P("head", None, "ctx"),
        P("ctx"),
        P("ctx", "head"),
        P(),
        P("head", None),
    )
    return jax.shard_map(
        shards, mesh=mesh, in_specs=placed, out_specs=P(("ctx", "head"), None), check_vma=False
    )
```
